32 devices in a mesh: dp: 4 (over z), fsdp: 8 (over y, x, core).
Axes of the slice: x: 2, y: 2, z: 4, core: 2. Of those that a mesh axis runs over, the one named last changes fastest.
Arguments:
- patches: bfloat16 [40960, 768], P(('dp', 'fsdp'))
- cotangent: bfloat16 [40960, 768], P(('dp', 'fsdp')), may hold values from -6 to 6
- clip_len: int32 [32, 2], P(('dp', 'fsdp')), may hold values from 0 to 1214, as said below
- pos_table: float32 [768, 1214], P(('dp', 'fsdp')), may hold values from -3 to 3
- vector_params: float32 [768, 8], P(('dp', 'fsdp'))
- w_qkv: float32 [768, 2304], P(('dp', 'fsdp')), may hold values from -0.21875 to 0.21875
- w_proj: float32 [768, 768], P(('dp', 'fsdp')), may hold values from -1.25 to 1.25
- w_fc1: float32 [768, 3072], P(('dp', 'fsdp')), may hold values from -0.21875 to 0.21875
- b_fc1: float32 [3072], P(('dp', 'fsdp')), may hold values from -2 to 2
- w_fc2: float32 [3072, 768], P(('dp', 'fsdp')), may hold values from -0.109375 to 0.109375
- mom_pos_table: float32 [768, 1214], P(('dp', 'fsdp')), may hold values from -24 to 24
- mom_vector_params: float32 [768, 8], P(('dp', 'fsdp')), may hold values from -320 to 320
- mom_w_qkv: float32 [768, 2304], P(('dp', 'fsdp')), may hold values from -320 to 320
- mom_w_proj: float32 [768, 768], P(('dp', 'fsdp')), may hold values from -320 to 320
- mom_w_fc1: float32 [768, 3072], P(('dp', 'fsdp')), may hold values from -320 to 320
- mom_b_fc1: float32 [3072], P(('dp', 'fsdp')), may hold values from -320 to 320
- mom_w_fc2: float32 [3072, 768], P(('dp', 'fsdp')), may hold values from -320 to 320
- ema_pos_table: float32 [768, 1214], P(('dp', 'fsdp')), may hold values from -3 to 3
- ema_vector_params: float32 [768, 8], P(('dp', 'fsdp')), may hold values from -3 to 3
- ema_w_qkv: float32 [768, 2304], P(('dp', 'fsdp')), may hold values from -0.21875 to 0.21875
- ema_w_proj: float32 [768, 768], P(('dp', 'fsdp')), may hold values from -1.25 to 1.25
- ema_w_fc1: float32 [768, 3072], P(('dp', 'fsdp')), may hold values from -0.21875 to 0.21875
- ema_b_fc1: float32 [3072], P(('dp', 'fsdp')), may hold values from -2 to 2
- ema_w_fc2: float32 [3072, 768], P(('dp', 'fsdp')), may hold values from -0.109375 to 0.109375
Outputs:
- layer_out: bfloat16 [40960, 768], P(('dp', 'fsdp'))
- patch_grad: bfloat16 [40960, 768], P(('dp', 'fsdp'))
- feature_stats: float32 [2, 768], replicated
- grad_pos_table: float32 [768, 1214], P(('dp', 'fsdp'))
- grad_vector_params: float32 [768, 8], P(('dp', 'fsdp'))
- grad_w_qkv: float32 [768, 2304], P(('dp', 'fsdp'))
- grad_w_proj: float32 [768, 768], P(('dp', 'fsdp'))
- grad_w_fc1: float32 [768, 3072], P(('dp', 'fsdp'))
- grad_b_fc1: float32 [3072], P(('dp', 'fsdp'))
- grad_w_fc2: float32 [3072, 768], P(('dp', 'fsdp'))
- update_pos_table: float32 [768, 1214], P(('dp', 'fsdp'))
- update_vector_params: float32 [768, 8], P(('dp', 'fsdp'))
- update_w_qkv: float32 [768, 2304], P(('dp', 'fsdp'))
- update_w_proj: float32 [768, 768], P(('dp', 'fsdp'))
- update_w_fc1: float32 [768, 3072], P(('dp', 'fsdp'))
- update_b_fc1: float32 [3072], P(('dp', 'fsdp'))
- update_w_fc2: float32 [3072, 768], P(('dp', 'fsdp'))
- next_mom_pos_table: float32 [768, 1214], P(('dp', 'fsdp'))
- next_mom_vector_params: float32 [768, 8], P(('dp', 'fsdp'))
- next_mom_w_qkv: float32 [768, 2304], P(('dp', 'fsdp'))
- next_mom_w_proj: float32 [768, 768], P(('dp', 'fsdp'))
- next_mom_w_fc1: float32 [768, 3072], P(('dp', 'fsdp'))
- next_mom_b_fc1: float32 [3072], P(('dp', 'fsdp'))
- next_mom_w_fc2: float32 [3072, 768], P(('dp', 'fsdp'))
- next_ema_pos_table: float32 [768, 1214], P(('dp', 'fsdp'))
- next_ema_vector_params: float32 [768, 8], P(('dp', 'fsdp'))
- next_ema_w_qkv: float32 [768, 2304], P(('dp', 'fsdp'))
- next_ema_w_proj: float32 [768, 768], P(('dp', 'fsdp'))
- next_ema_w_fc1: float32 [768, 3072], P(('dp', 'fsdp'))
- next_ema_b_fc1: float32 [3072], P(('dp', 'fsdp'))
- next_ema_w_fc2: float32 [3072, 768], P(('dp', 'fsdp'))
The draws below stay inside these ranges and needn't reach their ends.
Inputs may be any that keep to these rules, and one draw needn't show every extreme that they name: `clip_len`: each device's row is either (1214, 0), one clip at stride 10, or (514, 514), two clips at stride 16; exactly half of the devices hold each kind, which ones is drawn.
All inputs are finite; a program needn't handle non-finite values.
Results may differ from the reference program's by a relative error of at most 0.013.
Values may be sent and summed in bfloat16 or wider, within the bound.
A program may use at most 320 MiB of HBM per device.

```python
import jax
import jax.numpy as jnp
import numpy as np
from jax import lax

D = 768
HEADS = 12
FF = 3072
FREQ_L = 12
TIME_L = 101
FREQ_S = 8
TIME_S = 64
ROWS = 1280
PRIOR_STEPS = 3
LONG = 1214
SHORT = 514
TOKENS = 40960
DEVICES = 32


def draw_clip_len(key, part):
    order = jax.random.permutation(key, DEVICES)
    short_kind = (order % 2).astype(jnp.int32)
    first_len = jnp.where(short_kind == 1, SHORT, LONG).astype(jnp.int32)
    second_len = (short_kind * SHORT).astype(jnp.int32)
    return jnp.stack([first_len, second_len], axis=1).astype(jnp.int32)


def draw_patches(key, part):
    noise_key, shift_key = jax.random.split(key, 2)
    device = (jnp.arange(TOKENS) // ROWS).astype(jnp.float32)
    rising = (1.0 + 2.0 * device / max(DEVICES - 1, 1))[:, None]
    shift = 0.5 * jax.random.normal(shift_key, (1, D), jnp.float32)
    noise = jax.random.normal(noise_key, (TOKENS, D), jnp.float32)
    return (rising * noise + rising * shift).astype(jnp.bfloat16)


def draw_vector_params(key, part):
    noise = jax.random.normal(key, (D, 8), jnp.float32)
    column = jnp.arange(8)
    is_gain = jnp.logical_or(column == 0, column == 5)[None, :]
    return jnp.where(is_gain, 1.0 + 0.2 * noise, 0.3 * noise)


def level_of(key, extent, shards, least, top_value):
    def one(dim, blocks):
        draws = jax.random.uniform(jax.random.fold_in(jax.random.fold_in(key, 6), dim), (blocks,), jnp.float32, least / len(shards), top_value / len(shards))
        return jnp.repeat(jnp.exp(draws), extent[dim] // blocks).reshape((-1,) + (1,) * (len(extent) - dim - 1))

    factor_of = one(*shards[0])
    for cut in shards[1:]:
        factor_of = factor_of * one(*cut)
    return factor_of


def gaussian(key, dims, scale, reach, shards=(), held_as=jnp.bfloat16):
    values = jax.random.normal(key, dims, jnp.float32) * scale
    if len(shards) > 0:
        values = level_of(key, dims, shards, -0.22, 0.18) * values
    return jnp.clip(values, min=-reach, max=reach).astype(held_as)


def setup_inputs(seed: int = 0) -> dict:
    key_list = jax.random.split(jax.random.key(seed), 25)
    return {
        "patches": draw_patches(jax.random.fold_in(key_list[24], 71), 0),
        "cotangent": gaussian(key_list[1], (TOKENS, D), 1.0, 6.0, ((0, 32),)),
        "clip_len": draw_clip_len(jax.random.fold_in(key_list[24], 71), 0),
        "pos_table": gaussian(key_list[3], (D, LONG), 0.5, 3.0, ((0, 32),), jnp.float32),
        "vector_params": draw_vector_params(jax.random.fold_in(key_list[24], 71), 0),
        "w_qkv": gaussian(key_list[5], (D, 3 * D), D ** -0.5, 0.21875, ((0, 32),), jnp.float32),
        "w_proj": gaussian(key_list[6], (D, D), (D // 32) ** -0.5, 1.25, ((0, 32),), jnp.float32),
        "w_fc1": gaussian(key_list[7], (D, FF), D ** -0.5, 0.21875, ((0, 32),), jnp.float32),
        "b_fc1": gaussian(key_list[8], (FF,), 0.3, 2.0, ((0, 32),), jnp.float32),
        "w_fc2": gaussian(key_list[9], (FF, D), FF ** -0.5, 0.109375, ((0, 32),), jnp.float32),
        "mom_pos_table": gaussian(key_list[10], (D, LONG), ((DEVICES // 2) ** 0.5), 24.0, ((0, 32),), jnp.float32),
        "mom_vector_params": gaussian(key_list[11], (D, 8), ((TOKENS // 16) ** 0.5), 320.0, ((0, 32),), jnp.float32),
        "mom_w_qkv": gaussian(key_list[12], (D, 3 * D), ((TOKENS // 16) ** 0.5), 320.0, ((0, 32),), jnp.float32),
        "mom_w_proj": gaussian(key_list[13], (D, D), ((TOKENS // 16) ** 0.5), 320.0, ((0, 32),), jnp.float32),
        "mom_w_fc1": gaussian(key_list[14], (D, FF), ((TOKENS // 16) ** 0.5), 320.0, ((0, 32),), jnp.float32),
        "mom_b_fc1": gaussian(key_list[15], (FF,), ((TOKENS // 16) ** 0.5), 320.0, ((0, 32),), jnp.float32),
        "mom_w_fc2": gaussian(key_list[16], (FF, D), ((TOKENS // 16) ** 0.5), 320.0, ((0, 32),), jnp.float32),
        "ema_pos_table": gaussian(key_list[17], (D, LONG), 0.5, 3.0, ((0, 32),), jnp.float32),
        "ema_vector_params": gaussian(key_list[18], (D, 8), 0.5, 3.0, ((0, 32),), jnp.float32),
        "ema_w_qkv": gaussian(key_list[19], (D, 3 * D), D ** -0.5, 0.21875, ((0, 32),), jnp.float32),
        "ema_w_proj": gaussian(key_list[20], (D, D), (D // 32) ** -0.5, 1.25, ((0, 32),), jnp.float32),
        "ema_w_fc1": gaussian(key_list[21], (D, FF), D ** -0.5, 0.21875, ((0, 32),), jnp.float32),
        "ema_b_fc1": gaussian(key_list[22], (FF,), 0.3, 2.0, ((0, 32),), jnp.float32),
        "ema_w_fc2": gaussian(key_list[23], (FF, D), FF ** -0.5, 0.109375, ((0, 32),), jnp.float32),
    }


@jax.custom_vjp
def low(v):
    return lax.optimization_barrier(v.astype(jnp.bfloat16)).astype(jnp.float32)

@jax.custom_vjp
def low_back(v):
    return v

def low_keep(v):
    return (low(v), None)

def low_pass(kept, grad):
    return (grad,)

def back_keep(v):
    return (v, None)

def back_low(kept, grad):
    return (low(grad),)
low.defvjp(low_keep, low_pass)
low_back.defvjp(back_keep, back_low)
HIGHEST = lax.Precision.HIGHEST
NEG_FILL = -1e+30
NORM_EPS = 1e-06
INPUT_EPS = 1e-05
MOMENTUM = 0.9

def resize_rows(size_in, size_out):
    resize_table = np.zeros((size_out, size_in), np.float32)
    for target_row in range(size_out):
        source_pos = max((target_row + 0.5) * size_in / size_out - 0.5, 0.0)
        lower_cell = min(int(np.floor(source_pos)), size_in - 1)
        upper_cell = min(lower_cell + 1, size_in - 1)
        fraction = source_pos - lower_cell
        resize_table[target_row, lower_cell] += 1.0 - fraction
        resize_table[target_row, upper_cell] += fraction
    return resize_table

def short_from_long():
    result = np.zeros((SHORT, LONG), np.float32)
    result[0, 0] = 1.0
    result[1, 1] = 1.0
    result[2:, 2:] = np.kron(resize_rows(FREQ_L, FREQ_S), resize_rows(TIME_L, TIME_S))
    return jnp.asarray(result)

def row_flags(lengths):
    position = jnp.arange(ROWS, dtype=jnp.int32)
    first_len = lengths[0]
    second_len = lengths[1]
    in_first = position < first_len
    in_second = jnp.logical_and(position >= first_len, position < first_len + second_len)
    row_valid = jnp.logical_or(in_first, in_second).astype(jnp.float32)
    segment = jnp.where(in_first, 0, jnp.where(in_second, 1, 2)).astype(jnp.int32)
    offset = jnp.where(in_first, position, position - first_len).astype(jnp.int32)
    return (row_valid, segment, offset)

def make_selector(lengths, row_valid, offset):
    long_pick = jax.nn.one_hot(offset, LONG, dtype=jnp.float32)
    short_pick = jnp.dot(jax.nn.one_hot(offset, SHORT, dtype=jnp.float32), short_from_long(), precision=HIGHEST)
    return jnp.where(lengths[1] == 0, long_pick, short_pick) * row_valid[:, None]

def layer_norm(inputs, gain_row, bias_row):
    center = inputs - lax.optimization_barrier(jnp.mean(inputs, axis=-1, keepdims=True))
    spread = lax.optimization_barrier(jnp.mean(center * center, axis=-1, keepdims=True))
    return center * lax.rsqrt(spread + NORM_EPS) * gain_row + bias_row

def both_ways(tensor):
    return low_back(low(tensor))

def device_layer(normed, lengths, lowered):
    pos_low, vector_low, qkv_low, proj_low, fc1_low, bias_low, fc2_low = lowered
    row_valid, segment, offset = row_flags(lengths)
    selector = make_selector(lengths, row_valid, offset)
    pos_rows = jnp.dot(selector, pos_low.T, precision=HIGHEST)
    embedded = row_valid[:, None] * (normed + pos_rows)
    first_norm = both_ways(layer_norm(embedded, vector_low[:, 0], vector_low[:, 1]))
    projected = jnp.dot(first_norm, qkv_low, precision=HIGHEST)
    head_width = D // HEADS
    queries = both_ways(projected[:, :D] + vector_low[:, 2]).reshape(ROWS, HEADS, head_width)
    key_rows = both_ways(projected[:, D:2 * D]).reshape(ROWS, HEADS, head_width)
    values = both_ways(projected[:, 2 * D:] + vector_low[:, 3]).reshape(ROWS, HEADS, head_width)
    scores = low_back(jnp.einsum('qhd,khd->hqk', queries, key_rows, precision=HIGHEST) * head_width ** (-0.5))
    same_clip = (segment[:, None] == segment[None, :])[None]
    scores = jnp.where(same_clip, scores, NEG_FILL)
    softmaxed = low(jax.nn.softmax(scores, axis=-1))
    attended = both_ways(jnp.einsum('hqk,khd->qhd', softmaxed, values, precision=HIGHEST).reshape(ROWS, D))
    branch = low_back(jnp.dot(attended, proj_low, precision=HIGHEST) + vector_low[:, 4])
    residual = embedded + branch
    second_norm = both_ways(layer_norm(residual, vector_low[:, 5], vector_low[:, 6]))
    pre_act = low_back(jnp.dot(second_norm, fc1_low, precision=HIGHEST) + bias_low)
    activated = both_ways(jax.nn.gelu(pre_act, approximate=False))
    mlp_out = low_back(jnp.dot(activated, fc2_low, precision=HIGHEST) + vector_low[:, 7])
    return row_valid[:, None] * (residual + mlp_out)

def forward(inputs, params, clip_len):
    row_valid = jax.vmap(lambda lengths: row_flags(lengths)[0])(clip_len).reshape(TOKENS, 1)
    valid_count = jnp.sum(row_valid)
    feature_mean = lax.optimization_barrier(jnp.sum(row_valid * inputs, axis=0)) / valid_count
    feature_var = lax.optimization_barrier(jnp.sum(row_valid * inputs * inputs, axis=0)) / valid_count - feature_mean * feature_mean
    normed = (inputs - feature_mean) * lax.rsqrt(feature_var + INPUT_EPS)
    lowered = tuple((low(weight) for weight in params))

    def per_device(device_pair):
        return device_layer(device_pair[0], device_pair[1], lowered)
    blocks = lax.map(jax.checkpoint(per_device), (normed.reshape(DEVICES, ROWS, D), clip_len))
    return (blocks.reshape(TOKENS, D), jnp.stack([feature_mean, feature_var]))

def reference(patches, cotangent, clip_len, pos_table, vector_params, w_qkv, w_proj, w_fc1, b_fc1, w_fc2, mom_pos_table, mom_vector_params, mom_w_qkv, mom_w_proj, mom_w_fc1, mom_b_fc1, mom_w_fc2, ema_pos_table, ema_vector_params, ema_w_qkv, ema_w_proj, ema_w_fc1, ema_b_fc1, ema_w_fc2):
    params = (pos_table, vector_params, w_qkv, w_proj, w_fc1, b_fc1, w_fc2)
    momenta = (mom_pos_table, mom_vector_params, mom_w_qkv, mom_w_proj, mom_w_fc1, mom_b_fc1, mom_w_fc2)
    averages = (ema_pos_table, ema_vector_params, ema_w_qkv, ema_w_proj, ema_w_fc1, ema_b_fc1, ema_w_fc2)
    layer_out, pullback, feature_stats = jax.vjp(lambda inputs, weights: forward(inputs, weights, clip_len), patches.astype(jnp.float32), params, has_aux=True)
    patch_grad, grads = pullback(cotangent.astype(jnp.float32))
    rate = 0.02 * TOKENS ** (-0.5)
    average_keep = min(0.99, (1.0 + PRIOR_STEPS) / (10.0 + PRIOR_STEPS))
    next_moms = tuple((MOMENTUM * state + gradient for state, gradient in zip(momenta, grads)))
    updates = tuple((-(rate * (gradient + MOMENTUM * state)) for gradient, state in zip(grads, next_moms)))
    next_averages = tuple((average_keep * average + (1.0 - average_keep) * (weight + update) for average, weight, update in zip(averages, params, updates)))
    return (layer_out.astype(jnp.bfloat16), patch_grad.astype(jnp.bfloat16), feature_stats, grads[0], grads[1], grads[2], grads[3], grads[4], grads[5], grads[6], updates[0], updates[1], updates[2], updates[3], updates[4], updates[5], updates[6], next_moms[0], next_moms[1], next_moms[2], next_moms[3], next_moms[4], next_moms[5], next_moms[6], next_averages[0], next_averages[1], next_averages[2], next_averages[3], next_averages[4], next_averages[5], next_averages[6])
```

```python
from functools import partial

import jax
import jax.numpy as jnp
import ml_dtypes
import numpy as np
from jax import lax
from jax.experimental import pallas as pl
from jax.experimental.pallas import tpu as pltpu
from jax.sharding import PartitionSpec as P

HEADS = 12
FREQ_L = 12
TIME_L = 101
FREQ_S = 8
TIME_S = 64
PRIOR_STEPS = 3
LONG = 1214
SHORT = 514

NORM_EPS = 1e-06
INPUT_EPS = 1e-05
MOMENTUM = 0.9
MESH = pl.DeviceIdType.MESH
AXES = ("dp", "fsdp")
BF = jnp.bfloat16
F32 = jnp.float32
VMEM_LIMIT = 60 * 2**20
POS_PAD = 1280

TAIL_P = 0.305
TAIL_C = (
    0.121639732,
    0.122466826,
    0.10342081,
    0.121021868,
    -0.037977191,
    0.185717298,
    -0.152988541,
    0.036699245,
)


def resize_rows(size_in, size_out):
    resize_table = np.zeros((size_out, size_in), np.float64)
    for target_row in range(size_out):
        source_pos = max((target_row + 0.5) * size_in / size_out - 0.5, 0.0)
        lower_cell = min(int(np.floor(source_pos)), size_in - 1)
        upper_cell = min(lower_cell + 1, size_in - 1)
        fraction = source_pos - lower_cell
        resize_table[target_row, lower_cell] += 1.0 - fraction
        resize_table[target_row, upper_cell] += fraction
    return resize_table


def selectors(local_rows):
    table = np.zeros((3, local_rows, POS_PAD), np.float64)
    table[0, :LONG, :LONG] = np.eye(LONG)
    short = np.zeros((SHORT, LONG), np.float64)
    short[0, 0] = short[1, 1] = 1.0
    short[2:, 2:] = np.kron(resize_rows(FREQ_L, FREQ_S), resize_rows(TIME_L, TIME_S))
    high = short.astype(ml_dtypes.bfloat16).astype(np.float64)
    for first in (0, SHORT):
        table[1, first : first + SHORT, :LONG] = high
        table[2, first : first + SHORT, :LONG] = short - high
    return jnp.asarray(table.astype(ml_dtypes.bfloat16))


def nn(left, right):
    return lax.dot_general(left, right, (((1,), (0,)), ((), ())), preferred_element_type=F32)


def nt(left, right):
    return lax.dot_general(left, right, (((1,), (1,)), ((), ())), preferred_element_type=F32)


def tn(left, right):
    return lax.dot_general(left, right, (((0,), (0,)), ((), ())), preferred_element_type=F32)


class Place:
    def __init__(self, dp_size, fsdp_size):
        self.D, self.F = dp_size, fsdp_size
        self.X, self.Y = fsdp_size // 4, 2
        self.d = lax.axis_index("dp")
        self.f = lax.axis_index("fsdp")
        self.c = lax.rem(self.f, 2)
        self.x = lax.rem(lax.div(self.f, 2), self.X)
        self.y = lax.div(self.f, 2 * self.X)

    def fs(self, y, x, c):
        return (y * self.X + x) * 2 + c

    def up(self, value, step, size):
        return lax.rem(value + step, size)

    def partners(self):
        out = [(self.up(self.d, k, self.D), self.f) for k in range(1, self.D)]
        out += [(self.d, self.fs(self.y, self.up(self.x, k, self.X), self.c)) for k in range(1, self.X)]
        out += [(self.d, self.fs(self.up(self.y, k, self.Y), self.x, self.c)) for k in range(1, self.Y)]
        out.append((self.d, self.fs(self.y, self.x, 1 - self.c)))
        return out

    def everyone(self):
        out = [(self.up(self.d, k, self.D), self.f) for k in range(1, self.D)]
        return out + [(self.d, self.up(self.f, k, self.F)) for k in range(1, self.F)]


def meet(devices):
    barrier = pltpu.get_barrier_semaphore()
    for device in devices:
        pl.semaphore_signal(barrier, inc=1, device_id=device, device_id_type=MESH)
    pl.semaphore_wait(barrier, len(devices))


class Gather:
    @staticmethod
    def count(D, X, Y):
        return (D - 1) + 2 * (X - 1) + 2 * (Y - 1) + 1

    def __init__(self, at, src, out, send, recv, own):
        self.at, self.src, self.out, self.send, self.recv, self.own = at, src, out, send, recv, own
        D, X, Y = at.D, at.X, at.Y
        self.n_z = 0
        self.n_x = D - 1
        self.n_y = self.n_x + X - 1
        self.n_c = self.n_y + Y - 1

    def copy(self, src, dst, number, device):
        return pltpu.make_async_remote_copy(
            src_ref=src,
            dst_ref=dst,
            send_sem=self.send.at[number],
            recv_sem=self.recv.at[number],
            device_id=device,
            device_id_type=MESH,
        )

    def z_copy(self, k):
        at = self.at
        return self.copy(
            self.src,
            self.out.at[at.d, at.y, at.x, at.c],
            self.n_z + k - 1,
            (at.up(at.d, k, at.D), at.f),
        )

    def z_got(self, k):
        at = self.at
        here = self.out.at[at.up(at.d, at.D - k, at.D), at.y, at.x, at.c]
        return self.copy(here, here, self.n_z + k - 1, (at.up(at.d, at.D - k, at.D), at.f))

    def part(self, axis, order, y, x, c):
        if axis == order[0]:
            return self.out.at[:, y, x, c]
        return self.out.at[:, y, :, c] if axis == "y" else self.out.at[:, :, x, c]

    def side(self, axis, order, k, sent):
        at = self.at
        size = at.X if axis == "x" else at.Y
        first = self.n_x if axis == "x" else self.n_y
        mine = at.x if axis == "x" else at.y
        other = at.up(mine, k if sent else size - k, size)
        y, x = (at.y, other) if axis == "x" else (other, at.x)
        block = self.part(axis, order, at.y, at.x, at.c) if sent else self.part(axis, order, y, x, at.c)
        return self.copy(block, block, first + k - 1, (at.d, at.fs(y, x, at.c)))

    def pieces(self, order, c):
        at = self.at
        out = [self.out.at[:, at.y, at.x, c]]
        for axis in order:
            size = at.X if axis == "x" else at.Y
            for k in range(1, size):
                other = at.up(at.x if axis == "x" else at.y, size - k, size)
                y, x = (at.y, other) if axis == "x" else (other, at.x)
                out.append(self.part(axis, order, y, x, c))
        return out

    def sibling(self, block, number):
        at = self.at
        return self.copy(block, block, self.n_c + number, (at.d, at.fs(at.y, at.x, 1 - at.c)))

    def local(self):
        at = self.at
        return pltpu.make_async_copy(self.src, self.out.at[at.d, at.y, at.x, at.c], self.own)

    def size_of(self, axis):
        return self.at.X if axis == "x" else self.at.Y

    def phase(self, number):
        at = self.at
        if number == 0:
            self.local().start()
            for k in range(1, at.D):
                self.z_copy(k).start()
            return
        if number == 1:
            self.local().wait()
            for k in range(1, at.D):
                self.z_got(k).wait_recv()
        for core, order in ((0, ("x", "y")), (1, ("y", "x"))):

            @pl.when(at.c == core)
            def _(core=core, order=order):
                mine = self.pieces(order, core)
                first = 1 + (self.size_of(order[0]) - 1)
                if number == 1:
                    for k in range(1, self.size_of(order[0])):
                        self.side(order[0], order, k, True).start()
                    self.sibling(mine[0], 0).start()
                elif number == 2:
                    for k in range(1, self.size_of(order[0])):
                        self.side(order[0], order, k, False).wait_recv()
                    for k in range(1, self.size_of(order[1])):
                        self.side(order[1], order, k, True).start()
                    for i in range(1, first):
                        self.sibling(mine[i], i).start()
                elif number == 3:
                    for k in range(1, self.size_of(order[1])):
                        self.side(order[1], order, k, False).wait_recv()
                    for i in range(first, len(mine)):
                        self.sibling(mine[i], i).start()
                elif number == 4:
                    for k in range(1, at.D):
                        self.z_copy(k).wait_send()
                    for axis in order:
                        for k in range(1, self.size_of(axis)):
                            self.side(axis, order, k, True).wait_send()
                    for i, block in enumerate(mine):
                        self.sibling(block, i).wait_send()
                    for i, block in enumerate(self.pieces(order[::-1], 1 - core)):
                        self.sibling(block, i).wait_recv()


class Scatter:
    @staticmethod
    def count(D, X, Y):
        return 1 + (Y - 1) + (X - 1) + (D - 1)

    @staticmethod
    def scratch(D, X, Y, R, N):
        return [
            pltpu.VMEM((D, Y, X, R, N), BF),
            pltpu.VMEM((D, Y, X, R, N), BF),
            pltpu.VMEM((Y - 1, D, X, R, N), BF),
            pltpu.VMEM((Y - 1, D, R, N), BF),
        ] + ([] if X == Y else [pltpu.VMEM((X - 1, D, Y, R, N), BF), pltpu.VMEM((X - 1, D, R, N), BF)]) + [
            pltpu.VMEM((D - 1, R, N), BF)
        ]

    def __init__(self, at, grad, total, bufs, send, recv, own):
        self.at, self.grad, self.total = at, grad, total
        self.acc, self.r1, self.r2y, self.r3y = bufs[:4]
        self.r2x, self.r3x = (self.r2y, self.r3y) if at.X == at.Y else bufs[4:6]
        self.r4 = bufs[-1]
        self.send, self.recv, self.own = send, recv, own
        self.n_y = 1
        self.n_x = self.n_y + at.Y - 1
        self.n_z = self.n_x + at.X - 1

    def copy(self, src, dst, number, device):
        return pltpu.make_async_remote_copy(
            src_ref=src,
            dst_ref=dst,
            send_sem=self.send.at[number],
            recv_sem=self.recv.at[number],
            device_id=device,
            device_id_type=MESH,
        )

    def core_copy(self):
        at = self.at
        return self.copy(
            self.grad.at[:, :, :, 1 - at.c], self.r1, 0, (at.d, at.fs(at.y, at.x, 1 - at.c))
        )

    def local(self):
        return pltpu.make_async_copy(self.grad.at[:, :, :, self.at.c], self.acc, self.own)

    def side(self, axis, order, k):
        at = self.at
        if axis == "y":
            y = at.up(at.y, k, at.Y)
            device = (at.d, at.fs(y, at.x, at.c))
            if axis == order[0]:
                return self.copy(self.acc.at[:, y], self.r2y.at[k - 1], self.n_y + k - 1, device)
            return self.copy(self.acc.at[:, y, at.x], self.r3y.at[k - 1], self.n_y + k - 1, device)
        x = at.up(at.x, k, at.X)
        device = (at.d, at.fs(at.y, x, at.c))
        if axis == order[0]:
            return self.copy(self.acc.at[:, :, x], self.r2x.at[k - 1], self.n_x + k - 1, device)
        return self.copy(self.acc.at[:, at.y, x], self.r3x.at[k - 1], self.n_x + k - 1, device)

    def z_copy(self, k):
        at = self.at
        d = at.up(at.d, k, at.D)
        return self.copy(
            self.acc.at[d, at.y, at.x], self.r4.at[k - 1], self.n_z + k - 1, (d, at.f)
        )

    def size_of(self, axis):
        return self.at.X if axis == "x" else self.at.Y

    def phase(self, number):
        at, acc = self.at, self.acc
        if number == 0:
            self.local().start()
            self.core_copy().start()
            return
        if number == 1:
            self.local().wait()
            self.core_copy().wait_recv()

            def add(i, _):
                d, rest = lax.div(i, at.Y * at.X), lax.rem(i, at.Y * at.X)
                y, x = lax.div(rest, at.X), lax.rem(rest, at.X)
                acc[d, y, x] = acc[d, y, x] + self.r1[d, y, x]
                return 0

            lax.fori_loop(0, at.D * at.Y * at.X, add, 0)
        if number == 4:
            for k in range(1, at.D):
                self.z_copy(k).wait_recv()
            total = acc[at.d, at.y, at.x].astype(F32)
            for k in range(1, at.D):
                total = total + self.r4[k - 1].astype(F32)
            self.total[...] = total
            self.core_copy().wait_send()
            for k in range(1, at.D):
                self.z_copy(k).wait_send()
        for core, order in ((0, ("y", "x")), (1, ("x", "y"))):

            @pl.when(at.c == core)
            def _(core=core, order=order):
                n0, n1 = self.size_of(order[0]), self.size_of(order[1])
                if number == 1:
                    for k in range(1, n0):
                        self.side(order[0], order, k).start()
                elif number == 2:
                    for k in range(1, n0):
                        self.side(order[0], order, k).wait_recv()

                    def add(i, _):
                        d, j = lax.div(i, n1), lax.rem(i, n1)
                        y, x = (at.y, j) if order[0] == "y" else (j, at.x)
                        got = self.r2y if order[0] == "y" else self.r2x
                        value = acc[d, y, x]
                        for k in range(1, n0):
                            value = value + got[k - 1, d, j]
                        acc[d, y, x] = value
                        return 0

                    lax.fori_loop(0, at.D * n1, add, 0)
                    for k in range(1, n1):
                        self.side(order[1], order, k).start()
                elif number == 3:
                    for k in range(1, n1):
                        self.side(order[1], order, k).wait_recv()

                    def add(d, _):
                        got = self.r3y if order[1] == "y" else self.r3x
                        value = acc[d, at.y, at.x]
                        for k in range(1, n1):
                            value = value + got[k - 1, d]
                        acc[d, at.y, at.x] = value
                        return 0

                    lax.fori_loop(0, at.D, add, 0)
                elif number == 4:
                    for axis in order:
                        for k in range(1, self.size_of(axis)):
                            self.side(axis, order, k).wait_send()

        if number == 3:
            for k in range(1, at.D):
                self.z_copy(k).start()


class Total:
    @staticmethod
    def count(D, F):
        return (D - 1) + (F - 1)

    @staticmethod
    def scratch(D, F, rows, cols):
        return [pltpu.VMEM((D, rows, cols), F32), pltpu.VMEM((F, rows, cols), F32)]

    def __init__(self, at, bufs, send, recv):
        self.at, self.send, self.recv = at, send, recv
        self.z_buf, self.f_buf = bufs

    def copy(self, buf, slot, number, device):
        return pltpu.make_async_remote_copy(
            src_ref=buf.at[slot],
            dst_ref=buf.at[slot],
            send_sem=self.send.at[number],
            recv_sem=self.recv.at[number],
            device_id=device,
            device_id_type=MESH,
        )

    def z_copy(self, k, sent):
        at = self.at
        other = at.up(at.d, k if sent else at.D - k, at.D)
        return self.copy(self.z_buf, at.d if sent else other, k - 1, (other, at.f))

    def f_copy(self, k, sent):
        at = self.at
        other = at.up(at.f, k if sent else at.F - k, at.F)
        return self.copy(self.f_buf, at.f if sent else other, at.D - 1 + k - 1, (at.d, other))

    def start(self, value):
        at = self.at
        self.z_buf[at.d] = value
        for k in range(1, at.D):
            self.z_copy(k, True).start()

    def middle(self):
        at = self.at
        for k in range(1, at.D):
            self.z_copy(k, False).wait_recv()
        total = self.z_buf[0]
        for i in range(1, at.D):
            total = total + self.z_buf[i]
        self.f_buf[at.f] = total
        for k in range(1, at.F):
            self.f_copy(k, True).start()

    def end(self):
        at = self.at
        for k in range(1, at.F):
            self.f_copy(k, False).wait_recv()
        total = self.f_buf[0]
        for i in range(1, at.F):
            total = total + self.f_buf[i]
        for k in range(1, at.D):
            self.z_copy(k, True).wait_send()
        for k in range(1, at.F):
            self.f_copy(k, True).wait_send()
        return total


def chain(arrays):
    for step in range(len(arrays) + 4):
        for i, array in enumerate(arrays):
            if 0 <= step - i <= 4:
                array.phase(step - i)


def gather_kernel(D, F, count, patches_ref, valid_ref, *refs):
    srcs, stats_ref, outs = refs[:count], refs[count], refs[count + 1 : 2 * count + 1]
    z_buf, f_buf, s_send, s_recv, send, recv, own = refs[2 * count + 1 :]
    at = Place(D, F)
    meet(at.everyone())
    arrays = [
        Gather(at, srcs[i], outs[i], send.at[i], recv.at[i], own.at[i]) for i in range(count)
    ]
    for array in arrays[:2]:
        array.phase(0)
    rows = patches_ref.shape[0]
    step_rows = 64

    def accumulate(i, sums):
        block = pl.ds(pl.multiple_of(i * step_rows, step_rows), step_rows)
        values = patches_ref[block, :].astype(F32)
        values = values * valid_ref[block, :1]
        first = values.reshape(step_rows // 8, 8, -1)
        return (sums[0] + jnp.sum(first, axis=0), sums[1] + jnp.sum(first * first, axis=0))

    empty = jnp.zeros((8, patches_ref.shape[1]), F32)
    plain, square = lax.fori_loop(0, rows // step_rows, accumulate, (empty, empty))
    valid_sum = jnp.sum(valid_ref[...], axis=0, keepdims=True)[:, :1]
    row = lax.broadcasted_iota(jnp.int32, empty.shape, 0)
    plain = jnp.sum(plain, axis=0, keepdims=True)
    square = jnp.sum(square, axis=0, keepdims=True)
    packed = jnp.where(row == 0, plain, jnp.where(row == 1, square, jnp.where(row == 2, valid_sum, 0.0)))
    total = Total(at, (z_buf, f_buf), s_send, s_recv)
    total.start(packed)
    for array in arrays[2:]:
        array.phase(0)
    total.middle()
    for array in arrays[:2]:
        array.phase(1)
    stats_ref[...] = total.end()
    for array in arrays[2:]:
        array.phase(1)
    for number in (2, 3, 4):
        for array in arrays:
            array.phase(number)


def gather_all(D, F, patches, valid, shards, collective_id):
    X, Y = F // 4, 2
    count = len(shards)
    n = Gather.count(D, X, Y)
    hbm = pl.BlockSpec(memory_space=pl.ANY)
    vmem = pl.BlockSpec(memory_space=pltpu.VMEM)
    width = patches.shape[1]
    sent = sum(s.size for s in shards) * 2 * D * F
    return pl.pallas_call(
        partial(gather_kernel, D, F, count),
        name="gather_weights",
        out_shape=[jax.ShapeDtypeStruct((8, width), F32)]
        + [jax.ShapeDtypeStruct((D, Y, X, 2) + s.shape, s.dtype) for s in shards],
        in_specs=[vmem, vmem] + [hbm] * count,
        out_specs=[vmem] + [hbm] * count,
        scratch_shapes=Total.scratch(D, F, 8, width)
        + [pltpu.SemaphoreType.DMA((Total.count(D, F),)), pltpu.SemaphoreType.DMA((Total.count(D, F),))]
        + [
            pltpu.SemaphoreType.DMA((count, n)),
            pltpu.SemaphoreType.DMA((count, n)),
            pltpu.SemaphoreType.DMA((count,)),
        ],
        compiler_params=pltpu.CompilerParams(
            collective_id=collective_id, has_side_effects=True, vmem_limit_bytes=VMEM_LIMIT
        ),
        cost_estimate=pl.CostEstimate(flops=0, bytes_accessed=sent, transcendentals=0),
    )(patches, valid, *shards)


def scatter_kernel(D, F, count, per, small_ref, *refs):
    grads, small_out, totals = refs[:count], refs[count], refs[count + 1 : 2 * count + 1]
    rest = refs[2 * count + 1 :]
    bufs = [rest[i * per : (i + 1) * per] for i in range(count)]
    z_buf, f_buf, s_send, s_recv, send, recv, own = rest[count * per :]
    at = Place(D, F)
    meet(at.everyone())
    arrays = [
        Scatter(at, grads[i], totals[i], bufs[i], send.at[i], recv.at[i], own.at[i])
        for i in range(count)
    ]
    total = Total(at, (z_buf, f_buf), s_send, s_recv)
    for array in arrays:
        array.phase(0)
    total.start(small_ref[...])
    arrays[0].phase(1)
    total.middle()
    for array in arrays[1:]:
        array.phase(1)
    small_out[...] = total.end()
    for number in (2, 3, 4):
        for array in arrays:
            array.phase(number)


def scatter_all(D, F, small, grads, collective_id):
    X, Y = F // 4, 2
    count = len(grads)
    n = Scatter.count(D, X, Y)
    hbm = pl.BlockSpec(memory_space=pl.ANY)
    vmem = pl.BlockSpec(memory_space=pltpu.VMEM)
    scratch = []
    for g in grads:
        scratch += Scatter.scratch(D, X, Y, *g.shape[-2:])
    per = len(scratch) // count
    return pl.pallas_call(
        partial(scatter_kernel, D, F, count, per),
        name="scatter_grads",
        out_shape=[jax.ShapeDtypeStruct(small.shape, F32)]
        + [jax.ShapeDtypeStruct(g.shape[-2:], F32) for g in grads],
        in_specs=[vmem] + [hbm] * count,
        out_specs=[vmem] * (1 + count),
        scratch_shapes=scratch
        + Total.scratch(D, F, *small.shape)
        + [pltpu.SemaphoreType.DMA((Total.count(D, F),)), pltpu.SemaphoreType.DMA((Total.count(D, F),))]
        + [
            pltpu.SemaphoreType.DMA((count, n)),
            pltpu.SemaphoreType.DMA((count, n)),
            pltpu.SemaphoreType.DMA((count,)),
        ],
        compiler_params=pltpu.CompilerParams(
            collective_id=collective_id, has_side_effects=True, vmem_limit_bytes=VMEM_LIMIT
        ),
        cost_estimate=pl.CostEstimate(
            flops=0, bytes_accessed=sum(g.size for g in grads) * 4, transcendentals=0
        ),
    )(small, *grads)


def row_of(first, rows, width):
    return first + lax.broadcasted_iota(jnp.int32, (rows, width), 0)


def embed_kernel(len_ref, patches, stats, sel, sel_low, pos, vec, bias, w_ref, emb_out, norm_out, q_out, acc):
    rows, width = patches.shape
    mean, inv_std = stats[0:1, :], stats[1:2, :]
    normed = (patches[...].astype(F32) - mean) * inv_std
    acc[...] = nt(sel[0], pos[...])

    @pl.when(len_ref[1] > 0)
    def _():
        acc[...] += nt(sel_low[0], pos[...])

    row = row_of(pl.program_id(0) * rows, rows, width)
    embedded = jnp.where(row < len_ref[0] + len_ref[1], normed + acc[...], 0.0)
    emb_out[...] = embedded
    center = embedded - jnp.mean(embedded, axis=1, keepdims=True)
    spread = jnp.mean(center * center, axis=1, keepdims=True)
    first = (center * lax.rsqrt(spread + NORM_EPS) * vec[0:1, :] + vec[1:2, :]).astype(BF)
    norm_out[...] = first
    q_out[...] = (nn(first, w_ref[...]) + bias[...]).astype(BF)


def embed(lengths, patches, stats, table, pos, vec, qkv_bias, w_qkv):
    rows, width = patches.shape
    block = 256
    whole = lambda a: pl.BlockSpec(a.shape, lambda i, s: (0,) * a.ndim, pipeline_mode=pl.Buffered(1))
    by_row = lambda n: pl.BlockSpec((block, n), lambda i, s: (i, 0))
    return pl.pallas_call(
        embed_kernel,
        name="embed",
        grid_spec=pltpu.PrefetchScalarGridSpec(
            num_scalar_prefetch=1,
            grid=(rows // block,),
            in_specs=[
                by_row(width),
                whole(stats),
                pl.BlockSpec((1, block, POS_PAD), lambda i, s: (jnp.where(s[1] > 0, 1, 0), i, 0)),
                pl.BlockSpec((1, block, POS_PAD), lambda i, s: (2, i, 0)),
                whole(pos),
                whole(vec),
                whole(qkv_bias),
                whole(w_qkv),
            ],
            out_specs=[by_row(width), by_row(width), by_row(3 * width)],
            scratch_shapes=[pltpu.VMEM((block, width), F32)],
        ),
        out_shape=[
            jax.ShapeDtypeStruct((rows, width), F32),
            jax.ShapeDtypeStruct((rows, width), BF),
            jax.ShapeDtypeStruct((rows, 3 * width), BF),
        ],
        compiler_params=pltpu.CompilerParams(vmem_limit_bytes=VMEM_LIMIT),
        cost_estimate=pl.CostEstimate(
            flops=2 * rows * width * (3 * width + POS_PAD), bytes_accessed=24 * 2**20, transcendentals=0
        ),
    )(lengths, patches, stats, table, table, pos, vec, qkv_bias, w_qkv)


def attend_pair(q_ref, k_ref, v_ref, qs_ref, ks_ref, q_block):
    rows = q_ref.shape[0]
    lane = lax.broadcasted_iota(jnp.int32, (q_block, 128), 1)

    def half(values, head):
        keep = lane < 64 if head == 0 else lane >= 64
        return jnp.where(keep, values, jnp.zeros_like(values))

    def query(block, head):
        scaled = q_ref[block, :] * jnp.asarray(0.125, BF)
        return jnp.concatenate([half(scaled, head), qs_ref[block, :]], axis=1)

    keys = jnp.concatenate([k_ref[...], ks_ref[...]], axis=1)
    return keys, query, half


def forward_pair(q_ref, k_ref, v_ref, qs_ref, ks_ref, out_ref, lse_ref, key_buf, v_buf, o_buf):
    rows = q_ref.shape[0]
    q_block = 256
    keys, query, _ = attend_pair(q_ref, k_ref, v_ref, qs_ref, ks_ref, q_block)
    key_buf[...] = keys
    v_t = jnp.transpose(v_ref[...])
    ones = jnp.ones((16, rows), BF)
    for head in range(2):
        v_buf[head] = jnp.concatenate([v_t[64 * head : 64 * head + 64], ones], axis=0)
    for i in range(rows // q_block):
        block = pl.ds(i * q_block, q_block)
        for head in range(2):
            scores = nt(key_buf[...], query(block, head))
            top = jnp.max(scores, axis=0, keepdims=True)
            probs = jnp.exp(scores - top).astype(BF)
            out = nn(v_buf[head], probs)
            total = out[64:65, :]
            o_buf[64 * head : 64 * head + 64, block] = (out[:64] / total).astype(BF)
            lse_ref[0, head : head + 1, block] = top + jnp.log(total)
    out_ref[...] = jnp.transpose(o_buf[...])


def pair_specs(rows):
    pair = lambda first: pl.BlockSpec((rows, 128), lambda p: (0, first + p))
    whole = pl.BlockSpec((rows, 128), lambda p: (0, 0))
    return pair, whole


def attend_forward(qkv, q_seg, k_seg):
    rows = qkv.shape[0]
    pairs = HEADS // 2
    pair, whole = pair_specs(rows)
    return pl.pallas_call(
        forward_pair,
        name="attend_forward",
        grid=(pairs,),
        in_specs=[pair(0), pair(pairs), pair(2 * pairs), whole, whole],
        out_specs=[pair(0), pl.BlockSpec((1, 8, rows), lambda p: (p, 0, 0))],
        out_shape=[
            jax.ShapeDtypeStruct((rows, 128 * pairs), BF),
            jax.ShapeDtypeStruct((pairs, 8, rows), F32),
        ],
        scratch_shapes=[
            pltpu.VMEM((rows, 256), BF),
            pltpu.VMEM((2, 80, rows), BF),
            pltpu.VMEM((128, rows), BF),
        ],
        compiler_params=pltpu.CompilerParams(vmem_limit_bytes=VMEM_LIMIT),
        cost_estimate=pl.CostEstimate(
            flops=4 * 12 * rows * rows * 256,
            bytes_accessed=8 * rows * 768,
            transcendentals=12 * rows * rows,
        ),
    )(qkv, qkv, qkv, q_seg, k_seg)


def backward_pair(
    q_ref, k_ref, v_ref, do_ref, qs_ref, ks_ref, lse_ref, delta_ref,
    dq_ref, dk_ref, dv_ref, key_buf, kt_buf, dk_acc, dv_acc, dqt_buf,
):
    rows = q_ref.shape[0]
    q_block = 256
    keys, query, half = attend_pair(q_ref, k_ref, v_ref, qs_ref, ks_ref, q_block)
    key_buf[...] = keys
    kt_buf[...] = jnp.transpose(k_ref[...])
    for i in range(rows // q_block):
        block = pl.ds(i * q_block, q_block)
        for head in range(2):
            q_ext = query(block, head)
            d_out = half(do_ref[block, :], head)
            scores = nt(key_buf[...], q_ext)
            probs = jnp.exp(scores - lse_ref[0, head : head + 1, block])
            d_probs = nt(v_ref[...], d_out)
            d_scores = (probs * (d_probs - delta_ref[0, head : head + 1, block])).astype(BF)
            dv = nn(probs.astype(BF), d_out)
            dk = nn(d_scores, q_ext[:, :128])
            if i == 0 and head == 0:
                dv_acc[...] = dv
                dk_acc[...] = dk
            else:
                dv_acc[...] += dv
                dk_acc[...] += dk
            dq = nn(kt_buf[64 * head : 64 * head + 64, :], d_scores)
            dqt_buf[64 * head : 64 * head + 64, block] = (dq * 0.125).astype(BF)
    dq_ref[...] = jnp.transpose(dqt_buf[...])
    dk_ref[...] = dk_acc[...].astype(BF)
    dv_ref[...] = dv_acc[...].astype(BF)


def attend_backward(qkv, grad_attended, q_seg, k_seg, lse, delta):
    rows = qkv.shape[0]
    pairs = HEADS // 2
    pair, whole = pair_specs(rows)
    line = pl.BlockSpec((1, 8, rows), lambda p: (p, 0, 0))
    return pl.pallas_call(
        backward_pair,
        name="attend_backward",
        grid=(pairs,),
        in_specs=[pair(0), pair(pairs), pair(2 * pairs), pair(0), whole, whole, line, line],
        out_specs=[pair(0)] * 3,
        out_shape=[jax.ShapeDtypeStruct((rows, 128 * pairs), BF)] * 3,
        scratch_shapes=[
            pltpu.VMEM((rows, 256), BF),
            pltpu.VMEM((128, rows), BF),
            pltpu.VMEM((rows, 128), F32),
            pltpu.VMEM((rows, 128), F32),
            pltpu.VMEM((128, rows), BF),
        ],
        compiler_params=pltpu.CompilerParams(vmem_limit_bytes=VMEM_LIMIT),
        cost_estimate=pl.CostEstimate(
            flops=10 * 12 * rows * rows * 256,
            bytes_accessed=14 * rows * 768,
            transcendentals=12 * rows * rows,
        ),
    )(qkv, qkv, qkv, grad_attended, q_seg, k_seg, lse, delta)


def gelu_both(u):
    z = jnp.abs(u)
    falling = jnp.exp(-0.5 * u * u)
    t = 1.0 / (1.0 + TAIL_P * z)
    poly = TAIL_C[-1]
    for coefficient in TAIL_C[-2::-1]:
        poly = poly * t + coefficient
    tail = poly * t * falling
    upper = jnp.where(u >= 0, 1.0 - tail, tail)
    return u * upper, upper + u * falling * 0.3989422804014327


def norm_parts(values):
    center = values - jnp.mean(values, axis=1, keepdims=True)
    spread = jnp.mean(center * center, axis=1, keepdims=True)
    rho = lax.rsqrt(spread + NORM_EPS)
    return center * rho, rho


def norm_back(n, rho, grad, gain):
    q = grad * gain
    return rho * (q - jnp.mean(q, axis=1, keepdims=True) - n * jnp.mean(q * n, axis=1, keepdims=True))


def fold(values):
    return jnp.sum(values.reshape(-1, 8, values.shape[1]), axis=0)


def middle_kernel(
    len_ref, emb, att, cot, wo, w1, b1, w2, vec, pick,
    layer_out, res_grad, att_grad, delta_out, g_proj, g_fc1, g_b1, g_fc2, g_small,
    residual, second, second_t, masked, mlp, g_second, act_buf, pre_buf, branch,
):
    step = pl.program_id(0)
    rows, width = emb.shape
    block_rows = 256
    blocks = rows // block_rows
    valid_rows = len_ref[0] + len_ref[1]
    ones = jnp.ones((8, block_rows), BF)

    def take(i):
        return pl.ds(pl.multiple_of(i * block_rows, block_rows), block_rows)

    @pl.when(step == 0)
    def _():
        def one(i, _):
            block = take(i)
            branch_out = nn(att[block, :], wo[...]) + vec[4:5, :]
            res = emb[block, :] + branch_out
            residual[block, :] = res
            n, _rho = norm_parts(res)
            sn = (n * vec[5:6, :] + vec[6:7, :]).astype(BF)
            second[block, :] = sn
            second_t[i] = jnp.transpose(sn)
            row = row_of(i * block_rows, block_rows, width)
            masked[block, :] = jnp.where(row < valid_rows, cot[block, :], jnp.zeros((), BF))
            mlp[block, :] = jnp.zeros((block_rows, width), F32)
            g_second[block, :] = jnp.zeros((block_rows, width), F32)
            return 0

        lax.fori_loop(0, blocks, one, 0)

    bias = b1[...]
    for i in range(blocks):
        block = pl.ds(i * block_rows, block_rows)
        pre = nn(second[block, :], w1[...]) + bias
        act, slope = gelu_both(pre)
        act = act.astype(BF)
        act_buf[block, :] = act
        grad_act = nt(masked[block, :], w2[...]).astype(BF).astype(F32)
        grad_pre = (grad_act * slope).astype(BF)
        pre_buf[block, :] = grad_pre
        mlp[block, :] += nn(act, w2[...])
        g_second[block, :] += nt(grad_pre, w1[...])
    g_fc2[...] = tn(act_buf[...], masked[...]).astype(BF)
    for i in range(blocks):
        block = pl.ds(i * block_rows, block_rows)
        part = nn(second_t[i], pre_buf[block, :])
        line = nn(ones, pre_buf[block, :])
        total = part if i == 0 else total + part
        lines = line if i == 0 else lines + line
    g_fc1[...] = total.astype(BF)
    g_b1[...] = lines

    @pl.when(step == pl.num_programs(0) - 1)
    def _():
        def one(i, sums):
            block = take(i)
            res = residual[block, :]
            n, rho = norm_parts(res)
            row = row_of(i * block_rows, block_rows, width)
            keep = row < valid_rows
            layer_out[block, :] = jnp.where(keep, res + mlp[block, :] + vec[7:8, :], 0.0).astype(BF)
            grad = g_second[block, :].astype(BF).astype(F32)
            back = norm_back(n, rho, grad, vec[5:6, :])
            out_grad = masked[block, :]
            total = out_grad.astype(F32) + back
            res_grad[block, :] = total
            low = total.astype(BF)
            branch[block, :] = low
            into = nt(low, wo[...]).astype(BF)
            att_grad[block, :] = into
            product = into.astype(F32) * att[block, :].astype(F32)
            high = product.astype(BF)
            rest = (product - high.astype(F32)).astype(BF)
            delta = nn(high, pick[...]) + nn(rest, pick[...])
            delta_out[:, block] = jnp.transpose(delta)[: delta_out.shape[0], :]
            return (
                sums[0] + nn(ones, low)[0:8],
                sums[1] + fold(grad * n),
                sums[2] + fold(grad),
                sums[3] + nn(ones, out_grad)[0:8],
            )

        empty = jnp.zeros((8, width), F32)
        sums = lax.fori_loop(0, blocks, one, (empty,) * 4)
        g_proj[...] = tn(att[...], branch[...]).astype(BF)
        g_small[0:1, :] = sums[0][0:1]
        g_small[1:2, :] = jnp.sum(sums[1], axis=0, keepdims=True)
        g_small[2:3, :] = jnp.sum(sums[2], axis=0, keepdims=True)
        g_small[3:4, :] = sums[3][0:1]
        g_small[4:8, :] = jnp.zeros((4, width), F32)


def middle(lengths, emb, att, cot, wo, w1, b1, w2, vec):
    rows, width = emb.shape
    hidden = w1.shape[1]
    tile = 512
    once = pl.Buffered(1)
    whole = lambda shape: pl.BlockSpec(shape, lambda j, s: (0,) * len(shape), pipeline_mode=once)
    pick = np.zeros((width, 128), np.float32)
    pick[np.arange(width), np.arange(width) // 64] = 1.0
    pick = jnp.asarray(pick.astype(ml_dtypes.bfloat16))
    out_shape = [
        jax.ShapeDtypeStruct((rows, width), BF),
        jax.ShapeDtypeStruct((rows, width), F32),
        jax.ShapeDtypeStruct((rows, width), BF),
        jax.ShapeDtypeStruct((16, rows), F32),
        jax.ShapeDtypeStruct((width, width), BF),
        jax.ShapeDtypeStruct((width, hidden), BF),
        jax.ShapeDtypeStruct((8, hidden), F32),
        jax.ShapeDtypeStruct((hidden, width), BF),
        jax.ShapeDtypeStruct((8, width), F32),
    ]
    return pl.pallas_call(
        middle_kernel,
        name="middle",
        grid_spec=pltpu.PrefetchScalarGridSpec(
            num_scalar_prefetch=1,
            grid=(hidden // tile,),
            in_specs=[
                whole((rows, width)),
                whole((rows, width)),
                whole((rows, width)),
                whole((width, width)),
                pl.BlockSpec((width, tile), lambda j, s: (0, j)),
                pl.BlockSpec((1, tile), lambda j, s: (0, j)),
                pl.BlockSpec((tile, width), lambda j, s: (j, 0)),
                whole((8, width)),
                whole((width, 128)),
            ],
            out_specs=[whole(s.shape) for s in out_shape[:5]]
            + [
                pl.BlockSpec((width, tile), lambda j, s: (0, j)),
                pl.BlockSpec((8, tile), lambda j, s: (0, j)),
                pl.BlockSpec((tile, width), lambda j, s: (j, 0)),
                whole((8, width)),
            ],
            scratch_shapes=[
                pltpu.VMEM((rows, width), F32),
                pltpu.VMEM((rows, width), BF),
                pltpu.VMEM((rows // 256, width, 256), BF),
                pltpu.VMEM((rows, width), BF),
                pltpu.VMEM((rows, width), F32),
                pltpu.VMEM((rows, width), F32),
                pltpu.VMEM((rows, tile), BF),
                pltpu.VMEM((rows, tile), BF),
                pltpu.VMEM((rows, width), BF),
            ],
        ),
        out_shape=out_shape,
        compiler_params=pltpu.CompilerParams(vmem_limit_bytes=VMEM_LIMIT),
        cost_estimate=pl.CostEstimate(
            flops=2 * rows * width * (6 * hidden + 3 * width),
            bytes_accessed=40 * 2**20,
            transcendentals=rows * hidden,
        ),
    )(lengths, emb, att, cot, wo, w1, b1, w2, vec, pick)


def first_kernel(
    len_ref, gq, gk, gv, first, emb, res_grad, patches, stats, sel, sel_low, w_ref, vec,
    g_qkv, g_pos, g_masked, g_small, acc, pos_acc, sums,
):
    step = pl.program_id(0)
    rows, width = emb.shape
    last = step == pl.num_programs(0) - 1
    ones = jnp.ones((8, rows), BF)

    @pl.when(step == 0)
    def _():
        acc[...] = jnp.zeros_like(acc)
        pos_acc[...] = jnp.zeros_like(pos_acc)
        sums[...] = jnp.zeros_like(sums)

    parts = [gq[...], gk[...], gv[...]]
    for i, part in enumerate(parts):
        columns = slice(i * width, (i + 1) * width)
        acc[:, columns] += tn(first[...], part)
        into = nt(part, w_ref[:, columns])
        grad = into if i == 0 else grad + into
    grad = grad.astype(BF).astype(F32)
    n, rho = norm_parts(emb[...])
    total = res_grad[...] + norm_back(n, rho, grad, vec[0:1, :])
    row = row_of(step * rows, rows, width)
    total = jnp.where(row < len_ref[0] + len_ref[1], total, 0.0)
    g_masked[...] = total
    low = total.astype(BF)
    pos_acc[...] += tn(low, sel[0])

    @pl.when(len_ref[1] > 0)
    def _():
        pos_acc[...] += tn(low, sel_low[0])

    normed = (patches[...].astype(F32) - stats[0:1, :]) * stats[1:2, :]
    sums[0] += fold(grad * n)
    sums[1] += fold(grad)
    sums[2] += nn(ones, parts[0])
    sums[3] += nn(ones, parts[2])
    sums[4] += fold(total)
    sums[5] += fold(total * normed)

    @pl.when(last)
    def _():
        g_qkv[...] = acc[...].astype(BF)
        g_pos[...] = pos_acc[...].astype(BF)
        for i in range(6):
            line = sums[i]
            g_small[i : i + 1, :] = line[0:1] if i in (2, 3) else jnp.sum(line, axis=0, keepdims=True)
        g_small[6:8, :] = jnp.zeros((2, width), F32)


def first_back(lengths, gq, gk, gv, first, emb, res_grad, patches, stats, table, w_qkv, vec):
    rows, width = emb.shape
    block = 256
    once = pl.Buffered(1)
    whole = lambda shape: pl.BlockSpec(shape, lambda i, s: (0,) * len(shape), pipeline_mode=once)
    by_row = lambda n: pl.BlockSpec((block, n), lambda i, s: (i, 0))
    out_shape = [
        jax.ShapeDtypeStruct((width, 3 * width), BF),
        jax.ShapeDtypeStruct((width, POS_PAD), BF),
        jax.ShapeDtypeStruct((rows, width), F32),
        jax.ShapeDtypeStruct((8, width), F32),
    ]
    return pl.pallas_call(
        first_kernel,
        name="first_back",
        grid_spec=pltpu.PrefetchScalarGridSpec(
            num_scalar_prefetch=1,
            grid=(rows // block,),
            in_specs=[by_row(width)] * 7
            + [
                whole(stats.shape),
                pl.BlockSpec((1, block, POS_PAD), lambda i, s: (jnp.where(s[1] > 0, 1, 0), i, 0)),
                pl.BlockSpec((1, block, POS_PAD), lambda i, s: (2, i, 0)),
                whole(w_qkv.shape),
                whole(vec.shape),
            ],
            out_specs=[
                whole(out_shape[0].shape),
                whole(out_shape[1].shape),
                by_row(width),
                whole(out_shape[3].shape),
            ],
            scratch_shapes=[
                pltpu.VMEM((width, 3 * width), F32),
                pltpu.VMEM((width, POS_PAD), F32),
                pltpu.VMEM((6, 8, width), F32),
            ],
        ),
        out_shape=out_shape,
        compiler_params=pltpu.CompilerParams(vmem_limit_bytes=VMEM_LIMIT),
        cost_estimate=pl.CostEstimate(
            flops=2 * rows * width * (6 * width + POS_PAD),
            bytes_accessed=30 * 2**20,
            transcendentals=0,
        ),
    )(lengths, gq, gk, gv, first, emb, res_grad, patches, stats, table, table, w_qkv, vec)


def clip_features(lengths, local_rows):
    position = jnp.arange(local_rows, dtype=jnp.int32)
    first_len, both = lengths[0], lengths[0] + lengths[1]
    segment = jnp.where(position < first_len, 0, jnp.where(position < both, 1, 2))
    lane = jnp.arange(128, dtype=jnp.int32)
    same = (segment[:, None] == lane[None, :]).astype(F32)
    other = jnp.where(lane[None, :] < 3, -1e30 * (1.0 - same), 0.0)
    return same.astype(BF), other.astype(BF)


def local(
    D, F,
    patches, cotangent, clip_len,
    pos_table, vector_params, w_qkv, w_proj, w_fc1, b_fc1, w_fc2,
    *states,
):
    params = (pos_table, vector_params, w_qkv, w_proj, w_fc1, b_fc1, w_fc2)
    momenta, averages = states[:7], states[7:]
    local_rows, width = patches.shape
    hidden = w_fc1.shape[1]
    group_size = D * F
    X, Y = F // 4, 2
    lengths = clip_len[0]
    table = selectors(local_rows)
    q_seg, k_seg = clip_features(lengths, local_rows)
    valid = jnp.broadcast_to(
        (jnp.arange(local_rows) < lengths[0] + lengths[1]).astype(F32)[:, None], (local_rows, 128)
    )
    n_vec, n_bias = vector_params.size, b_fc1.size
    small = jnp.concatenate([vector_params.reshape(-1), b_fc1])
    small = jnp.pad(small, (0, 2048 - small.size)).astype(BF).reshape(16, 128)
    shards = (
        small,
        jnp.pad(pos_table, ((0, 0), (0, POS_PAD - LONG))).astype(BF),
        w_qkv.astype(BF),
        w_proj.astype(BF),
        w_fc1.astype(BF),
        w_fc2.astype(BF),
    )
    sums, *full = gather_all(D, F, patches, valid, shards, 0)
    small_full, pos_full, qkv_full, proj_full, fc1_full, fc2_full = full
    small_full = small_full.reshape(group_size, 2048).astype(F32)
    vec = small_full[:, :n_vec].reshape(width, 8).T
    bias_full = small_full[:, n_vec : n_vec + n_bias].reshape(1, hidden)
    pos_full, qkv_full, proj_full, fc1_full, fc2_full = (
        w.reshape(-1, w.shape[-1]) for w in (pos_full, qkv_full, proj_full, fc1_full, fc2_full)
    )
    valid_count = sums[2, 0]
    feature_mean = sums[0] / valid_count
    feature_var = sums[1] / valid_count - feature_mean * feature_mean
    inv_std = lax.rsqrt(feature_var + INPUT_EPS)
    stats = jnp.stack([feature_mean, inv_std] + [jnp.zeros_like(inv_std)] * 6)
    qkv_bias = jnp.concatenate([vec[2], jnp.zeros_like(vec[2]), vec[3]])[None, :]
    emb, first, qkv = embed(lengths, patches, stats, table, pos_full, vec, qkv_bias, qkv_full)
    attended, lse = attend_forward(qkv, q_seg, k_seg)
    layer_out, res_grad, att_grad, delta, g_proj, g_fc1, g_b1, g_fc2, g_small_mid = middle(
        lengths, emb, attended, cotangent, proj_full, fc1_full, bias_full, fc2_full, vec
    )
    delta = jnp.pad(delta[:HEADS].reshape(HEADS // 2, 2, local_rows), ((0, 0), (0, 6), (0, 0)))
    gq, gk, gv = attend_backward(qkv, att_grad, q_seg, k_seg, lse, delta)
    g_qkv, g_pos, g_masked, g_small_first = first_back(
        lengths, gq, gk, gv, first, emb, res_grad, patches, stats, table, qkv_full, vec
    )
    small_grads = jnp.concatenate(
        [
            g_small_first[:4],
            g_small_mid[:4],
            g_small_first[4:6],
            g_b1[0].reshape(-1, width),
            jnp.zeros((16 - 10 - hidden // width, width), F32),
        ]
    )
    grads = [
        g.reshape(D, Y, X, 2, -1, g.shape[-1]) for g in (g_fc2, g_fc1, g_proj, g_qkv, g_pos)
    ]
    small_sum, *totals = scatter_all(D, F, small_grads, grads, 1)
    normed = (patches.astype(F32) - feature_mean) * inv_std
    valid_col = valid[:, :1]
    patch_grad = (
        inv_std
        * (
            g_masked
            - valid_col * (small_sum[8] / valid_count)
            - valid_col * normed * (small_sum[9] / valid_count)
        )
    ).astype(BF)
    me = lax.axis_index("dp") * F + lax.axis_index("fsdp")
    n_rows = vector_params.shape[0]
    g_vec = lax.dynamic_slice(small_sum[:8], (0, me * n_rows), (8, n_rows)).T
    g_bias = lax.dynamic_slice(small_sum[10 : 10 + hidden // width].reshape(-1), (me * n_bias,), (n_bias,))
    grad_shards = (totals[4][:, :LONG], g_vec, totals[3], totals[2], totals[1], g_bias, totals[0])
    rate = 0.02 * (local_rows * group_size) ** (-0.5)
    average_keep = min(0.99, (1.0 + PRIOR_STEPS) / (10.0 + PRIOR_STEPS))
    next_moms = tuple(MOMENTUM * m + g for m, g in zip(momenta, grad_shards))
    updates = tuple(-(rate * (g + MOMENTUM * m)) for g, m in zip(grad_shards, next_moms))
    next_averages = tuple(
        average_keep * a + (1.0 - average_keep) * (w + u)
        for a, w, u in zip(averages, params, updates)
    )
    feature_stats = jnp.stack([feature_mean, feature_var])
    return (
        (layer_out, patch_grad, feature_stats) + grad_shards + updates + next_moms + next_averages
    )


def solution(mesh):
    rows, line = P(AXES, None), P(AXES)
    params = (rows, rows, rows, rows, rows, line, rows)
    return jax.shard_map(
        partial(local, mesh.shape["dp"], mesh.shape["fsdp"]),
        mesh=mesh,
        in_specs=(rows,) * 3 + params * 3,
        out_specs=(rows, rows, P()) + params * 4,
        check_vma=False,
    )
```

```python
from functools import partial

import jax
import jax.numpy as jnp
import ml_dtypes
import numpy as np
from jax import lax
from jax.experimental import pallas as pl
from jax.experimental.pallas import tpu as pltpu
from jax.sharding import PartitionSpec as P

HEADS = 12
FREQ_L = 12
TIME_L = 101
FREQ_S = 8
TIME_S = 64
PRIOR_STEPS = 3
LONG = 1214
SHORT = 514

NORM_EPS = 1e-06
INPUT_EPS = 1e-05
MOMENTUM = 0.9
MESH = pl.DeviceIdType.MESH
AXES = ("dp", "fsdp")
BF = jnp.bfloat16
F32 = jnp.float32
VMEM_LIMIT = 60 * 2**20
POS_PAD = 1280
FORWARD_PARTS = (1, 4, 3)
BACKWARD_PARTS = (3, 4, 1)

TAIL_P = 0.305
TAIL_C = (
    0.121639732,
    0.122466826,
    0.10342081,
    0.121021868,
    -0.037977191,
    0.185717298,
    -0.152988541,
    0.036699245,
)


def resize_rows(size_in, size_out):
    resize_table = np.zeros((size_out, size_in), np.float64)
    for target_row in range(size_out):
        source_pos = max((target_row + 0.5) * size_in / size_out - 0.5, 0.0)
        lower_cell = min(int(np.floor(source_pos)), size_in - 1)
        upper_cell = min(lower_cell + 1, size_in - 1)
        fraction = source_pos - lower_cell
        resize_table[target_row, lower_cell] += 1.0 - fraction
        resize_table[target_row, upper_cell] += fraction
    return resize_table


def selectors(local_rows):
    table = np.zeros((3, local_rows, POS_PAD), np.float64)
    table[0, :LONG, :LONG] = np.eye(LONG)
    short = np.zeros((SHORT, LONG), np.float64)
    short[0, 0] = short[1, 1] = 1.0
    short[2:, 2:] = np.kron(resize_rows(FREQ_L, FREQ_S), resize_rows(TIME_L, TIME_S))
    high = short.astype(ml_dtypes.bfloat16).astype(np.float64)
    for first in (0, SHORT):
        table[1, first : first + SHORT, :LONG] = high
        table[2, first : first + SHORT, :LONG] = short - high
    return jnp.asarray(table.astype(ml_dtypes.bfloat16))


def nn(left, right):
    return lax.dot_general(left, right, (((1,), (0,)), ((), ())), preferred_element_type=F32)


def nt(left, right):
    return lax.dot_general(left, right, (((1,), (1,)), ((), ())), preferred_element_type=F32)


def tn(left, right):
    return lax.dot_general(left, right, (((0,), (0,)), ((), ())), preferred_element_type=F32)


class Place:
    def __init__(self, dp_size, fsdp_size):
        self.D, self.F = dp_size, fsdp_size
        self.X, self.Y = fsdp_size // 4, 2
        self.d = lax.axis_index("dp")
        self.f = lax.axis_index("fsdp")
        self.c = lax.rem(self.f, 2)
        self.x = lax.rem(lax.div(self.f, 2), self.X)
        self.y = lax.div(self.f, 2 * self.X)

    def fs(self, y, x, c):
        return (y * self.X + x) * 2 + c

    def up(self, value, step, size):
        return lax.rem(value + step, size)

    def partners(self):
        out = [(self.up(self.d, k, self.D), self.f) for k in range(1, self.D)]
        out += [(self.d, self.fs(self.y, self.up(self.x, k, self.X), self.c)) for k in range(1, self.X)]
        out += [(self.d, self.fs(self.up(self.y, k, self.Y), self.x, self.c)) for k in range(1, self.Y)]
        out.append((self.d, self.fs(self.y, self.x, 1 - self.c)))
        return out

    def everyone(self):
        out = [(self.up(self.d, k, self.D), self.f) for k in range(1, self.D)]
        return out + [(self.d, self.up(self.f, k, self.F)) for k in range(1, self.F)]


def meet(devices):
    barrier = pltpu.get_barrier_semaphore()
    for device in devices:
        pl.semaphore_signal(barrier, inc=1, device_id=device, device_id_type=MESH)
    pl.semaphore_wait(barrier, len(devices))


class Gather:
    @staticmethod
    def count(D, X, Y):
        return (D - 1) + 2 * (X - 1) + 2 * (Y - 1) + 1

    def __init__(self, at, src, out, send, recv, own):
        self.at, self.src, self.out, self.send, self.recv, self.own = at, src, out, send, recv, own
        D, X, Y = at.D, at.X, at.Y
        self.n_z = 0
        self.n_x = D - 1
        self.n_y = self.n_x + X - 1
        self.n_c = self.n_y + Y - 1

    def copy(self, src, dst, number, device):
        return pltpu.make_async_remote_copy(
            src_ref=src,
            dst_ref=dst,
            send_sem=self.send.at[number],
            recv_sem=self.recv.at[number],
            device_id=device,
            device_id_type=MESH,
        )

    def z_copy(self, k):
        at = self.at
        return self.copy(
            self.src,
            self.out.at[at.d, at.y, at.x, at.c],
            self.n_z + k - 1,
            (at.up(at.d, k, at.D), at.f),
        )

    def z_got(self, k):
        at = self.at
        here = self.out.at[at.up(at.d, at.D - k, at.D), at.y, at.x, at.c]
        return self.copy(here, here, self.n_z + k - 1, (at.up(at.d, at.D - k, at.D), at.f))

    def part(self, axis, order, y, x, c):
        if axis == order[0]:
            return self.out.at[:, y, x, c]
        return self.out.at[:, y, :, c] if axis == "y" else self.out.at[:, :, x, c]

    def side(self, axis, order, k, sent):
        at = self.at
        size = at.X if axis == "x" else at.Y
        first = self.n_x if axis == "x" else self.n_y
        mine = at.x if axis == "x" else at.y
        other = at.up(mine, k if sent else size - k, size)
        y, x = (at.y, other) if axis == "x" else (other, at.x)
        block = self.part(axis, order, at.y, at.x, at.c) if sent else self.part(axis, order, y, x, at.c)
        return self.copy(block, block, first + k - 1, (at.d, at.fs(y, x, at.c)))

    def pieces(self, order, c):
        at = self.at
        out = [self.out.at[:, at.y, at.x, c]]
        for axis in order:
            size = at.X if axis == "x" else at.Y
            for k in range(1, size):
                other = at.up(at.x if axis == "x" else at.y, size - k, size)
                y, x = (at.y, other) if axis == "x" else (other, at.x)
                out.append(self.part(axis, order, y, x, c))
        return out

    def sibling(self, block, number):
        at = self.at
        return self.copy(block, block, self.n_c + number, (at.d, at.fs(at.y, at.x, 1 - at.c)))

    def local(self):
        at = self.at
        return pltpu.make_async_copy(self.src, self.out.at[at.d, at.y, at.x, at.c], self.own)

    def size_of(self, axis):
        return self.at.X if axis == "x" else self.at.Y

    def phase(self, number):
        at = self.at
        if number == 0:
            self.local().start()
            for k in range(1, at.D):
                self.z_copy(k).start()
            return
        if number == 1:
            self.local().wait()
            for k in range(1, at.D):
                self.z_got(k).wait_recv()
        for core, order in ((0, ("x", "y")), (1, ("y", "x"))):

            @pl.when(at.c == core)
            def _(core=core, order=order):
                mine = self.pieces(order, core)
                first = 1 + (self.size_of(order[0]) - 1)
                if number == 1:
                    for k in range(1, self.size_of(order[0])):
                        self.side(order[0], order, k, True).start()
                    self.sibling(mine[0], 0).start()
                elif number == 2:
                    for k in range(1, self.size_of(order[0])):
                        self.side(order[0], order, k, False).wait_recv()
                    for k in range(1, self.size_of(order[1])):
                        self.side(order[1], order, k, True).start()
                    for i in range(1, first):
                        self.sibling(mine[i], i).start()
                elif number == 3:
                    for k in range(1, self.size_of(order[1])):
                        self.side(order[1], order, k, False).wait_recv()
                    for i in range(first, len(mine)):
                        self.sibling(mine[i], i).start()
                elif number == 4:
                    for k in range(1, at.D):
                        self.z_copy(k).wait_send()
                    for axis in order:
                        for k in range(1, self.size_of(axis)):
                            self.side(axis, order, k, True).wait_send()
                    for i, block in enumerate(mine):
                        self.sibling(block, i).wait_send()
                    for i, block in enumerate(self.pieces(order[::-1], 1 - core)):
                        self.sibling(block, i).wait_recv()


class Scatter:
    @staticmethod
    def count(D, X, Y):
        return 1 + (Y - 1) + (X - 1) + (D - 1)

    @staticmethod
    def scratch(D, X, Y, R, N):
        return [
            pltpu.VMEM((D, Y, X, R, N), BF),
            pltpu.VMEM((D, Y, X, R, N), BF),
            pltpu.VMEM((Y - 1, D, X, R, N), BF),
            pltpu.VMEM((Y - 1, D, R, N), BF),
        ] + ([] if X == Y else [pltpu.VMEM((X - 1, D, Y, R, N), BF), pltpu.VMEM((X - 1, D, R, N), BF)]) + [
            pltpu.VMEM((D - 1, R, N), BF)
        ]

    def __init__(self, at, grad, total, bufs, send, recv, own):
        self.at, self.grad, self.total = at, grad, total
        self.acc, self.r1, self.r2y, self.r3y = bufs[:4]
        self.r2x, self.r3x = (self.r2y, self.r3y) if at.X == at.Y else bufs[4:6]
        self.r4 = bufs[-1]
        self.send, self.recv, self.own = send, recv, own
        self.n_y = 1
        self.n_x = self.n_y + at.Y - 1
        self.n_z = self.n_x + at.X - 1

    def copy(self, src, dst, number, device):
        return pltpu.make_async_remote_copy(
            src_ref=src,
            dst_ref=dst,
            send_sem=self.send.at[number],
            recv_sem=self.recv.at[number],
            device_id=device,
            device_id_type=MESH,
        )

    def core_copy(self):
        at = self.at
        return self.copy(
            self.grad.at[:, :, :, 1 - at.c], self.r1, 0, (at.d, at.fs(at.y, at.x, 1 - at.c))
        )

    def local(self):
        return pltpu.make_async_copy(self.grad.at[:, :, :, self.at.c], self.acc, self.own)

    def side(self, axis, order, k):
        at = self.at
        if axis == "y":
            y = at.up(at.y, k, at.Y)
            device = (at.d, at.fs(y, at.x, at.c))
            if axis == order[0]:
                return self.copy(self.acc.at[:, y], self.r2y.at[k - 1], self.n_y + k - 1, device)
            return self.copy(self.acc.at[:, y, at.x], self.r3y.at[k - 1], self.n_y + k - 1, device)
        x = at.up(at.x, k, at.X)
        device = (at.d, at.fs(at.y, x, at.c))
        if axis == order[0]:
            return self.copy(self.acc.at[:, :, x], self.r2x.at[k - 1], self.n_x + k - 1, device)
        return self.copy(self.acc.at[:, at.y, x], self.r3x.at[k - 1], self.n_x + k - 1, device)

    def z_copy(self, k):
        at = self.at
        d = at.up(at.d, k, at.D)
        return self.copy(
            self.acc.at[d, at.y, at.x], self.r4.at[k - 1], self.n_z + k - 1, (d, at.f)
        )

    def size_of(self, axis):
        return self.at.X if axis == "x" else self.at.Y

    def phase(self, number):
        at, acc = self.at, self.acc
        if number == 0:
            self.local().start()
            self.core_copy().start()
            return
        if number == 1:
            self.local().wait()
            self.core_copy().wait_recv()

            def add(i, _):
                d, rest = lax.div(i, at.Y * at.X), lax.rem(i, at.Y * at.X)
                y, x = lax.div(rest, at.X), lax.rem(rest, at.X)
                acc[d, y, x] = acc[d, y, x] + self.r1[d, y, x]
                return 0

            lax.fori_loop(0, at.D * at.Y * at.X, add, 0)
        if number == 4:
            for k in range(1, at.D):
                self.z_copy(k).wait_recv()
            total = acc[at.d, at.y, at.x].astype(F32)
            for k in range(1, at.D):
                total = total + self.r4[k - 1].astype(F32)
            self.total[...] = total
            self.core_copy().wait_send()
            for k in range(1, at.D):
                self.z_copy(k).wait_send()
        for core, order in ((0, ("y", "x")), (1, ("x", "y"))):

            @pl.when(at.c == core)
            def _(core=core, order=order):
                n0, n1 = self.size_of(order[0]), self.size_of(order[1])
                if number == 1:
                    for k in range(1, n0):
                        self.side(order[0], order, k).start()
                elif number == 2:
                    for k in range(1, n0):
                        self.side(order[0], order, k).wait_recv()

                    def add(i, _):
                        d, j = lax.div(i, n1), lax.rem(i, n1)
                        y, x = (at.y, j) if order[0] == "y" else (j, at.x)
                        got = self.r2y if order[0] == "y" else self.r2x
                        value = acc[d, y, x]
                        for k in range(1, n0):
                            value = value + got[k - 1, d, j]
                        acc[d, y, x] = value
                        return 0

                    lax.fori_loop(0, at.D * n1, add, 0)
                    for k in range(1, n1):
                        self.side(order[1], order, k).start()
                elif number == 3:
                    for k in range(1, n1):
                        self.side(order[1], order, k).wait_recv()

                    def add(d, _):
                        got = self.r3y if order[1] == "y" else self.r3x
                        value = acc[d, at.y, at.x]
                        for k in range(1, n1):
                            value = value + got[k - 1, d]
                        acc[d, at.y, at.x] = value
                        return 0

                    lax.fori_loop(0, at.D, add, 0)
                elif number == 4:
                    for axis in order:
                        for k in range(1, self.size_of(axis)):
                            self.side(axis, order, k).wait_send()

        if number == 3:
            for k in range(1, at.D):
                self.z_copy(k).start()


class Total:
    @staticmethod
    def count(D, F):
        return (D - 1) + (F - 1)

    @staticmethod
    def scratch(D, F, rows, cols):
        return [pltpu.VMEM((D, rows, cols), F32), pltpu.VMEM((F, rows, cols), F32)]

    def __init__(self, at, bufs, send, recv):
        self.at, self.send, self.recv = at, send, recv
        self.z_buf, self.f_buf = bufs

    def copy(self, buf, slot, number, device):
        return pltpu.make_async_remote_copy(
            src_ref=buf.at[slot],
            dst_ref=buf.at[slot],
            send_sem=self.send.at[number],
            recv_sem=self.recv.at[number],
            device_id=device,
            device_id_type=MESH,
        )

    def z_copy(self, k, sent):
        at = self.at
        other = at.up(at.d, k if sent else at.D - k, at.D)
        return self.copy(self.z_buf, at.d if sent else other, k - 1, (other, at.f))

    def f_copy(self, k, sent):
        at = self.at
        other = at.up(at.f, k if sent else at.F - k, at.F)
        return self.copy(self.f_buf, at.f if sent else other, at.D - 1 + k - 1, (at.d, other))

    def start(self, value):
        at = self.at
        self.z_buf[at.d] = value
        for k in range(1, at.D):
            self.z_copy(k, True).start()

    def middle(self):
        at = self.at
        for k in range(1, at.D):
            self.z_copy(k, False).wait_recv()
        total = self.z_buf[0]
        for i in range(1, at.D):
            total = total + self.z_buf[i]
        self.f_buf[at.f] = total
        for k in range(1, at.F):
            self.f_copy(k, True).start()

    def end(self):
        at = self.at
        for k in range(1, at.F):
            self.f_copy(k, False).wait_recv()
        total = self.f_buf[0]
        for i in range(1, at.F):
            total = total + self.f_buf[i]
        for k in range(1, at.D):
            self.z_copy(k, True).wait_send()
        for k in range(1, at.F):
            self.f_copy(k, True).wait_send()
        return total


LAGS = (0, 1, 3, 5, 6)


def steps_of(arrays):
    for step in range(len(arrays) + LAGS[-1]):
        yield [
            (arrays[i], LAGS.index(step - i))
            for i in reversed(range(len(arrays)))
            if step - i in LAGS
        ]


def spread(arrays, slots):
    steps = list(steps_of(arrays))
    due = {slot: [] for slot in range(slots)}
    for i, step in enumerate(steps):
        due[(i * (slots - 1)) // (len(steps) - 1)] += step
    return due


def columns(ref, part, parts):
    size = ref.shape[-1] // parts
    return ref.at[(slice(None),) * (len(ref.shape) - 1) + (pl.ds(part * size, size),)]


def gather_kernel(D, F, parts, patches_ref, valid_ref, *refs):
    count = len(parts)
    srcs, stats_ref, outs = refs[:count], refs[count], refs[count + 1 : 2 * count + 1]
    z_buf, f_buf, s_send, s_recv, send, recv, own = refs[2 * count + 1 :]
    at = Place(D, F)
    meet(at.everyone())
    pieces = [
        (columns(srcs[i], j, parts[i]), columns(outs[i], j, parts[i]))
        for i in range(count)
        for j in range(parts[i])
    ]
    arrays = [
        Gather(at, src, out, send.at[i], recv.at[i], own.at[i]) for i, (src, out) in enumerate(pieces)
    ]
    steps = list(steps_of(arrays))
    arrays[0].phase(0)
    arrays[1].phase(0)
    rows = patches_ref.shape[0]
    step_rows = 64

    def accumulate(i, sums):
        block = pl.ds(pl.multiple_of(i * step_rows, step_rows), step_rows)
        values = patches_ref[block, :].astype(F32)
        values = values * valid_ref[block, :1]
        first = values.reshape(step_rows // 8, 8, -1)
        return (sums[0] + jnp.sum(first, axis=0), sums[1] + jnp.sum(first * first, axis=0))

    empty = jnp.zeros((8, patches_ref.shape[1]), F32)
    plain, square = lax.fori_loop(0, rows // step_rows, accumulate, (empty, empty))
    valid_sum = jnp.sum(valid_ref[...], axis=0, keepdims=True)[:, :1]
    row = lax.broadcasted_iota(jnp.int32, empty.shape, 0)
    plain = jnp.sum(plain, axis=0, keepdims=True)
    square = jnp.sum(square, axis=0, keepdims=True)
    packed = jnp.where(row == 0, plain, jnp.where(row == 1, square, jnp.where(row == 2, valid_sum, 0.0)))
    total = Total(at, (z_buf, f_buf), s_send, s_recv)
    total.start(packed)
    for number, step in enumerate(steps):
        for array, phase in step:
            if phase > 0 or array not in arrays[:2]:
                array.phase(phase)
        if number == 3:
            total.middle()
        if number == 6:
            stats_ref[...] = total.end()


def gather_all(D, F, patches, valid, shards, parts, collective_id):
    X, Y = F // 4, 2
    count = len(shards)
    n = Gather.count(D, X, Y)
    hbm = pl.BlockSpec(memory_space=pl.ANY)
    vmem = pl.BlockSpec(memory_space=pltpu.VMEM)
    width = patches.shape[1]
    sent = sum(s.size for s in shards) * 2 * D * F
    return pl.pallas_call(
        partial(gather_kernel, D, F, parts),
        name="gather_weights",
        out_shape=[jax.ShapeDtypeStruct((8, width), F32)]
        + [jax.ShapeDtypeStruct((D, Y, X, 2) + s.shape, s.dtype) for s in shards],
        in_specs=[vmem, vmem] + [hbm] * count,
        out_specs=[vmem] + [hbm] * count,
        scratch_shapes=Total.scratch(D, F, 8, width)
        + [pltpu.SemaphoreType.DMA((Total.count(D, F),)), pltpu.SemaphoreType.DMA((Total.count(D, F),))]
        + [
            pltpu.SemaphoreType.DMA((sum(parts), n)),
            pltpu.SemaphoreType.DMA((sum(parts), n)),
            pltpu.SemaphoreType.DMA((sum(parts),)),
        ],
        compiler_params=pltpu.CompilerParams(
            collective_id=collective_id, has_side_effects=True, vmem_limit_bytes=VMEM_LIMIT
        ),
        cost_estimate=pl.CostEstimate(flops=0, bytes_accessed=sent, transcendentals=0),
    )(patches, valid, *shards)


def pieces_of(grads, totals, parts):
    return [
        (columns(g, j, n), columns(t, j, n)) for g, t, n in zip(grads, totals, parts) for j in range(n)
    ]


def scatter_arrays(at, pieces, bufs, send, recv, own):
    per = len(bufs) // len(pieces)
    return [
        Scatter(at, grad, total, bufs[i * per : (i + 1) * per], send.at[i], recv.at[i], own.at[i])
        for i, (grad, total) in enumerate(pieces)
    ]


def scatter_scratch(D, X, Y, grads, parts):
    out = []
    for g, n in zip(grads, parts):
        for _ in range(n):
            out += Scatter.scratch(D, X, Y, g.shape[-2], g.shape[-1] // n)
    return out


def copy_semaphores(count, n):
    return [
        pltpu.SemaphoreType.DMA((count, n)),
        pltpu.SemaphoreType.DMA((count, n)),
        pltpu.SemaphoreType.DMA((count,)),
    ]


def scatter_kernel(D, F, parts, small_ref, *refs):
    count = len(parts)
    grads, small_out, totals = refs[:count], refs[count], refs[count + 1 : 2 * count + 1]
    rest = refs[2 * count + 1 :]
    bufs, (z_buf, f_buf, s_send, s_recv, send, recv, own) = rest[:-7], rest[-7:]
    at = Place(D, F)
    meet(at.everyone())
    arrays = scatter_arrays(at, pieces_of(grads, totals, parts), bufs, send, recv, own)
    total = Total(at, (z_buf, f_buf), s_send, s_recv)
    for number, step in enumerate(steps_of(arrays)):
        for array, phase in step:
            array.phase(phase)
        if number == 0:
            total.start(small_ref[...])
        if number == 3:
            total.middle()
        if number == 6:
            small_out[...] = total.end()


def scatter_all(D, F, small, grads, parts, collective_id):
    X, Y = F // 4, 2
    count = len(grads)
    n = Scatter.count(D, X, Y)
    hbm = pl.BlockSpec(memory_space=pl.ANY)
    vmem = pl.BlockSpec(memory_space=pltpu.VMEM)
    scratch = scatter_scratch(D, X, Y, grads, parts)
    return pl.pallas_call(
        partial(scatter_kernel, D, F, parts),
        name="scatter_grads",
        out_shape=[jax.ShapeDtypeStruct(small.shape, F32)]
        + [jax.ShapeDtypeStruct(g.shape[-2:], F32) for g in grads],
        in_specs=[vmem] + [hbm] * count,
        out_specs=[vmem] * (1 + count),
        scratch_shapes=scratch
        + Total.scratch(D, F, *small.shape)
        + [pltpu.SemaphoreType.DMA((Total.count(D, F),)), pltpu.SemaphoreType.DMA((Total.count(D, F),))]
        + copy_semaphores(sum(parts), n),
        compiler_params=pltpu.CompilerParams(
            collective_id=collective_id, has_side_effects=True, vmem_limit_bytes=VMEM_LIMIT
        ),
        cost_estimate=pl.CostEstimate(
            flops=0, bytes_accessed=sum(g.size for g in grads) * 4, transcendentals=0
        ),
    )(small, *grads)


def row_of(first, rows, width):
    return first + lax.broadcasted_iota(jnp.int32, (rows, width), 0)


def embed_kernel(len_ref, patches, stats, sel, sel_low, pos, vec, bias, w_ref, emb_out, norm_out, q_out, acc):
    rows, width = patches.shape
    mean, inv_std = stats[0:1, :], stats[1:2, :]
    normed = (patches[...].astype(F32) - mean) * inv_std
    acc[...] = nt(sel[0], pos[...])

    @pl.when(len_ref[1] > 0)
    def _():
        acc[...] += nt(sel_low[0], pos[...])

    row = row_of(pl.program_id(0) * rows, rows, width)
    embedded = jnp.where(row < len_ref[0] + len_ref[1], normed + acc[...], 0.0)
    emb_out[...] = embedded
    center = embedded - jnp.mean(embedded, axis=1, keepdims=True)
    spread = jnp.mean(center * center, axis=1, keepdims=True)
    first = (center * lax.rsqrt(spread + NORM_EPS) * vec[0:1, :] + vec[1:2, :]).astype(BF)
    norm_out[...] = first
    q_out[...] = (nn(first, w_ref[...]) + bias[...]).astype(BF)


def embed(lengths, patches, stats, table, pos, vec, qkv_bias, w_qkv):
    rows, width = patches.shape
    block = 256
    whole = lambda a: pl.BlockSpec(a.shape, lambda i, s: (0,) * a.ndim, pipeline_mode=pl.Buffered(1))
    by_row = lambda n: pl.BlockSpec((block, n), lambda i, s: (i, 0))
    return pl.pallas_call(
        embed_kernel,
        name="embed",
        grid_spec=pltpu.PrefetchScalarGridSpec(
            num_scalar_prefetch=1,
            grid=(rows // block,),
            in_specs=[
                by_row(width),
                whole(stats),
                pl.BlockSpec((1, block, POS_PAD), lambda i, s: (jnp.where(s[1] > 0, 1, 0), i, 0)),
                pl.BlockSpec((1, block, POS_PAD), lambda i, s: (2, i, 0)),
                whole(pos),
                whole(vec),
                whole(qkv_bias),
                whole(w_qkv),
            ],
            out_specs=[by_row(width), by_row(width), by_row(3 * width)],
            scratch_shapes=[pltpu.VMEM((block, width), F32)],
        ),
        out_shape=[
            jax.ShapeDtypeStruct((rows, width), F32),
            jax.ShapeDtypeStruct((rows, width), BF),
            jax.ShapeDtypeStruct((rows, 3 * width), BF),
        ],
        compiler_params=pltpu.CompilerParams(vmem_limit_bytes=VMEM_LIMIT),
        cost_estimate=pl.CostEstimate(
            flops=2 * rows * width * (3 * width + POS_PAD), bytes_accessed=24 * 2**20, transcendentals=0
        ),
    )(lengths, patches, stats, table, table, pos, vec, qkv_bias, w_qkv)


def attend_pair(q_ref, k_ref, v_ref, qs_ref, ks_ref, q_block):
    rows = q_ref.shape[0]
    lane = lax.broadcasted_iota(jnp.int32, (q_block, 128), 1)

    def half(values, head):
        keep = lane < 64 if head == 0 else lane >= 64
        return jnp.where(keep, values, jnp.zeros_like(values))

    def query(block, head):
        scaled = q_ref[block, :] * jnp.asarray(0.125, BF)
        return jnp.concatenate([half(scaled, head), qs_ref[block, :]], axis=1)

    keys = jnp.concatenate([k_ref[...], ks_ref[...]], axis=1)
    return keys, query, half


def forward_pair(D, F, q_ref, k_ref, v_ref, qs_ref, ks_ref, proj_ref, fc1_ref, fc2_ref, *refs):
    out_ref, lse_ref, proj_out, fc1_out, fc2_out = refs[:5]
    key_buf, v_buf, o_buf, send, recv, own = refs[5:]
    pair = pl.program_id(0)
    rows = q_ref.shape[0]
    q_block = 256
    blocks = rows // q_block
    at = Place(D, F)

    @pl.when(pair == 0)
    def _():
        meet(at.partners())

    pieces = pieces_of((proj_ref, fc1_ref, fc2_ref), (proj_out, fc1_out, fc2_out), FORWARD_PARTS)
    arrays = [
        Gather(at, src, out, send.at[i], recv.at[i], own.at[i]) for i, (src, out) in enumerate(pieces)
    ]
    due = spread(arrays, (HEADS // 2) * blocks)
    keys, query, _ = attend_pair(q_ref, k_ref, v_ref, qs_ref, ks_ref, q_block)
    key_buf[...] = keys
    v_t = jnp.transpose(v_ref[...])
    ones = jnp.ones((16, rows), BF)
    for head in range(2):
        v_buf[head] = jnp.concatenate([v_t[64 * head : 64 * head + 64], ones], axis=0)
    for i in range(blocks):
        run_due(due, pair, i, blocks)
        block = pl.ds(i * q_block, q_block)
        for head in range(2):
            scores = nt(key_buf[...], query(block, head))
            top = jnp.max(scores, axis=0, keepdims=True)
            probs = jnp.exp(scores - top).astype(BF)
            out = nn(v_buf[head], probs)
            total = out[64:65, :]
            o_buf[64 * head : 64 * head + 64, block] = (out[:64] / total).astype(BF)
            lse_ref[0, head : head + 1, block] = top + jnp.log(total)
    out_ref[...] = jnp.transpose(o_buf[...])


def run_due(due, pair, i, blocks):
    for k in range(HEADS // 2):
        if due[k * blocks + i]:

            @pl.when(pair == k)
            def _(work=due[k * blocks + i]):
                for array, number in work:
                    array.phase(number)


def pair_specs(rows):
    pair = lambda first: pl.BlockSpec((rows, 128), lambda p: (0, first + p))
    whole = pl.BlockSpec((rows, 128), lambda p: (0, 0))
    return pair, whole


def attend_forward(D, F, qkv, q_seg, k_seg, shards, collective_id):
    rows = qkv.shape[0]
    pairs = HEADS // 2
    pair, whole = pair_specs(rows)
    hbm = pl.BlockSpec(memory_space=pl.ANY)
    X, Y = F // 4, 2
    n = Gather.count(D, X, Y)
    return pl.pallas_call(
        partial(forward_pair, D, F),
        name="attend_forward",
        grid=(pairs,),
        in_specs=[pair(0), pair(pairs), pair(2 * pairs), whole, whole] + [hbm] * 3,
        out_specs=[pair(0), pl.BlockSpec((1, 8, rows), lambda p: (p, 0, 0))] + [hbm] * 3,
        out_shape=[
            jax.ShapeDtypeStruct((rows, 128 * pairs), BF),
            jax.ShapeDtypeStruct((pairs, 8, rows), F32),
        ]
        + [jax.ShapeDtypeStruct((D, Y, X, 2) + s.shape, s.dtype) for s in shards],
        scratch_shapes=[
            pltpu.VMEM((rows, 256), BF),
            pltpu.VMEM((2, 80, rows), BF),
            pltpu.VMEM((128, rows), BF),
        ]
        + copy_semaphores(sum(FORWARD_PARTS), n),
        compiler_params=pltpu.CompilerParams(
            collective_id=collective_id, has_side_effects=True, vmem_limit_bytes=VMEM_LIMIT
        ),
        cost_estimate=pl.CostEstimate(
            flops=4 * 12 * rows * rows * 256,
            bytes_accessed=8 * rows * 768,
            transcendentals=12 * rows * rows,
        ),
    )(qkv, qkv, qkv, q_seg, k_seg, *shards)


def backward_pair(
    D, F,
    q_ref, k_ref, v_ref, do_ref, qs_ref, ks_ref, lse_ref, delta_ref, g_fc2, g_fc1, g_proj, *refs,
):
    dq_ref, dk_ref, dv_ref, t_fc2, t_fc1, t_proj = refs[:6]
    key_buf, kt_buf, dk_acc, dv_acc, dqt_buf = refs[6:11]
    bufs, (send, recv, own) = refs[11:-3], refs[-3:]
    pair = pl.program_id(0)
    rows = q_ref.shape[0]
    q_block = 256
    blocks = rows // q_block
    at = Place(D, F)

    @pl.when(pair == 0)
    def _():
        meet(at.partners())

    pieces = pieces_of((g_fc2, g_fc1, g_proj), (t_fc2, t_fc1, t_proj), BACKWARD_PARTS)
    arrays = scatter_arrays(at, pieces, bufs, send, recv, own)
    due = spread(arrays, (HEADS // 2) * blocks)
    keys, query, half = attend_pair(q_ref, k_ref, v_ref, qs_ref, ks_ref, q_block)
    key_buf[...] = keys
    kt_buf[...] = jnp.transpose(k_ref[...])
    for i in range(blocks):
        run_due(due, pair, i, blocks)
        block = pl.ds(i * q_block, q_block)
        for head in range(2):
            q_ext = query(block, head)
            d_out = half(do_ref[block, :], head)
            scores = nt(key_buf[...], q_ext)
            probs = jnp.exp(scores - lse_ref[0, head : head + 1, block])
            d_probs = nt(v_ref[...], d_out)
            d_scores = (probs * (d_probs - delta_ref[0, head : head + 1, block])).astype(BF)
            dv = nn(probs.astype(BF), d_out)
            dk = nn(d_scores, q_ext[:, :128])
            if i == 0 and head == 0:
                dv_acc[...] = dv
                dk_acc[...] = dk
            else:
                dv_acc[...] += dv
                dk_acc[...] += dk
            dq = nn(kt_buf[64 * head : 64 * head + 64, :], d_scores)
            dqt_buf[64 * head : 64 * head + 64, block] = (dq * 0.125).astype(BF)
    dq_ref[...] = jnp.transpose(dqt_buf[...])
    dk_ref[...] = dk_acc[...].astype(BF)
    dv_ref[...] = dv_acc[...].astype(BF)


def attend_backward(D, F, qkv, grad_attended, q_seg, k_seg, lse, delta, grads, collective_id):
    rows = qkv.shape[0]
    pairs = HEADS // 2
    pair, whole = pair_specs(rows)
    line = pl.BlockSpec((1, 8, rows), lambda p: (p, 0, 0))
    hbm = pl.BlockSpec(memory_space=pl.ANY)
    X, Y = F // 4, 2
    n = Scatter.count(D, X, Y)
    return pl.pallas_call(
        partial(backward_pair, D, F),
        name="attend_backward",
        grid=(pairs,),
        in_specs=[pair(0), pair(pairs), pair(2 * pairs), pair(0), whole, whole, line, line] + [hbm] * 3,
        out_specs=[pair(0)] * 3 + [pl.BlockSpec(g.shape[-2:], lambda p: (0, 0)) for g in grads],
        out_shape=[jax.ShapeDtypeStruct((rows, 128 * pairs), BF)] * 3
        + [jax.ShapeDtypeStruct(g.shape[-2:], F32) for g in grads],
        scratch_shapes=[
            pltpu.VMEM((rows, 256), BF),
            pltpu.VMEM((128, rows), BF),
            pltpu.VMEM((rows, 128), F32),
            pltpu.VMEM((rows, 128), F32),
            pltpu.VMEM((128, rows), BF),
        ]
        + scatter_scratch(D, X, Y, grads, BACKWARD_PARTS)
        + copy_semaphores(sum(BACKWARD_PARTS), n),
        compiler_params=pltpu.CompilerParams(
            collective_id=collective_id, has_side_effects=True, vmem_limit_bytes=VMEM_LIMIT
        ),
        cost_estimate=pl.CostEstimate(
            flops=10 * 12 * rows * rows * 256,
            bytes_accessed=14 * rows * 768,
            transcendentals=12 * rows * rows,
        ),
    )(qkv, qkv, qkv, grad_attended, q_seg, k_seg, lse, delta, *grads)


def gelu_both(u):
    z = jnp.abs(u)
    falling = jnp.exp(-0.5 * u * u)
    t = 1.0 / (1.0 + TAIL_P * z)
    poly = TAIL_C[-1]
    for coefficient in TAIL_C[-2::-1]:
        poly = poly * t + coefficient
    tail = poly * t * falling
    upper = jnp.where(u >= 0, 1.0 - tail, tail)
    return u * upper, upper + u * falling * 0.3989422804014327


def norm_parts(values):
    center = values - jnp.mean(values, axis=1, keepdims=True)
    spread = jnp.mean(center * center, axis=1, keepdims=True)
    rho = lax.rsqrt(spread + NORM_EPS)
    return center * rho, rho


def norm_back(n, rho, grad, gain):
    q = grad * gain
    return rho * (q - jnp.mean(q, axis=1, keepdims=True) - n * jnp.mean(q * n, axis=1, keepdims=True))


def fold(values):
    return jnp.sum(values.reshape(-1, 8, values.shape[1]), axis=0)


def middle_kernel(
    len_ref, emb, att, cot, wo, w1, b1, w2, vec, pick,
    layer_out, res_grad, att_grad, delta_out, g_proj, g_fc1, g_b1, g_fc2, g_small,
    residual, second, second_t, masked, mlp, g_second, act_buf, pre_buf, branch,
):
    step = pl.program_id(0)
    rows, width = emb.shape
    block_rows = 256
    blocks = rows // block_rows
    valid_rows = len_ref[0] + len_ref[1]
    ones = jnp.ones((8, block_rows), BF)

    def take(i):
        return pl.ds(pl.multiple_of(i * block_rows, block_rows), block_rows)

    @pl.when(step == 0)
    def _():
        def one(i, _):
            block = take(i)
            branch_out = nn(att[block, :], wo[...]) + vec[4:5, :]
            res = emb[block, :] + branch_out
            residual[block, :] = res
            n, _rho = norm_parts(res)
            sn = (n * vec[5:6, :] + vec[6:7, :]).astype(BF)
            second[block, :] = sn
            second_t[i] = jnp.transpose(sn)
            row = row_of(i * block_rows, block_rows, width)
            masked[block, :] = jnp.where(row < valid_rows, cot[block, :], jnp.zeros((), BF))
            mlp[block, :] = jnp.zeros((block_rows, width), F32)
            g_second[block, :] = jnp.zeros((block_rows, width), F32)
            return 0

        lax.fori_loop(0, blocks, one, 0)

    bias = b1[...]
    for i in range(blocks):
        block = pl.ds(i * block_rows, block_rows)
        pre = nn(second[block, :], w1[...]) + bias
        act, slope = gelu_both(pre)
        act = act.astype(BF)
        act_buf[block, :] = act
        grad_act = nt(masked[block, :], w2[...]).astype(BF).astype(F32)
        grad_pre = (grad_act * slope).astype(BF)
        pre_buf[block, :] = grad_pre
        mlp[block, :] += nn(act, w2[...])
        g_second[block, :] += nt(grad_pre, w1[...])
    g_fc2[...] = tn(act_buf[...], masked[...]).astype(BF)
    for i in range(blocks):
        block = pl.ds(i * block_rows, block_rows)
        part = nn(second_t[i], pre_buf[block, :])
        line = nn(ones, pre_buf[block, :])
        total = part if i == 0 else total + part
        lines = line if i == 0 else lines + line
    g_fc1[...] = total.astype(BF)
    g_b1[...] = lines

    @pl.when(step == pl.num_programs(0) - 1)
    def _():
        def one(i, sums):
            block = take(i)
            res = residual[block, :]
            n, rho = norm_parts(res)
            row = row_of(i * block_rows, block_rows, width)
            keep = row < valid_rows
            layer_out[block, :] = jnp.where(keep, res + mlp[block, :] + vec[7:8, :], 0.0).astype(BF)
            grad = g_second[block, :].astype(BF).astype(F32)
            back = norm_back(n, rho, grad, vec[5:6, :])
            out_grad = masked[block, :]
            total = out_grad.astype(F32) + back
            res_grad[block, :] = total
            low = total.astype(BF)
            branch[block, :] = low
            into = nt(low, wo[...]).astype(BF)
            att_grad[block, :] = into
            product = into.astype(F32) * att[block, :].astype(F32)
            high = product.astype(BF)
            rest = (product - high.astype(F32)).astype(BF)
            delta = nn(high, pick[...]) + nn(rest, pick[...])
            delta_out[:, block] = jnp.transpose(delta)[: delta_out.shape[0], :]
            return (
                sums[0] + nn(ones, low)[0:8],
                sums[1] + fold(grad * n),
                sums[2] + fold(grad),
                sums[3] + nn(ones, out_grad)[0:8],
            )

        empty = jnp.zeros((8, width), F32)
        sums = lax.fori_loop(0, blocks, one, (empty,) * 4)
        g_proj[...] = tn(att[...], branch[...]).astype(BF)
        g_small[0:1, :] = sums[0][0:1]
        g_small[1:2, :] = jnp.sum(sums[1], axis=0, keepdims=True)
        g_small[2:3, :] = jnp.sum(sums[2], axis=0, keepdims=True)
        g_small[3:4, :] = sums[3][0:1]
        g_small[4:8, :] = jnp.zeros((4, width), F32)


def middle(lengths, emb, att, cot, wo, w1, b1, w2, vec):
    rows, width = emb.shape
    hidden = w1.shape[1]
    tile = 512
    once = pl.Buffered(1)
    whole = lambda shape: pl.BlockSpec(shape, lambda j, s: (0,) * len(shape), pipeline_mode=once)
    pick = np.zeros((width, 128), np.float32)
    pick[np.arange(width), np.arange(width) // 64] = 1.0
    pick = jnp.asarray(pick.astype(ml_dtypes.bfloat16))
    out_shape = [
        jax.ShapeDtypeStruct((rows, width), BF),
        jax.ShapeDtypeStruct((rows, width), F32),
        jax.ShapeDtypeStruct((rows, width), BF),
        jax.ShapeDtypeStruct((16, rows), F32),
        jax.ShapeDtypeStruct((width, width), BF),
        jax.ShapeDtypeStruct((width, hidden), BF),
        jax.ShapeDtypeStruct((8, hidden), F32),
        jax.ShapeDtypeStruct((hidden, width), BF),
        jax.ShapeDtypeStruct((8, width), F32),
    ]
    return pl.pallas_call(
        middle_kernel,
        name="middle",
        grid_spec=pltpu.PrefetchScalarGridSpec(
            num_scalar_prefetch=1,
            grid=(hidden // tile,),
            in_specs=[
                whole((rows, width)),
                whole((rows, width)),
                whole((rows, width)),
                whole((width, width)),
                pl.BlockSpec((width, tile), lambda j, s: (0, j)),
                pl.BlockSpec((1, tile), lambda j, s: (0, j)),
                pl.BlockSpec((tile, width), lambda j, s: (j, 0)),
                whole((8, width)),
                whole((width, 128)),
            ],
            out_specs=[whole(s.shape) for s in out_shape[:5]]
            + [
                pl.BlockSpec((width, tile), lambda j, s: (0, j)),
                pl.BlockSpec((8, tile), lambda j, s: (0, j)),
                pl.BlockSpec((tile, width), lambda j, s: (j, 0)),
                whole((8, width)),
            ],
            scratch_shapes=[
                pltpu.VMEM((rows, width), F32),
                pltpu.VMEM((rows, width), BF),
                pltpu.VMEM((rows // 256, width, 256), BF),
                pltpu.VMEM((rows, width), BF),
                pltpu.VMEM((rows, width), F32),
                pltpu.VMEM((rows, width), F32),
                pltpu.VMEM((rows, tile), BF),
                pltpu.VMEM((rows, tile), BF),
                pltpu.VMEM((rows, width), BF),
            ],
        ),
        out_shape=out_shape,
        compiler_params=pltpu.CompilerParams(vmem_limit_bytes=VMEM_LIMIT),
        cost_estimate=pl.CostEstimate(
            flops=2 * rows * width * (6 * hidden + 3 * width),
            bytes_accessed=40 * 2**20,
            transcendentals=rows * hidden,
        ),
    )(lengths, emb, att, cot, wo, w1, b1, w2, vec, pick)


def first_kernel(
    len_ref, gq, gk, gv, first, emb, res_grad, patches, stats, sel, sel_low, w_ref, vec,
    g_qkv, g_pos, g_masked, g_small, acc, pos_acc, sums,
):
    step = pl.program_id(0)
    rows, width = emb.shape
    last = step == pl.num_programs(0) - 1
    ones = jnp.ones((8, rows), BF)

    @pl.when(step == 0)
    def _():
        acc[...] = jnp.zeros_like(acc)
        pos_acc[...] = jnp.zeros_like(pos_acc)
        sums[...] = jnp.zeros_like(sums)

    parts = [gq[...], gk[...], gv[...]]
    for i, part in enumerate(parts):
        columns = slice(i * width, (i + 1) * width)
        acc[:, columns] += tn(first[...], part)
        into = nt(part, w_ref[:, columns])
        grad = into if i == 0 else grad + into
    grad = grad.astype(BF).astype(F32)
    n, rho = norm_parts(emb[...])
    total = res_grad[...] + norm_back(n, rho, grad, vec[0:1, :])
    row = row_of(step * rows, rows, width)
    total = jnp.where(row < len_ref[0] + len_ref[1], total, 0.0)
    g_masked[...] = total
    low = total.astype(BF)
    pos_acc[...] += tn(low, sel[0])

    @pl.when(len_ref[1] > 0)
    def _():
        pos_acc[...] += tn(low, sel_low[0])

    normed = (patches[...].astype(F32) - stats[0:1, :]) * stats[1:2, :]
    sums[0] += fold(grad * n)
    sums[1] += fold(grad)
    sums[2] += nn(ones, parts[0])
    sums[3] += nn(ones, parts[2])
    sums[4] += fold(total)
    sums[5] += fold(total * normed)

    @pl.when(last)
    def _():
        g_qkv[...] = acc[...].astype(BF)
        g_pos[...] = pos_acc[...].astype(BF)
        for i in range(6):
            line = sums[i]
            g_small[i : i + 1, :] = line[0:1] if i in (2, 3) else jnp.sum(line, axis=0, keepdims=True)
        g_small[6:8, :] = jnp.zeros((2, width), F32)


def first_back(lengths, gq, gk, gv, first, emb, res_grad, patches, stats, table, w_qkv, vec):
    rows, width = emb.shape
    block = 256
    once = pl.Buffered(1)
    whole = lambda shape: pl.BlockSpec(shape, lambda i, s: (0,) * len(shape), pipeline_mode=once)
    by_row = lambda n: pl.BlockSpec((block, n), lambda i, s: (i, 0))
    out_shape = [
        jax.ShapeDtypeStruct((width, 3 * width), BF),
        jax.ShapeDtypeStruct((width, POS_PAD), BF),
        jax.ShapeDtypeStruct((rows, width), F32),
        jax.ShapeDtypeStruct((8, width), F32),
    ]
    return pl.pallas_call(
        first_kernel,
        name="first_back",
        grid_spec=pltpu.PrefetchScalarGridSpec(
            num_scalar_prefetch=1,
            grid=(rows // block,),
            in_specs=[by_row(width)] * 7
            + [
                whole(stats.shape),
                pl.BlockSpec((1, block, POS_PAD), lambda i, s: (jnp.where(s[1] > 0, 1, 0), i, 0)),
                pl.BlockSpec((1, block, POS_PAD), lambda i, s: (2, i, 0)),
                whole(w_qkv.shape),
                whole(vec.shape),
            ],
            out_specs=[
                whole(out_shape[0].shape),
                whole(out_shape[1].shape),
                by_row(width),
                whole(out_shape[3].shape),
            ],
            scratch_shapes=[
                pltpu.VMEM((width, 3 * width), F32),
                pltpu.VMEM((width, POS_PAD), F32),
                pltpu.VMEM((6, 8, width), F32),
            ],
        ),
        out_shape=out_shape,
        compiler_params=pltpu.CompilerParams(vmem_limit_bytes=VMEM_LIMIT),
        cost_estimate=pl.CostEstimate(
            flops=2 * rows * width * (6 * width + POS_PAD),
            bytes_accessed=30 * 2**20,
            transcendentals=0,
        ),
    )(lengths, gq, gk, gv, first, emb, res_grad, patches, stats, table, table, w_qkv, vec)


def clip_features(lengths, local_rows):
    position = jnp.arange(local_rows, dtype=jnp.int32)
    first_len, both = lengths[0], lengths[0] + lengths[1]
    segment = jnp.where(position < first_len, 0, jnp.where(position < both, 1, 2))
    lane = jnp.arange(128, dtype=jnp.int32)
    same = (segment[:, None] == lane[None, :]).astype(F32)
    other = jnp.where(lane[None, :] < 3, -1e30 * (1.0 - same), 0.0)
    return same.astype(BF), other.astype(BF)


def local(
    D, F,
    patches, cotangent, clip_len,
    pos_table, vector_params, w_qkv, w_proj, w_fc1, b_fc1, w_fc2,
    *states,
):
    params = (pos_table, vector_params, w_qkv, w_proj, w_fc1, b_fc1, w_fc2)
    momenta, averages = states[:7], states[7:]
    local_rows, width = patches.shape
    hidden = w_fc1.shape[1]
    group_size = D * F
    X, Y = F // 4, 2
    lengths = clip_len[0]
    table = selectors(local_rows)
    q_seg, k_seg = clip_features(lengths, local_rows)
    valid = jnp.broadcast_to(
        (jnp.arange(local_rows) < lengths[0] + lengths[1]).astype(F32)[:, None], (local_rows, 128)
    )
    n_vec, n_bias = vector_params.size, b_fc1.size
    small = jnp.concatenate([vector_params.reshape(-1), b_fc1])
    small = jnp.pad(small, (0, 2048 - small.size)).astype(BF).reshape(16, 128)
    shards = (
        small,
        jnp.pad(pos_table, ((0, 0), (0, POS_PAD - LONG))).astype(BF),
        w_qkv.astype(BF),
    )
    later = (w_proj.astype(BF), w_fc1.astype(BF), w_fc2.astype(BF))
    sums, small_full, pos_full, qkv_full = gather_all(D, F, patches, valid, shards, (1, 2, 3), 0)
    small_full = small_full.reshape(group_size, 2048).astype(F32)
    vec = small_full[:, :n_vec].reshape(width, 8).T
    bias_full = small_full[:, n_vec : n_vec + n_bias].reshape(1, hidden)
    pos_full, qkv_full = (w.reshape(-1, w.shape[-1]) for w in (pos_full, qkv_full))
    valid_count = sums[2, 0]
    feature_mean = sums[0] / valid_count
    feature_var = sums[1] / valid_count - feature_mean * feature_mean
    inv_std = lax.rsqrt(feature_var + INPUT_EPS)
    stats = jnp.stack([feature_mean, inv_std] + [jnp.zeros_like(inv_std)] * 6)
    qkv_bias = jnp.concatenate([vec[2], jnp.zeros_like(vec[2]), vec[3]])[None, :]
    emb, first, qkv = embed(lengths, patches, stats, table, pos_full, vec, qkv_bias, qkv_full)
    attended, lse, *full = attend_forward(D, F, qkv, q_seg, k_seg, later, 1)
    proj_full, fc1_full, fc2_full = (w.reshape(-1, w.shape[-1]) for w in full)
    layer_out, res_grad, att_grad, delta, g_proj, g_fc1, g_b1, g_fc2, g_small_mid = middle(
        lengths, emb, attended, cotangent, proj_full, fc1_full, bias_full, fc2_full, vec
    )
    delta = jnp.pad(delta[:HEADS].reshape(HEADS // 2, 2, local_rows), ((0, 0), (0, 6), (0, 0)))
    spans = lambda g: g.reshape(D, Y, X, 2, -1, g.shape[-1])
    gq, gk, gv, t_fc2, t_fc1, t_proj = attend_backward(
        D, F, qkv, att_grad, q_seg, k_seg, lse, delta, [spans(g) for g in (g_fc2, g_fc1, g_proj)], 2
    )
    g_qkv, g_pos, g_masked, g_small_first = first_back(
        lengths, gq, gk, gv, first, emb, res_grad, patches, stats, table, qkv_full, vec
    )
    small_grads = jnp.concatenate(
        [
            g_small_first[:4],
            g_small_mid[:4],
            g_small_first[4:6],
            g_b1[0].reshape(-1, width),
            jnp.zeros((16 - 10 - hidden // width, width), F32),
        ]
    )
    small_sum, t_qkv, t_pos = scatter_all(D, F, small_grads, [spans(g_qkv), spans(g_pos)], (3, 2), 3)
    normed = (patches.astype(F32) - feature_mean) * inv_std
    valid_col = valid[:, :1]
    patch_grad = (
        inv_std
        * (
            g_masked
            - valid_col * (small_sum[8] / valid_count)
            - valid_col * normed * (small_sum[9] / valid_count)
        )
    ).astype(BF)
    me = lax.axis_index("dp") * F + lax.axis_index("fsdp")
    n_rows = vector_params.shape[0]
    g_vec = lax.dynamic_slice(small_sum[:8], (0, me * n_rows), (8, n_rows)).T
    g_bias = lax.dynamic_slice(small_sum[10 : 10 + hidden // width].reshape(-1), (me * n_bias,), (n_bias,))
    grad_shards = (t_pos[:, :LONG], g_vec, t_qkv, t_proj, t_fc1, g_bias, t_fc2)
    rate = 0.02 * (local_rows * group_size) ** (-0.5)
    average_keep = min(0.99, (1.0 + PRIOR_STEPS) / (10.0 + PRIOR_STEPS))
    next_moms = tuple(MOMENTUM * m + g for m, g in zip(momenta, grad_shards))
    updates = tuple(-(rate * (g + MOMENTUM * m)) for g, m in zip(grad_shards, next_moms))
    next_averages = tuple(
        average_keep * a + (1.0 - average_keep) * (w + u)
        for a, w, u in zip(averages, params, updates)
    )
    feature_stats = jnp.stack([feature_mean, feature_var])
    return (
        (layer_out, patch_grad, feature_stats) + grad_shards + updates + next_moms + next_averages
    )


def solution(mesh):
    rows, line = P(AXES, None), P(AXES)
    params = (rows, rows, rows, rows, rows, line, rows)
    return jax.shard_map(
        partial(local, mesh.shape["dp"], mesh.shape["fsdp"]),
        mesh=mesh,
        in_specs=(rows,) * 3 + params * 3,
        out_specs=(rows, rows, P()) + params * 4,
        check_vma=False,
    )
```

```python
from functools import partial

import jax
import jax.numpy as jnp
import ml_dtypes
import numpy as np
from jax import lax
from jax.experimental import pallas as pl
from jax.experimental.pallas import tpu as pltpu
from jax.sharding import PartitionSpec as P

HEADS = 12
FREQ_L = 12
TIME_L = 101
FREQ_S = 8
TIME_S = 64
PRIOR_STEPS = 3
LONG = 1214
SHORT = 514

NORM_EPS = 1e-06
INPUT_EPS = 1e-05
MOMENTUM = 0.9
MESH = pl.DeviceIdType.MESH
AXES = ("dp", "fsdp")
BF = jnp.bfloat16
F32 = jnp.float32
VMEM_LIMIT = 60 * 2**20
POS_PAD = 1280
HEAD_PARTS = (2, 3)
FORWARD_PARTS = (1, 4, 3)
BACKWARD_PARTS = (2, 1, 1)
BACKWARD_LAGS = (0, 2, 4, 6, 8)
EARLY_PAIRS = 4
MIDDLE_LAGS = (0, 2, 4, 6, 8)
EARLY_TILES = 3


TAIL_P = 0.305
TAIL_C = (
    0.121639732,
    0.122466826,
    0.10342081,
    0.121021868,
    -0.037977191,
    0.185717298,
    -0.152988541,
    0.036699245,
)


def resize_rows(size_in, size_out):
    resize_table = np.zeros((size_out, size_in), np.float64)
    for target_row in range(size_out):
        source_pos = max((target_row + 0.5) * size_in / size_out - 0.5, 0.0)
        lower_cell = min(int(np.floor(source_pos)), size_in - 1)
        upper_cell = min(lower_cell + 1, size_in - 1)
        fraction = source_pos - lower_cell
        resize_table[target_row, lower_cell] += 1.0 - fraction
        resize_table[target_row, upper_cell] += fraction
    return resize_table


def selectors(local_rows):
    table = np.zeros((2, local_rows, POS_PAD), np.float64)
    table[0, :LONG, :LONG] = np.eye(LONG)
    short = np.zeros((SHORT, LONG), np.float64)
    short[0, 0] = short[1, 1] = 1.0
    short[2:, 2:] = np.kron(resize_rows(FREQ_L, FREQ_S), resize_rows(TIME_L, TIME_S))
    for first in (0, SHORT):
        table[1, first : first + SHORT, :LONG] = short
    return jnp.asarray(table.astype(ml_dtypes.bfloat16))


def nn(left, right):
    return lax.dot_general(left, right, (((1,), (0,)), ((), ())), preferred_element_type=F32)


def nt(left, right):
    return lax.dot_general(left, right, (((1,), (1,)), ((), ())), preferred_element_type=F32)


def tn(left, right):
    return lax.dot_general(left, right, (((0,), (0,)), ((), ())), preferred_element_type=F32)


class Place:
    def __init__(self, dp_size, fsdp_size):
        self.D, self.F = dp_size, fsdp_size
        self.X, self.Y = fsdp_size // 4, 2
        self.d = lax.axis_index("dp")
        self.f = lax.axis_index("fsdp")
        self.c = lax.rem(self.f, 2)
        self.x = lax.rem(lax.div(self.f, 2), self.X)
        self.y = lax.div(self.f, 2 * self.X)

    def fs(self, y, x, c):
        return (y * self.X + x) * 2 + c

    def up(self, value, step, size):
        return lax.rem(value + step, size)

    def partners(self):
        out = [(self.up(self.d, k, self.D), self.f) for k in range(1, self.D)]
        out += [(self.d, self.fs(self.y, self.up(self.x, k, self.X), self.c)) for k in range(1, self.X)]
        out += [(self.d, self.fs(self.up(self.y, k, self.Y), self.x, self.c)) for k in range(1, self.Y)]
        out.append((self.d, self.fs(self.y, self.x, 1 - self.c)))
        return out

    def everyone(self):
        out = [(self.up(self.d, k, self.D), self.f) for k in range(1, self.D)]
        return out + [(self.d, self.up(self.f, k, self.F)) for k in range(1, self.F)]


def meet(devices):
    barrier = pltpu.get_barrier_semaphore()
    for device in devices:
        pl.semaphore_signal(barrier, inc=1, device_id=device, device_id_type=MESH)
    pl.semaphore_wait(barrier, len(devices))


class Gather:
    @staticmethod
    def count(D, X, Y):
        return (D - 1) + 2 * (X - 1) + 2 * (Y - 1) + 1

    def __init__(self, at, src, out, send, recv, own):
        self.at, self.src, self.out, self.send, self.recv, self.own = at, src, out, send, recv, own
        D, X, Y = at.D, at.X, at.Y
        self.n_z = 0
        self.n_x = D - 1
        self.n_y = self.n_x + X - 1
        self.n_c = self.n_y + Y - 1

    def copy(self, src, dst, number, device):
        return pltpu.make_async_remote_copy(
            src_ref=src,
            dst_ref=dst,
            send_sem=self.send.at[number],
            recv_sem=self.recv.at[number],
            device_id=device,
            device_id_type=MESH,
        )

    def z_copy(self, k):
        at = self.at
        return self.copy(
            self.src,
            self.out.at[at.d, at.y, at.x, at.c],
            self.n_z + k - 1,
            (at.up(at.d, k, at.D), at.f),
        )

    def z_got(self, k):
        at = self.at
        here = self.out.at[at.up(at.d, at.D - k, at.D), at.y, at.x, at.c]
        return self.copy(here, here, self.n_z + k - 1, (at.up(at.d, at.D - k, at.D), at.f))

    def part(self, axis, order, y, x, c):
        if axis == order[0]:
            return self.out.at[:, y, x, c]
        return self.out.at[:, y, :, c] if axis == "y" else self.out.at[:, :, x, c]

    def side(self, axis, order, k, sent):
        at = self.at
        size = at.X if axis == "x" else at.Y
        first = self.n_x if axis == "x" else self.n_y
        mine = at.x if axis == "x" else at.y
        other = at.up(mine, k if sent else size - k, size)
        y, x = (at.y, other) if axis == "x" else (other, at.x)
        block = self.part(axis, order, at.y, at.x, at.c) if sent else self.part(axis, order, y, x, at.c)
        return self.copy(block, block, first + k - 1, (at.d, at.fs(y, x, at.c)))

    def pieces(self, order, c):
        at = self.at
        out = [self.out.at[:, at.y, at.x, c]]
        for axis in order:
            size = at.X if axis == "x" else at.Y
            for k in range(1, size):
                other = at.up(at.x if axis == "x" else at.y, size - k, size)
                y, x = (at.y, other) if axis == "x" else (other, at.x)
                out.append(self.part(axis, order, y, x, c))
        return out

    def sibling(self, block, number):
        at = self.at
        return self.copy(block, block, self.n_c + number, (at.d, at.fs(at.y, at.x, 1 - at.c)))

    def local(self):
        at = self.at
        return pltpu.make_async_copy(self.src, self.out.at[at.d, at.y, at.x, at.c], self.own)

    def size_of(self, axis):
        return self.at.X if axis == "x" else self.at.Y

    def phase(self, number):
        at = self.at
        if number == 0:
            self.local().start()
            for k in range(1, at.D):
                self.z_copy(k).start()
            return
        if number == 1:
            self.local().wait()
            for k in range(1, at.D):
                self.z_got(k).wait_recv()
        for core, order in ((0, ("x", "y")), (1, ("y", "x"))):

            @pl.when(at.c == core)
            def _(core=core, order=order):
                mine = self.pieces(order, core)
                first = 1 + (self.size_of(order[0]) - 1)
                if number == 1:
                    for k in range(1, self.size_of(order[0])):
                        self.side(order[0], order, k, True).start()
                    self.sibling(mine[0], 0).start()
                elif number == 2:
                    for k in range(1, self.size_of(order[0])):
                        self.side(order[0], order, k, False).wait_recv()
                    for k in range(1, self.size_of(order[1])):
                        self.side(order[1], order, k, True).start()
                    for i in range(1, first):
                        self.sibling(mine[i], i).start()
                elif number == 3:
                    for k in range(1, self.size_of(order[1])):
                        self.side(order[1], order, k, False).wait_recv()
                    for i in range(first, len(mine)):
                        self.sibling(mine[i], i).start()
                elif number == 4:
                    for k in range(1, at.D):
                        self.z_copy(k).wait_send()
                    for axis in order:
                        for k in range(1, self.size_of(axis)):
                            self.side(axis, order, k, True).wait_send()
                    for i, block in enumerate(mine):
                        self.sibling(block, i).wait_send()
                    for i, block in enumerate(self.pieces(order[::-1], 1 - core)):
                        self.sibling(block, i).wait_recv()


class Scatter:
    @staticmethod
    def count(D, X, Y):
        return 1 + (Y - 1) + (X - 1) + (D - 1)

    @staticmethod
    def scratch(D, X, Y, R, N, held=False):
        out = [] if held else [pltpu.VMEM((D, Y, X, R, N), BF)]
        out.append(pltpu.VMEM((D, Y, X, R, N), BF))
        out += [pltpu.VMEM((Y - 1, D, X, R, N), BF), pltpu.VMEM((Y - 1, D, R, N), BF)]
        if X != Y:
            out += [pltpu.VMEM((X - 1, D, Y, R, N), BF), pltpu.VMEM((X - 1, D, R, N), BF)]
        return out + [pltpu.VMEM((D - 1, R, N), BF)]

    def __init__(self, at, grad, total, bufs, send, recv, own):
        self.at, self.grad, self.total = at, grad, total
        self.held = len(bufs) % 2 == 0
        bufs = list(bufs)
        self.acc = None if self.held else bufs.pop(0)
        self.r1, self.r2y, self.r3y = bufs[:3]
        self.r2x, self.r3x = (self.r2y, self.r3y) if at.X == at.Y else bufs[3:5]
        self.r4 = bufs[-1]
        self.send, self.recv, self.own = send, recv, own
        self.n_y = 1
        self.n_x = self.n_y + at.Y - 1
        self.n_z = self.n_x + at.X - 1

    def view(self, d, y, x):
        return self.grad.at[d, y, x, self.at.c] if self.held else self.acc.at[d, y, x]

    def get(self, d, y, x):
        return self.grad[d, y, x, self.at.c] if self.held else self.acc[d, y, x]

    def put(self, d, y, x, value):
        if self.held:
            self.grad[d, y, x, self.at.c] = value
        else:
            self.acc[d, y, x] = value

    def fill(self, values):
        at = self.at
        R = self.grad.shape[-2]

        def one(i, _):
            rest, c = lax.div(i, 2), lax.rem(i, 2)
            rest, x = lax.div(rest, at.X), lax.rem(rest, at.X)
            d, y = lax.div(rest, at.Y), lax.rem(rest, at.Y)
            first = i * R
            if R % 8 == 0:
                block = values[pl.ds(pl.multiple_of(first, 8), R), :].astype(BF)
            else:
                shape = (16, values.shape[0])
                row = lax.broadcasted_iota(jnp.int32, shape, 0)
                pick = jnp.where(lax.broadcasted_iota(jnp.int32, shape, 1) == row + first, 1.0, 0.0)
                block = nn(pick.astype(BF), values[...].astype(BF))[:R].astype(BF)
            self.grad[d, y, x, c] = block
            return 0

        lax.fori_loop(0, at.D * at.F, one, 0)

    def copy(self, src, dst, number, device):
        return pltpu.make_async_remote_copy(
            src_ref=src,
            dst_ref=dst,
            send_sem=self.send.at[number],
            recv_sem=self.recv.at[number],
            device_id=device,
            device_id_type=MESH,
        )

    def core_copy(self):
        at = self.at
        return self.copy(
            self.grad.at[:, :, :, 1 - at.c], self.r1, 0, (at.d, at.fs(at.y, at.x, 1 - at.c))
        )

    def local(self):
        return pltpu.make_async_copy(self.grad.at[:, :, :, self.at.c], self.acc, self.own)

    def side(self, axis, order, k):
        at, all_d = self.at, slice(None)
        if axis == "y":
            y = at.up(at.y, k, at.Y)
            device = (at.d, at.fs(y, at.x, at.c))
            if axis == order[0]:
                src, dst = self.view(all_d, y, slice(None)), self.r2y
            else:
                src, dst = self.view(all_d, y, at.x), self.r3y
            return self.copy(src, dst.at[k - 1], self.n_y + k - 1, device)
        x = at.up(at.x, k, at.X)
        device = (at.d, at.fs(at.y, x, at.c))
        if axis == order[0]:
            src, dst = self.view(all_d, slice(None), x), self.r2x
        else:
            src, dst = self.view(all_d, at.y, x), self.r3x
        return self.copy(src, dst.at[k - 1], self.n_x + k - 1, device)

    def z_copy(self, k):
        at = self.at
        d = at.up(at.d, k, at.D)
        return self.copy(self.view(d, at.y, at.x), self.r4.at[k - 1], self.n_z + k - 1, (d, at.f))

    def size_of(self, axis):
        return self.at.X if axis == "x" else self.at.Y

    def store(self, total):
        self.total[...] = total

    def phase(self, number):
        at = self.at
        if number == 0:
            if not self.held:
                self.local().start()
            self.core_copy().start()
            return
        if number == 1:
            if not self.held:
                self.local().wait()
            self.core_copy().wait_recv()

            def add(i, _):
                d, rest = lax.div(i, at.Y * at.X), lax.rem(i, at.Y * at.X)
                y, x = lax.div(rest, at.X), lax.rem(rest, at.X)
                self.put(d, y, x, self.get(d, y, x) + self.r1[d, y, x])
                return 0

            lax.fori_loop(0, at.D * at.Y * at.X, add, 0)
        if number == 4:
            for k in range(1, at.D):
                self.z_copy(k).wait_recv()
            total = self.get(at.d, at.y, at.x).astype(F32)
            for k in range(1, at.D):
                total = total + self.r4[k - 1].astype(F32)
            self.store(total)
            self.core_copy().wait_send()
            for k in range(1, at.D):
                self.z_copy(k).wait_send()
        for core, order in ((0, ("y", "x")), (1, ("x", "y"))):

            @pl.when(at.c == core)
            def _(core=core, order=order):
                n0, n1 = self.size_of(order[0]), self.size_of(order[1])
                if number == 1:
                    for k in range(1, n0):
                        self.side(order[0], order, k).start()
                elif number == 2:
                    for k in range(1, n0):
                        self.side(order[0], order, k).wait_recv()

                    def add(i, _):
                        d, j = lax.div(i, n1), lax.rem(i, n1)
                        y, x = (at.y, j) if order[0] == "y" else (j, at.x)
                        got = self.r2y if order[0] == "y" else self.r2x
                        value = self.get(d, y, x)
                        for k in range(1, n0):
                            value = value + got[k - 1, d, j]
                        self.put(d, y, x, value)
                        return 0

                    lax.fori_loop(0, at.D * n1, add, 0)
                    for k in range(1, n1):
                        self.side(order[1], order, k).start()
                elif number == 3:
                    for k in range(1, n1):
                        self.side(order[1], order, k).wait_recv()

                    def add(d, _):
                        got = self.r3y if order[1] == "y" else self.r3x
                        value = self.get(d, at.y, at.x)
                        for k in range(1, n1):
                            value = value + got[k - 1, d]
                        self.put(d, at.y, at.x, value)
                        return 0

                    lax.fori_loop(0, at.D, add, 0)
                elif number == 4:
                    for axis in order:
                        for k in range(1, self.size_of(axis)):
                            self.side(axis, order, k).wait_send()

        if number == 3:
            for k in range(1, at.D):
                self.z_copy(k).start()


class Total:
    @staticmethod
    def count(D, F):
        return (D - 1) + (F - 1)

    @staticmethod
    def scratch(D, F, rows, cols):
        return [pltpu.VMEM((D, rows, cols), F32), pltpu.VMEM((F, rows, cols), F32)]

    def __init__(self, at, bufs, send, recv):
        self.at, self.send, self.recv = at, send, recv
        self.z_buf, self.f_buf = bufs

    def copy(self, buf, slot, number, device):
        return pltpu.make_async_remote_copy(
            src_ref=buf.at[slot],
            dst_ref=buf.at[slot],
            send_sem=self.send.at[number],
            recv_sem=self.recv.at[number],
            device_id=device,
            device_id_type=MESH,
        )

    def z_copy(self, k, sent):
        at = self.at
        other = at.up(at.d, k if sent else at.D - k, at.D)
        return self.copy(self.z_buf, at.d if sent else other, k - 1, (other, at.f))

    def f_copy(self, k, sent):
        at = self.at
        other = at.up(at.f, k if sent else at.F - k, at.F)
        return self.copy(self.f_buf, at.f if sent else other, at.D - 1 + k - 1, (at.d, other))

    def start(self, value):
        at = self.at
        self.z_buf[at.d] = value
        for k in range(1, at.D):
            self.z_copy(k, True).start()

    def middle(self):
        at = self.at
        for k in range(1, at.D):
            self.z_copy(k, False).wait_recv()
        total = self.z_buf[0]
        for i in range(1, at.D):
            total = total + self.z_buf[i]
        self.f_buf[at.f] = total
        for k in range(1, at.F):
            self.f_copy(k, True).start()

    def end(self):
        at = self.at
        for k in range(1, at.F):
            self.f_copy(k, False).wait_recv()
        total = self.f_buf[0]
        for i in range(1, at.F):
            total = total + self.f_buf[i]
        for k in range(1, at.D):
            self.z_copy(k, True).wait_send()
        for k in range(1, at.F):
            self.f_copy(k, True).wait_send()
        return total


LAGS = (0, 2, 4, 6, 8)


def steps_of(arrays, lags=(0, 1, 3, 5, 6)):
    for step in range(len(arrays) + lags[-1]):
        yield [
            (arrays[i], lags.index(step - i))
            for i in reversed(range(len(arrays)))
            if step - i in lags
        ]


def spread(arrays, slots):
    steps = list(steps_of(arrays, LAGS))
    due = {slot: [] for slot in range(slots)}
    for i, step in enumerate(steps):
        due[(i * (slots - 1)) // (len(steps) - 1)] += step
    return due


def columns(ref, part, parts):
    size = ref.shape[-1] // parts
    return ref.at[(slice(None),) * (len(ref.shape) - 1) + (pl.ds(part * size, size),)]


def placed(values, first, width):
    count = values.shape[1]
    row = lax.broadcasted_iota(jnp.int32, (count, width), 0)
    column = lax.broadcasted_iota(jnp.int32, (count, width), 1)
    return nn(values, jnp.where(column == row + first, 1.0, 0.0).astype(BF))


def head_kernel(
    D, F,
    lens, patches, pos_in, vec_in, qkv_in, bias_in, proj_in, fc1_in, fc2_in,
    stats, vec, bias, qs, ks, proj_b, fc1_b, fc2_b, pos_out, qkv_out,
    pos_b, qkv_b, z_buf, f_buf, s_send, s_recv, send, recv, own,
):
    at = Place(D, F)
    rows, width = patches.shape
    pos_b[...] = jnp.zeros_like(pos_b)
    pos_b[:, :LONG] = pos_in[...].astype(BF)
    qkv_b[...] = qkv_in[...].astype(BF)
    meet(at.everyone())
    pieces = pieces_of((pos_b, qkv_b), (pos_out, qkv_out), HEAD_PARTS)
    arrays = [
        Gather(at, src, out, send.at[i], recv.at[i], own.at[i]) for i, (src, out) in enumerate(pieces)
    ]
    steps = list(steps_of(arrays))
    arrays[0].phase(0)
    arrays[1].phase(0)
    step_rows = 64
    valid_rows = lens[0, 0] + lens[0, 1]

    def accumulate(i, sums):
        block = pl.ds(pl.multiple_of(i * step_rows, step_rows), step_rows)
        row = i * step_rows + lax.broadcasted_iota(jnp.int32, (step_rows, width), 0)
        values = jnp.where(row < valid_rows, patches[block, :].astype(F32), 0.0)
        first = values.reshape(step_rows // 8, 8, -1)
        return (sums[0] + jnp.sum(first, axis=0), sums[1] + jnp.sum(first * first, axis=0))

    empty = jnp.zeros((8, width), F32)
    plain, square = lax.fori_loop(0, rows // step_rows, accumulate, (empty, empty))
    row = lax.broadcasted_iota(jnp.int32, empty.shape, 0)
    plain = jnp.sum(plain, axis=0, keepdims=True)
    square = jnp.sum(square, axis=0, keepdims=True)
    me = at.d * F + at.f
    count = jnp.zeros((1, width), F32) + valid_rows.astype(F32)
    packed = jnp.where(row == 0, plain, jnp.where(row == 1, square, jnp.where(row == 2, count, 0.0)))
    n_bias = bias_in.shape[1]
    hidden = n_bias * D * F
    own_bias = jnp.broadcast_to(bias_in[...].astype(BF), (8, n_bias))
    for i in range(hidden // width):
        packed = jnp.where(row == 4 + i, placed(own_bias, me * n_bias - i * width, width), packed)
    own_vec = placed(vec_in[...].astype(BF), me * vec_in.shape[1], width)
    total = Total(at, (z_buf, f_buf), s_send, s_recv)
    total.start(jnp.concatenate([packed, own_vec], axis=0))
    for number, step in enumerate(steps):
        for array, phase in step:
            if phase > 0 or array not in arrays[:2]:
                array.phase(phase)
        if number == 1:
            proj_b[...] = proj_in[...].astype(BF)
            fc1_b[...] = fc1_in[...].astype(BF)
            fc2_b[...] = fc2_in[...].astype(BF)
            position = lax.broadcasted_iota(jnp.int32, qs.shape, 0)
            lane = lax.broadcasted_iota(jnp.int32, qs.shape, 1)
            segment = jnp.where(position < lens[0, 0], 0, jnp.where(position < valid_rows, 1, 2))
            same = segment == lane
            qs[...] = jnp.where(same, 1.0, 0.0).astype(BF)
            ks[...] = jnp.where(same, 0.0, jnp.where(lane < 3, -1e30, 0.0)).astype(BF)
        if number == 3:
            total.middle()
        if number == 6:
            summed = total.end()
            inv_count = 1.0 / summed[2:3]
            mean = summed[0:1] * inv_count
            mean = summed[0:1] / summed[2:3]
            var = summed[1:2] / summed[2:3] - mean * mean
            stats[0:1, :] = mean
            stats[1:2, :] = lax.rsqrt(var + INPUT_EPS)
            stats[2:3, :] = inv_count
            stats[3:4, :] = count
            stats[4:5, :] = var
            stats[5:8, :] = jnp.zeros((3, width), F32)
            vec[...] = summed[8:16]
            for i in range(hidden // width):
                bias[0:1, i * width : (i + 1) * width] = summed[4 + i : 5 + i]


def head(D, F, clip_len, patches, pos, vec, w_qkv, bias, w_proj, w_fc1, w_fc2, collective_id):
    X, Y = F // 4, 2
    rows, width = patches.shape
    hidden = bias.shape[0] * D * F
    count = sum(HEAD_PARTS)
    n = Gather.count(D, X, Y)
    hbm = pl.BlockSpec(memory_space=pl.ANY)
    vmem = pl.BlockSpec(memory_space=pltpu.VMEM)
    own_rows = pos.shape[0]
    sent = [(own_rows, POS_PAD), w_qkv.shape]
    return pl.pallas_call(
        partial(head_kernel, D, F),
        name="head",
        out_shape=[
            jax.ShapeDtypeStruct((8, width), F32),
            jax.ShapeDtypeStruct((8, width), F32),
            jax.ShapeDtypeStruct((1, hidden), F32),
            jax.ShapeDtypeStruct((rows, 128), BF),
            jax.ShapeDtypeStruct((rows, 128), BF),
        ]
        + [jax.ShapeDtypeStruct(w.shape, BF) for w in (w_proj, w_fc1, w_fc2)]
        + [jax.ShapeDtypeStruct((D, Y, X, 2) + shape, BF) for shape in sent],
        in_specs=[pl.BlockSpec(memory_space=pltpu.SMEM)] + [vmem] * 8,
        out_specs=[vmem] * 8 + [hbm] * 2,
        scratch_shapes=[pltpu.VMEM(shape, BF) for shape in sent]
        + Total.scratch(D, F, 16, width)
        + [pltpu.SemaphoreType.DMA((Total.count(D, F),)), pltpu.SemaphoreType.DMA((Total.count(D, F),))]
        + copy_semaphores(count, n),
        compiler_params=pltpu.CompilerParams(
            collective_id=collective_id, has_side_effects=True, vmem_limit_bytes=VMEM_LIMIT
        ),
        cost_estimate=pl.CostEstimate(flops=0, bytes_accessed=20 * 2**20, transcendentals=0),
    )(clip_len, patches, pos, vec.T, w_qkv, bias.reshape(1, -1), w_proj, w_fc1, w_fc2)


def pieces_of(grads, totals, parts):
    return [
        (columns(g, j, n), columns(t, j, n)) for g, t, n in zip(grads, totals, parts) for j in range(n)
    ]


def scatter_arrays(at, pieces, bufs, send, recv, own):
    per = len(bufs) // len(pieces)
    return [
        Scatter(at, grad, total, bufs[i * per : (i + 1) * per], send.at[i], recv.at[i], own.at[i])
        for i, (grad, total) in enumerate(pieces)
    ]


def blocks_shape(D, X, Y, rows, N):
    return (D, Y, X, 2, rows // (D * X * Y * 2), N)


def scatter_scratch(D, X, Y, grads, parts):
    out = []
    for g, n in zip(grads, parts):
        for _ in range(n):
            out += Scatter.scratch(D, X, Y, g.shape[-2], g.shape[-1] // n)
    return out


def copy_semaphores(count, n):
    return [
        pltpu.SemaphoreType.DMA((count, n)),
        pltpu.SemaphoreType.DMA((count, n)),
        pltpu.SemaphoreType.DMA((count,)),
    ]


def row_of(first, rows, width):
    return first + lax.broadcasted_iota(jnp.int32, (rows, width), 0)


def attend_pair(q_ref, k_ref, v_ref, qs_ref, ks_ref, q_block):
    rows = q_ref.shape[0]
    lane = lax.broadcasted_iota(jnp.int32, (q_block, 128), 1)

    def half(values, head):
        keep = lane < 64 if head == 0 else lane >= 64
        return jnp.where(keep, values, jnp.zeros_like(values))

    def query(block, head):
        scaled = q_ref[block, :] * jnp.asarray(0.125, BF)
        return jnp.concatenate([half(scaled, head), qs_ref[block, :]], axis=1)

    keys = jnp.concatenate([k_ref[...], ks_ref[...]], axis=1)
    return keys, query, half


def forward_kernel(
    D, F,
    lens, patches, stats, sel_long, sel_short, pos, vec, w_ref, qs_ref, ks_ref, proj_ref, fc1_ref, fc2_ref,
    emb_out, norm_out, qkv_out, out_ref, lse_ref, proj_out, fc1_out, fc2_out,
    qkv_buf, q_ref, k_ref, key_buf, v_buf, o_buf, send, recv, own,
):
    step = pl.program_id(0)
    part_rows, width = patches.shape
    rows = qkv_buf.shape[0]
    parts = rows // part_rows
    pairs = HEADS // 2
    q_block = 256
    blocks = rows // q_block
    at = Place(D, F)

    @pl.when(step == 0)
    def _():
        meet(at.partners())

    pieces = pieces_of((proj_ref, fc1_ref, fc2_ref), (proj_out, fc1_out, fc2_out), FORWARD_PARTS)
    arrays = [
        Gather(at, src, out, send.at[i], recv.at[i], own.at[i]) for i, (src, out) in enumerate(pieces)
    ]
    due = spread(arrays, parts + 2 * pairs + 1)

    @pl.when(step < parts)
    def _():
        run_due({k: due[k] for k in range(parts)}, step, parts, 0, 1)
        mean, inv_std = stats[0:1, :], stats[1:2, :]
        normed = (patches[...].astype(F32) - mean) * inv_std
        row = lax.broadcasted_iota(jnp.int32, (part_rows, width), 0).astype(F32)
        first_row = (step * part_rows).astype(F32)
        sel = jnp.where(lens[0, 1] > 0, sel_short[0], sel_long[0])
        embedded = jnp.where(row + first_row < stats[3:4, :], normed + nt(sel, pos[...]), 0.0)
        emb_out[...] = embedded
        n, _rho = norm_parts(embedded)
        first = (n * vec[0:1, :] + vec[1:2, :]).astype(BF)
        norm_out[...] = jnp.transpose(first)
        bias = jnp.concatenate([vec[2:3, :], jnp.zeros((1, width), F32), vec[3:4, :]], axis=1)
        projected = (nn(first, w_ref[...]) + bias).astype(BF)
        qkv_out[...] = projected
        qkv_buf[pl.ds(pl.multiple_of(step * part_rows, part_rows), part_rows), :] = projected

    @pl.when(step >= parts)
    def _():
        pair = step - parts
        slots = {k: due[k + parts] for k in range(2 * pairs + 1)}

        def columns_of(i):
            return qkv_buf[:, pl.ds(pl.multiple_of(i * width + pair * 128, 128), 128)]

        q_ref[...] = columns_of(0)
        k_ref[...] = columns_of(1)
        keys, query, _ = attend_pair(q_ref, k_ref, None, qs_ref, ks_ref, q_block)
        key_buf[...] = keys
        v_t = jnp.transpose(columns_of(2))
        ones = jnp.ones((16, rows), BF)
        for head in range(2):
            v_buf[head] = jnp.concatenate([v_t[64 * head : 64 * head + 64], ones], axis=0)
        for i in range(blocks):
            if i in (0, 3):
                run_due(slots, pair, pairs, i // 3, 2)
            block = pl.ds(i * q_block, q_block)
            for head in range(2):
                scores = nt(key_buf[...], query(block, head))
                top = jnp.max(scores, axis=0, keepdims=True)
                probs = jnp.exp(scores - top).astype(BF)
                out = nn(v_buf[head], probs)
                total = out[64:65, :]
                o_buf[64 * head : 64 * head + 64, block] = (out[:64] / total).astype(BF)
                lse_ref[0, head : head + 1, block] = top + jnp.log(total)
        out_ref[...] = jnp.transpose(o_buf[...])
        run_due(slots, pair, pairs, 2, 2)


def run_due(due, step, steps, point, points):
    for k in range(steps):
        work = due.get(k * points + point, [])
        if k < steps - 1 and point >= points:
            continue
        if work:

            @pl.when(step == k)
            def _(work=work):
                for array, number in work:
                    array.phase(number)


def timed(arrays, starts, lags, slots):
    due = {slot: [] for slot in range(slots)}
    for array, start in reversed(list(zip(arrays, starts))):
        for number, lag in enumerate(lags):
            due[min(start + lag, slots - 1)].append((array, number))
    for work in due.values():
        work.sort(key=lambda item: item[1])
    return due


def pair_specs(rows):
    pair = lambda first: pl.BlockSpec((rows, 128), lambda p: (0, first + p))
    whole = pl.BlockSpec((rows, 128), lambda p: (0, 0))
    return pair, whole


def forward(D, F, clip_len, patches, stats, table, pos, vec, w_qkv, q_seg, k_seg, shards, collective_id):
    rows, width = patches.shape
    pairs = HEADS // 2
    part = 256
    parts = rows // part
    hbm = pl.BlockSpec(memory_space=pl.ANY)
    once = lambda a: pl.BlockSpec(a.shape, lambda p: (0,) * a.ndim, pipeline_mode=pl.Buffered(1))
    by_row = lambda n: pl.BlockSpec((part, n), lambda p: (jnp.minimum(p, parts - 1), 0))
    X, Y = F // 4, 2
    n = Gather.count(D, X, Y)
    return pl.pallas_call(
        partial(forward_kernel, D, F),
        name="forward",
        grid=(parts + pairs,),
        in_specs=[
            pl.BlockSpec(memory_space=pltpu.SMEM),
            by_row(width),
            once(stats),
            pl.BlockSpec((1, part, POS_PAD), lambda p: (0, jnp.minimum(p, parts - 1), 0)),
            pl.BlockSpec((1, part, POS_PAD), lambda p: (1, jnp.minimum(p, parts - 1), 0)),
        ]
        + [once(a) for a in (pos, vec, w_qkv, q_seg, k_seg)]
        + [hbm] * 3,
        out_specs=[
            by_row(width),
            pl.BlockSpec((width, part), lambda p: (0, jnp.minimum(p, parts - 1))),
            by_row(3 * width),
            pl.BlockSpec((rows, 128), lambda p: (0, jnp.maximum(p - parts, 0))),
            pl.BlockSpec((1, 8, rows), lambda p: (jnp.maximum(p - parts, 0), 0, 0)),
        ]
        + [hbm] * 3,
        out_shape=[
            jax.ShapeDtypeStruct((rows, width), F32),
            jax.ShapeDtypeStruct((width, rows), BF),
            jax.ShapeDtypeStruct((rows, 3 * width), BF),
            jax.ShapeDtypeStruct((rows, 128 * pairs), BF),
            jax.ShapeDtypeStruct((pairs, 8, rows), F32),
        ]
        + [jax.ShapeDtypeStruct((D, Y, X, 2) + s.shape, s.dtype) for s in shards],
        scratch_shapes=[
            pltpu.VMEM((rows, 3 * width), BF),
            pltpu.VMEM((rows, 128), BF),
            pltpu.VMEM((rows, 128), BF),
            pltpu.VMEM((rows, 256), BF),
            pltpu.VMEM((2, 80, rows), BF),
            pltpu.VMEM((128, rows), BF),
        ]
        + copy_semaphores(sum(FORWARD_PARTS), n),
        compiler_params=pltpu.CompilerParams(
            collective_id=collective_id, has_side_effects=True, vmem_limit_bytes=VMEM_LIMIT
        ),
        cost_estimate=pl.CostEstimate(
            flops=4 * 12 * rows * rows * 256 + 2 * rows * width * (3 * width + POS_PAD),
            bytes_accessed=40 * 2**20,
            transcendentals=12 * rows * rows,
        ),
    )(clip_len, patches, stats, table, table, pos, vec, w_qkv, q_seg, k_seg, *shards)


class PairScatter(Scatter):
    def __init__(self, pair, *rest):
        super().__init__(*rest)
        self.pair = pair

    def store(self, total):
        width = self.total.shape[-1] // 3
        for i in range(3):
            first = i * width + 128 * self.pair
            self.total[:, first : first + 128] = total[:, 128 * i : 128 * i + 128]


def backward_pair(
    D, F,
    q_ref, k_ref, v_ref, do_ref, qs_ref, ks_ref, lse_ref, delta_ref, first_t, g_fc2, g_proj, g_fc1, *refs,
):
    dq_ref, dk_ref, dv_ref, g_last, t_fc2, t_proj, t_fc1, t_qkv = refs[:8]
    key_buf, kt_buf, dk_acc, dv_acc, dqt_buf, wide = refs[8:14]
    pairs = HEADS // 2
    held, rest = refs[14 : 14 + EARLY_PAIRS], refs[14 + EARLY_PAIRS : -3]
    send, recv, own = refs[-3:]
    pair = pl.program_id(0)
    rows = q_ref.shape[0]
    q_block = 256
    blocks = rows // q_block
    at = Place(D, F)

    @pl.when(pair == 0)
    def _():
        meet(at.partners())

    pieces = pieces_of((g_fc2, g_proj, g_fc1), (t_fc2, t_proj, t_fc1), BACKWARD_PARTS)
    early = sum(BACKWARD_PARTS)
    per_held = 4 if at.X == at.Y else 6
    split = len(rest) - per_held * EARLY_PAIRS
    arrays = scatter_arrays(at, pieces, rest[:split], send, recv, own)
    for p in range(EARLY_PAIRS):
        bufs = rest[split + p * per_held : split + (p + 1) * per_held]
        i = early + p
        arrays.append(PairScatter(p, at, held[p], t_qkv, bufs, send.at[i], recv.at[i], own.at[i]))
    starts = list(range(early)) + [max(early + p, 2 * p + 2) for p in range(EARLY_PAIRS)]
    due = timed(arrays, starts, BACKWARD_LAGS, 2 * pairs + 1)
    keys, query, half = attend_pair(q_ref, k_ref, v_ref, qs_ref, ks_ref, q_block)
    key_buf[...] = keys
    kt_buf[...] = jnp.transpose(k_ref[...])
    for i in range(blocks):
        if i in (0, 3):
            run_due(due, pair, pairs, i // 3, 2)
        block = pl.ds(i * q_block, q_block)
        for head in range(2):
            q_ext = query(block, head)
            d_out = half(do_ref[block, :], head)
            scores = nt(key_buf[...], q_ext)
            probs = jnp.exp(scores - lse_ref[0, head : head + 1, block])
            d_probs = nt(v_ref[...], d_out)
            d_scores = (probs * (d_probs - delta_ref[0, head : head + 1, block])).astype(BF)
            dv = nn(probs.astype(BF), d_out)
            dk = nn(d_scores, q_ext[:, :128])
            if i == 0 and head == 0:
                dv_acc[...] = dv
                dk_acc[...] = dk
            else:
                dv_acc[...] += dv
                dk_acc[...] += dk
            dq = nn(kt_buf[64 * head : 64 * head + 64, :], d_scores)
            dqt_buf[64 * head : 64 * head + 64, block] = (dq * 0.125).astype(BF)
    dq_ref[...] = jnp.transpose(dqt_buf[...])
    dk_ref[...] = dk_acc[...].astype(BF)
    dv_ref[...] = dv_acc[...].astype(BF)
    joined = jnp.concatenate([dq_ref[...], dk_ref[...], dv_ref[...]], axis=1)
    wide[...] = nn(first_t[...], joined)
    for p in range(EARLY_PAIRS):

        @pl.when(pair == p)
        def _(p=p):
            arrays[early + p].fill(wide)

    @pl.when(pair >= EARLY_PAIRS)
    def _():
        g_last[...] = wide[...].astype(BF)

    run_due(due, pair, pairs, 2, 2)


def attend_backward(D, F, qkv, grad_attended, q_seg, k_seg, lse, delta, first_t, grads, collective_id):
    rows = qkv.shape[0]
    width = first_t.shape[0]
    pairs = HEADS // 2
    pair, whole = pair_specs(rows)
    line = pl.BlockSpec((1, 8, rows), lambda p: (p, 0, 0))
    hbm = pl.BlockSpec(memory_space=pl.ANY)
    once = lambda shape: pl.BlockSpec(shape, lambda p: (0,) * len(shape), pipeline_mode=pl.Buffered(1))
    X, Y = F // 4, 2
    n = Scatter.count(D, X, Y)
    own_rows = width // (D * F)
    held = [pltpu.VMEM(blocks_shape(D, X, Y, width, 384), BF)] * EARLY_PAIRS
    held_scratch = []
    for _ in range(EARLY_PAIRS):
        held_scratch += Scatter.scratch(D, X, Y, own_rows, 384, held=True)
    totals = [jax.ShapeDtypeStruct(g.shape[-2:], F32) for g in grads]
    totals.append(jax.ShapeDtypeStruct((own_rows, 3 * width), F32))
    return pl.pallas_call(
        partial(backward_pair, D, F),
        name="attend_backward",
        grid=(pairs,),
        in_specs=[pair(0), pair(pairs), pair(2 * pairs), pair(0), whole, whole, line, line]
        + [once(first_t.shape)]
        + [hbm] * 3,
        out_specs=[pair(0)] * 3
        + [pl.BlockSpec((width, 384), lambda p: (0, jnp.maximum(p - EARLY_PAIRS, 0)))]
        + [once(t.shape) for t in totals],
        out_shape=[jax.ShapeDtypeStruct((rows, 128 * pairs), BF)] * 3
        + [jax.ShapeDtypeStruct((width, 384 * (pairs - EARLY_PAIRS)), BF)]
        + totals,
        scratch_shapes=[
            pltpu.VMEM((rows, 256), BF),
            pltpu.VMEM((128, rows), BF),
            pltpu.VMEM((rows, 128), F32),
            pltpu.VMEM((rows, 128), F32),
            pltpu.VMEM((128, rows), BF),
            pltpu.VMEM((width, 384), F32),
        ]
        + held
        + scatter_scratch(D, X, Y, grads, BACKWARD_PARTS)
        + held_scratch
        + copy_semaphores(sum(BACKWARD_PARTS) + EARLY_PAIRS, n),
        compiler_params=pltpu.CompilerParams(
            collective_id=collective_id, has_side_effects=True, vmem_limit_bytes=VMEM_LIMIT
        ),
        cost_estimate=pl.CostEstimate(
            flops=10 * 12 * rows * rows * 256,
            bytes_accessed=14 * rows * 768,
            transcendentals=12 * rows * rows,
        ),
    )(qkv, qkv, qkv, grad_attended, q_seg, k_seg, lse, delta, first_t, *grads)


def gelu_both(u):
    z = jnp.abs(u)
    falling = jnp.exp(-0.5 * u * u)
    t = 1.0 / (1.0 + TAIL_P * z)
    poly = TAIL_C[-1]
    for coefficient in TAIL_C[-2::-1]:
        poly = poly * t + coefficient
    tail = poly * t * falling
    upper = jnp.where(u >= 0, 1.0 - tail, tail)
    return u * upper, upper + u * falling * 0.3989422804014327


def norm_parts(values):
    center = values - jnp.mean(values, axis=1, keepdims=True)
    spread = jnp.mean(center * center, axis=1, keepdims=True)
    rho = lax.rsqrt(spread + NORM_EPS)
    return center * rho, rho


def norm_back(n, rho, grad, gain):
    q = grad * gain
    return rho * (q - jnp.mean(q, axis=1, keepdims=True) - n * jnp.mean(q * n, axis=1, keepdims=True))


def fold(values):
    return jnp.sum(values.reshape(-1, 8, values.shape[1]), axis=0)


def middle_kernel(
    D, F, tiles,
    stats, emb, att, cot, wo, w1, b1, w2, vec, pick,
    layer_out, res_grad, att_grad, delta_out, g_proj, g_fc1, g_b1, g_fc2, g_small, t_fc1,
    residual, second, second_t, mlp, g_second, act_buf, pre_buf, wide, *rest,
):
    step = pl.program_id(0)
    rows, width = emb.shape
    tile = w1.shape[1]
    block_rows = 256
    blocks = rows // block_rows
    ones = jnp.ones((8, block_rows), BF)
    masked, branch = layer_out, second
    at = Place(D, F)
    held, bufs, (send, recv, own) = rest[:EARLY_TILES], rest[EARLY_TILES:-3], rest[-3:]
    per = len(bufs) // EARLY_TILES
    arrays = [
        Scatter(
            at, held[j], t_fc1.at[:, pl.ds(j * tile, tile)], bufs[j * per : (j + 1) * per],
            send.at[j], recv.at[j], own.at[j],
        )
        for j in range(EARLY_TILES)
    ]
    due = timed(arrays, [2 * j + 2 for j in range(EARLY_TILES)], MIDDLE_LAGS, 2 * tiles + 2)

    def take(i):
        return pl.ds(pl.multiple_of(i * block_rows, block_rows), block_rows)

    def flags(i):
        row = lax.broadcasted_iota(jnp.int32, (block_rows, width), 0).astype(F32)
        return row + jnp.asarray(i * block_rows, jnp.int32).astype(F32) < stats[3:4, :]

    @pl.when(step == 0)
    def _():
        meet(at.partners())

        def one(i, _):
            block = take(i)
            branch_out = nn(att[block, :], wo[...]) + vec[4:5, :]
            res = emb[block, :] + branch_out
            residual[block, :] = res
            n, _rho = norm_parts(res)
            sn = (n * vec[5:6, :] + vec[6:7, :]).astype(BF)
            second[block, :] = sn
            second_t[i] = jnp.transpose(sn)
            masked[block, :] = jnp.where(flags(i), cot[block, :].astype(F32), 0.0).astype(BF)
            mlp[block, :] = jnp.zeros((block_rows, width), F32)
            g_second[block, :] = jnp.zeros((block_rows, width), F32)
            return 0

        lax.fori_loop(0, blocks, one, 0)

    bias = b1[...]
    for i in range(blocks):
        if i in (0, 3):
            run_due(due, step, tiles, i // 3, 2)
        block = pl.ds(i * block_rows, block_rows)
        pre = nn(second[block, :], w1[...]) + bias
        act, slope = gelu_both(pre)
        act = act.astype(BF)
        act_buf[block, :] = act
        grad_act = nt(masked[block, :], w2[...]).astype(BF).astype(F32)
        grad_pre = (grad_act * slope).astype(BF)
        pre_buf[block, :] = grad_pre
        mlp[block, :] += nn(act, w2[...])
        g_second[block, :] += nt(grad_pre, w1[...])
    g_fc2[...] = tn(act_buf[...], masked[...]).astype(BF)
    for i in range(blocks):
        block = pl.ds(i * block_rows, block_rows)
        part = nn(second_t[i], pre_buf[block, :])
        line = nn(ones, pre_buf[block, :])
        total = part if i == 0 else total + part
        lines = line if i == 0 else lines + line
    wide[...] = total
    g_b1[...] = lines
    for j in range(EARLY_TILES):

        @pl.when(step == j)
        def _(j=j):
            arrays[j].fill(wide)

    @pl.when(step >= EARLY_TILES)
    def _():
        g_fc1[...] = wide[...].astype(BF)

    run_due(due, step, tiles, 2, 2)

    @pl.when(step == tiles - 1)
    def _():
        def one(i, sums):
            block = take(i)
            res = residual[block, :]
            n, rho = norm_parts(res)
            out_grad = masked[block, :]
            layer_out[block, :] = jnp.where(flags(i), res + mlp[block, :] + vec[7:8, :], 0.0).astype(BF)
            grad = g_second[block, :].astype(BF).astype(F32)
            back = norm_back(n, rho, grad, vec[5:6, :])
            total = out_grad.astype(F32) + back
            res_grad[block, :] = total
            low = total.astype(BF)
            branch[block, :] = low
            into = nt(low, wo[...]).astype(BF)
            att_grad[block, :] = into
            product = into.astype(F32) * att[block, :].astype(F32)
            high = product.astype(BF)
            rest = (product - high.astype(F32)).astype(BF)
            delta = nn(high, pick[...]) + nn(rest, pick[...])
            delta_out[:, block] = jnp.transpose(delta)[: delta_out.shape[0], :]
            return (
                sums[0] + nn(ones, low)[0:8],
                sums[1] + fold(grad * n),
                sums[2] + fold(grad),
                sums[3] + nn(ones, out_grad)[0:8],
            )

        empty = jnp.zeros((8, width), F32)
        sums = lax.fori_loop(0, blocks, one, (empty,) * 4)
        g_proj[...] = tn(att[...], branch[...]).astype(BF)
        g_small[0:1, :] = sums[0][0:1]
        g_small[1:2, :] = jnp.sum(sums[1], axis=0, keepdims=True)
        g_small[2:3, :] = jnp.sum(sums[2], axis=0, keepdims=True)
        g_small[3:4, :] = sums[3][0:1]
        g_small[4:8, :] = jnp.zeros((4, width), F32)

    run_due(due, step, tiles, 3, 2)


def middle(D, F, stats, emb, att, cot, wo, w1, b1, w2, vec, collective_id):
    rows, width = emb.shape
    hidden = w1.shape[1]
    tile = 512
    tiles = hidden // tile
    X, Y = F // 4, 2
    own_rows = width // (D * F)
    once = pl.Buffered(1)
    whole = lambda shape: pl.BlockSpec(shape, lambda j: (0,) * len(shape), pipeline_mode=once)
    pick = np.zeros((width, 128), np.float32)
    pick[np.arange(width), np.arange(width) // 64] = 1.0
    pick = jnp.asarray(pick.astype(ml_dtypes.bfloat16))
    out_shape = [
        jax.ShapeDtypeStruct((rows, width), BF),
        jax.ShapeDtypeStruct((rows, width), F32),
        jax.ShapeDtypeStruct((rows, width), BF),
        jax.ShapeDtypeStruct((16, rows), F32),
        jax.ShapeDtypeStruct((width, width), BF),
        jax.ShapeDtypeStruct((width, tile * (tiles - EARLY_TILES)), BF),
        jax.ShapeDtypeStruct((8, hidden), F32),
        jax.ShapeDtypeStruct((hidden, width), BF),
        jax.ShapeDtypeStruct((8, width), F32),
        jax.ShapeDtypeStruct((own_rows, tile * EARLY_TILES), F32),
    ]
    scatter = []
    for _ in range(EARLY_TILES):
        scatter += Scatter.scratch(D, X, Y, own_rows, tile, held=True)
    return pl.pallas_call(
        partial(middle_kernel, D, F, tiles),
        name="middle",
        grid=(tiles,),
        in_specs=[
            whole(stats.shape),
            whole((rows, width)),
            whole((rows, width)),
            whole((rows, width)),
            whole((width, width)),
            pl.BlockSpec((width, tile), lambda j: (0, j)),
            pl.BlockSpec((1, tile), lambda j: (0, j)),
            pl.BlockSpec((tile, width), lambda j: (j, 0)),
            whole((8, width)),
            whole((width, 128)),
        ],
        out_specs=[whole(s.shape) for s in out_shape[:5]]
        + [
            pl.BlockSpec((width, tile), lambda j: (0, jnp.maximum(j - EARLY_TILES, 0))),
            pl.BlockSpec((8, tile), lambda j: (0, j)),
            pl.BlockSpec((tile, width), lambda j: (j, 0)),
            whole((8, width)),
            whole(out_shape[9].shape),
        ],
        scratch_shapes=[
            pltpu.VMEM((rows, width), F32),
            pltpu.VMEM((rows, width), BF),
            pltpu.VMEM((rows // 256, width, 256), BF),
            pltpu.VMEM((rows, width), F32),
            pltpu.VMEM((rows, width), F32),
            pltpu.VMEM((rows, tile), BF),
            pltpu.VMEM((rows, tile), BF),
            pltpu.VMEM((width, tile), F32),
        ]
        + [pltpu.VMEM(blocks_shape(D, X, Y, width, tile), BF)] * EARLY_TILES
        + scatter
        + copy_semaphores(EARLY_TILES, Scatter.count(D, X, Y)),
        out_shape=out_shape,
        compiler_params=pltpu.CompilerParams(
            collective_id=collective_id, has_side_effects=True, vmem_limit_bytes=VMEM_LIMIT
        ),
        cost_estimate=pl.CostEstimate(
            flops=2 * rows * width * (6 * hidden + 3 * width),
            bytes_accessed=40 * 2**20,
            transcendentals=rows * hidden,
        ),
    )(stats, emb, att, cot, wo, w1, b1, w2, vec, pick)


def last_kernel(
    D, F,
    lens, gq, gk, gv, emb, res_grad, patches, stats, sel_long, sel_short, w_ref, vec, small_in, bias_in, g_last,
    patch_grad, small_out, t_last, t_pos,
    pos_acc, masked, normed_buf, sums, pos_a, pos_b, z_buf, f_buf, s_send, s_recv, *rest,
):
    step = pl.program_id(0)
    rows, width = emb.shape
    total_rows = patch_grad.shape[0]
    steps = total_rows // rows
    ones = jnp.ones((8, rows), BF)
    at = Place(D, F)
    bufs, (send, recv, own) = rest[:-3], rest[-3:]
    per_held = 4 if at.X == at.Y else 6
    early = Scatter(at, g_last, t_last, bufs[: per_held + 1], send.at[0], recv.at[0], own.at[0])
    pos_blocks = (pos_a, pos_b)
    half = POS_PAD // 2
    pos = [
        Scatter(
            at, pos_blocks[i], t_pos.at[:, pl.ds(half * i, half)],
            bufs[per_held + 1 + per_held * i : per_held + 1 + per_held * (i + 1)],
            send.at[1 + i], recv.at[1 + i], own.at[1 + i],
        )
        for i in range(2)
    ]
    total = Total(at, (z_buf, f_buf), s_send, s_recv)

    @pl.when(step == 0)
    def _():
        meet(at.everyone())
        early.phase(0)
        sums[...] = jnp.zeros_like(sums)

    for number in range(1, 5):

        @pl.when(step == number)
        def _(number=number):
            early.phase(number)

    parts = [gq[...], gk[...], gv[...]]
    for i, part in enumerate(parts):
        into = nt(part, w_ref[:, i * width : (i + 1) * width])
        grad = into if i == 0 else grad + into
    grad = grad.astype(BF).astype(F32)
    n, rho = norm_parts(emb[...])
    row = lax.broadcasted_iota(jnp.int32, (rows, width), 0).astype(F32) + (step * rows).astype(F32)
    valid = row < stats[3:4, :]
    whole = jnp.where(valid, res_grad[...] + norm_back(n, rho, grad, vec[0:1, :]), 0.0)
    block = pl.ds(pl.multiple_of(step * rows, rows), rows)
    masked[block, :] = whole
    sel = jnp.where(lens[0, 1] > 0, sel_short[0], sel_long[0])
    moved = tn(whole.astype(BF), sel)

    @pl.when(step == 0)
    def _():
        pos_acc[...] = moved

    @pl.when(step > 0)
    def _():
        pos_acc[...] += moved

    normed = (patches[...].astype(F32) - stats[0:1, :]) * stats[1:2, :]
    normed_buf[block, :] = jnp.where(valid, normed, 0.0)
    sums[0] += fold(grad * n)
    sums[1] += fold(grad)
    sums[2] += nn(ones, parts[0])
    sums[3] += nn(ones, parts[2])
    sums[4] += fold(whole)
    sums[5] += fold(whole * normed)

    @pl.when(step == steps - 1)
    def _():
        lines = []
        for i in range(6):
            line = sums[i]
            lines.append(line[0:1] if i in (2, 3) else jnp.sum(line, axis=0, keepdims=True))
        own_vec = lines[:4] + [small_in[i : i + 1, :] for i in range(4)]
        ahead = LONG - (POS_PAD - 128)
        own_vec = [jnp.zeros((ahead, width), F32)] + own_vec + [jnp.zeros((128 - ahead - 8, width), F32)]
        pos_acc[:, POS_PAD - 128 :] += jnp.transpose(jnp.concatenate(own_vec, axis=0))
        pos[0].fill(pos_acc.at[:, :half])
        pos[0].phase(0)
        pos[1].fill(pos_acc.at[:, half:])
        pos[1].phase(0)
        hidden = bias_in.shape[1]
        own_lines = lines[4:] + [bias_in[0:1, i * width : (i + 1) * width] for i in range(hidden // width)]
        own_lines += [jnp.zeros((1, width), F32)] * (8 - len(own_lines))
        total.start(jnp.concatenate(own_lines, axis=0))
        pos[0].phase(1)
        pos[1].phase(1)
        total.middle()
        pos[0].phase(2)
        pos[1].phase(2)
        summed = total.end()
        small_out[...] = summed
        pos[0].phase(3)
        pos[1].phase(3)
        inv_std, inv_count = stats[1:2, :], stats[2:3, :]
        plain, scaled = summed[0:1] * inv_count, summed[1:2] * inv_count

        def one(i, _):
            part = pl.ds(pl.multiple_of(i * 64, 64), 64)
            valid = flag_buf(i)
            value = masked[part, :] - valid * plain - normed_buf[part, :] * scaled
            patch_grad[part, :] = (inv_std * value).astype(BF)
            return 0

        valid_rows = stats[3:4, :]

        def flag_buf(i):
            row = lax.broadcasted_iota(jnp.int32, (64, width), 0).astype(F32)
            return jnp.where(row + (i * 64).astype(F32) < valid_rows, 1.0, 0.0)

        lax.fori_loop(0, total_rows // 64, one, 0)
        pos[0].phase(4)
        pos[1].phase(4)


def last_back(D, F, clip_len, gq, gk, gv, emb, res_grad, patches, stats, table, w_qkv, vec, small, bias, g_last, collective_id):
    rows, width = emb.shape
    block = 256
    once = pl.Buffered(1)
    whole = lambda shape: pl.BlockSpec(shape, lambda i: (0,) * len(shape), pipeline_mode=once)
    by_row = lambda n: pl.BlockSpec((block, n), lambda i: (i, 0))
    X, Y = F // 4, 2
    own_rows = width // (D * F)
    n = Scatter.count(D, X, Y)
    out_shape = [
        jax.ShapeDtypeStruct((rows, width), BF),
        jax.ShapeDtypeStruct((8, width), F32),
        jax.ShapeDtypeStruct((own_rows, g_last.shape[-1]), F32),
        jax.ShapeDtypeStruct((own_rows, POS_PAD), F32),
    ]
    return pl.pallas_call(
        partial(last_kernel, D, F),
        name="last_back",
        grid=(rows // block,),
        in_specs=[pl.BlockSpec(memory_space=pltpu.SMEM)]
        + [by_row(width)] * 6
        + [
            whole(stats.shape),
            pl.BlockSpec((1, block, POS_PAD), lambda i: (0, i, 0)),
            pl.BlockSpec((1, block, POS_PAD), lambda i: (1, i, 0)),
            whole(w_qkv.shape),
            whole(vec.shape),
        ]
        + [whole(small.shape), whole(bias.shape), pl.BlockSpec(memory_space=pl.ANY)],
        out_specs=[whole(o.shape) for o in out_shape],
        out_shape=out_shape,
        scratch_shapes=[
            pltpu.VMEM((width, POS_PAD), F32),
            pltpu.VMEM((rows, width), F32),
            pltpu.VMEM((rows, width), F32),
            pltpu.VMEM((6, 8, width), F32),
            pltpu.VMEM(blocks_shape(D, X, Y, width, POS_PAD // 2), BF),
            pltpu.VMEM(blocks_shape(D, X, Y, width, POS_PAD // 2), BF),
        ]
        + Total.scratch(D, F, 8, width)
        + [pltpu.SemaphoreType.DMA((Total.count(D, F),)), pltpu.SemaphoreType.DMA((Total.count(D, F),))]
        + Scatter.scratch(D, X, Y, own_rows, g_last.shape[-1])
        + Scatter.scratch(D, X, Y, own_rows, POS_PAD // 2, held=True) * 2
        + copy_semaphores(3, n),
        compiler_params=pltpu.CompilerParams(
            collective_id=collective_id, has_side_effects=True, vmem_limit_bytes=VMEM_LIMIT
        ),
        cost_estimate=pl.CostEstimate(
            flops=2 * rows * width * (6 * width + POS_PAD),
            bytes_accessed=30 * 2**20,
            transcendentals=0,
        ),
    )(clip_len, gq, gk, gv, emb, res_grad, patches, stats, table, table, w_qkv, vec, small, bias, g_last)


def average_keep():
    return min(0.99, (1.0 + PRIOR_STEPS) / (10.0 + PRIOR_STEPS))


def stepped(rate, g, w, m, e):
    keep = average_keep()
    moved = MOMENTUM * m + g
    update = -(rate * (g + MOMENTUM * moved))
    return g, update, moved, keep * e + (1.0 - keep) * (w + update)


def optimizer_kernel(rate, t_pos, t_early, t_late, t_proj, t_most, t_last, t_fc2, *refs):
    states, outs = refs[:18], refs[18:]
    names = 6

    def write(i, where, g):
        w, m, e = (states[3 * i + j][where] for j in range(3))
        for out, value in zip(outs[4 * i : 4 * i + 4], stepped(rate, g, w, m, e)):
            out[where] = value

    everything = (slice(None), slice(None))
    write(0, everything, t_pos[:, :LONG])
    ahead = LONG - (POS_PAD - 128)
    write(1, everything, jnp.transpose(t_pos[:, POS_PAD - 128 :])[ahead : ahead + 8])
    width = t_early.shape[1] // 3
    early = 128 * EARLY_PAIRS
    for i in range(3):
        first = i * width
        write(2, (slice(None), slice(first, first + early)), t_early[:, first : first + early])
        for k in range(HEADS // 2 - EARLY_PAIRS):
            to = first + early + 128 * k
            source = 384 * k + 128 * i
            write(2, (slice(None), slice(to, to + 128)), t_late[:, source : source + 128])
    write(3, everything, t_proj[...])
    most = t_most.shape[1]
    write(4, (slice(None), slice(0, most)), t_most[...])
    write(4, (slice(None), slice(most, most + t_last.shape[1])), t_last[...])
    write(5, everything, t_fc2[...])


def optimize(rate, totals, states):
    vmem = pl.BlockSpec(memory_space=pltpu.VMEM)
    flat = [a for group in states for a in group]
    out = pl.pallas_call(
        partial(optimizer_kernel, rate),
        name="optimizer",
        in_specs=[vmem] * (len(totals) + len(flat)),
        out_specs=[vmem] * (4 * len(states)),
        out_shape=[jax.ShapeDtypeStruct(group[0].shape, F32) for group in states for _ in range(4)],
        compiler_params=pltpu.CompilerParams(vmem_limit_bytes=VMEM_LIMIT),
    )(*totals, *flat)
    return [tuple(out[4 * i : 4 * i + 4]) for i in range(len(states))]


def local(
    D, F,
    patches, cotangent, clip_len,
    pos_table, vector_params, w_qkv, w_proj, w_fc1, b_fc1, w_fc2,
    *states,
):
    params = (pos_table, vector_params, w_qkv, w_proj, w_fc1, b_fc1, w_fc2)
    momenta, averages = states[:7], states[7:]
    local_rows, width = patches.shape
    hidden = w_fc1.shape[1]
    group_size = D * F
    X, Y = F // 4, 2
    table = selectors(local_rows)
    stats, vec, bias_full, q_seg, k_seg, proj_b, fc1_b, fc2_b, pos_full, qkv_full = head(
        D, F, clip_len, patches, pos_table, vector_params, w_qkv, b_fc1, w_proj, w_fc1, w_fc2, 0
    )
    pos_full, qkv_full = (w.reshape(-1, w.shape[-1]) for w in (pos_full, qkv_full))
    emb, first_t, qkv, attended, lse, *full = forward(
        D, F, clip_len, patches, stats, table, pos_full, vec, qkv_full, q_seg, k_seg,
        (proj_b, fc1_b, fc2_b), 1,
    )
    proj_full, fc1_full, fc2_full = (w.reshape(-1, w.shape[-1]) for w in full)
    layer_out, res_grad, att_grad, delta, g_proj, g_fc1, g_b1, g_fc2, g_small_mid, t_fc1_most = middle(
        D, F, stats, emb, attended, cotangent, proj_full, fc1_full, bias_full, fc2_full, vec, 4
    )
    delta = jnp.pad(delta[:HEADS].reshape(HEADS // 2, 2, local_rows), ((0, 0), (0, 6), (0, 0)))
    spans = lambda g: g.reshape(D, Y, X, 2, -1, g.shape[-1])
    gq, gk, gv, g_last, t_fc2, t_proj, t_fc1, t_qkv = attend_backward(
        D, F, qkv, att_grad, q_seg, k_seg, lse, delta, first_t,
        [spans(g) for g in (g_fc2, g_proj, g_fc1)], 2,
    )
    patch_grad, small_sum, t_late, t_pos = last_back(
        D, F, clip_len, gq, gk, gv, emb, res_grad, patches, stats, table, qkv_full, vec,
        g_small_mid, g_b1, spans(g_last), 3,
    )
    rate = 0.02 * (local_rows * group_size) ** (-0.5)
    groups = list(zip(params, momenta, averages))
    groups[1] = tuple(a.T for a in groups[1])
    big = [groups[i] for i in (0, 1, 2, 3, 4, 6)]
    done = optimize(rate, (t_pos, t_qkv, t_late, t_proj, t_fc1_most, t_fc1, t_fc2), big)
    me = lax.axis_index("dp") * F + lax.axis_index("fsdp")
    n_bias = b_fc1.size
    g_bias = lax.dynamic_slice(small_sum[2 : 2 + hidden // width].reshape(-1), (me * n_bias,), (n_bias,))
    done[1] = tuple(a.T for a in done[1])
    done.insert(5, stepped(rate, g_bias, *groups[5]))
    feature_stats = jnp.stack([stats[0], stats[4]])
    return (layer_out, patch_grad, feature_stats) + tuple(d[i] for i in range(4) for d in done)


def solution(mesh):
    rows, line = P(AXES, None), P(AXES)
    params = (rows, rows, rows, rows, rows, line, rows)
    return jax.shard_map(
        partial(local, mesh.shape["dp"], mesh.shape["fsdp"]),
        mesh=mesh,
        in_specs=(rows,) * 3 + params * 3,
        out_specs=(rows, rows, P()) + params * 4,
        check_vma=False,
    )
```

```python
from functools import partial

import jax
import jax.numpy as jnp
import ml_dtypes
import numpy as np
from jax import lax
from jax.experimental import pallas as pl
from jax.experimental.pallas import tpu as pltpu
from jax.sharding import PartitionSpec as P

HEADS = 12
FREQ_L = 12
TIME_L = 101
FREQ_S = 8
TIME_S = 64
PRIOR_STEPS = 3
LONG = 1214
SHORT = 514

NORM_EPS = 1e-06
INPUT_EPS = 1e-05
MOMENTUM = 0.9
MESH = pl.DeviceIdType.MESH
AXES = ("dp", "fsdp")
BF = jnp.bfloat16
F32 = jnp.float32
VMEM_LIMIT = 60 * 2**20
POS_PAD = 1280
HEAD_PARTS = (2, 3)
FORWARD_PARTS = (1, 4, 3)
BACKWARD_PARTS = (2, 1, 1)
BACKWARD_LAGS = ((0, 2, 4, 6, 8),) * 4 + ((0, 2, 4, 6, 7), (0, 1, 2, 3, 4))
EARLY_PAIRS = 4
PAIR_GROUP = 2
MIDDLE_LAGS = ((0, 2, 4, 6, 8),) * 3
EARLY_TILES = 3


TAIL_P = 0.305
TAIL_C = (
    0.121639732,
    0.122466826,
    0.10342081,
    0.121021868,
    -0.037977191,
    0.185717298,
    -0.152988541,
    0.036699245,
)


def resize_rows(size_in, size_out):
    resize_table = np.zeros((size_out, size_in), np.float64)
    for target_row in range(size_out):
        source_pos = max((target_row + 0.5) * size_in / size_out - 0.5, 0.0)
        lower_cell = min(int(np.floor(source_pos)), size_in - 1)
        upper_cell = min(lower_cell + 1, size_in - 1)
        fraction = source_pos - lower_cell
        resize_table[target_row, lower_cell] += 1.0 - fraction
        resize_table[target_row, upper_cell] += fraction
    return resize_table


def selectors(local_rows):
    table = np.zeros((2, local_rows, POS_PAD), np.float64)
    table[0, :LONG, :LONG] = np.eye(LONG)
    short = np.zeros((SHORT, LONG), np.float64)
    short[0, 0] = short[1, 1] = 1.0
    short[2:, 2:] = np.kron(resize_rows(FREQ_L, FREQ_S), resize_rows(TIME_L, TIME_S))
    for first in (0, SHORT):
        table[1, first : first + SHORT, :LONG] = short
    return jnp.asarray(table.astype(ml_dtypes.bfloat16))


def nn(left, right):
    return lax.dot_general(left, right, (((1,), (0,)), ((), ())), preferred_element_type=F32)


def nt(left, right):
    return lax.dot_general(left, right, (((1,), (1,)), ((), ())), preferred_element_type=F32)


def tn(left, right):
    return lax.dot_general(left, right, (((0,), (0,)), ((), ())), preferred_element_type=F32)


class Place:
    def __init__(self, dp_size, fsdp_size):
        self.D, self.F = dp_size, fsdp_size
        self.X, self.Y = fsdp_size // 4, 2
        self.d = lax.axis_index("dp")
        self.f = lax.axis_index("fsdp")
        self.c = lax.rem(self.f, 2)
        self.x = lax.rem(lax.div(self.f, 2), self.X)
        self.y = lax.div(self.f, 2 * self.X)

    def fs(self, y, x, c):
        return (y * self.X + x) * 2 + c

    def up(self, value, step, size):
        return lax.rem(value + step, size)

    def partners(self):
        out = [(self.up(self.d, k, self.D), self.f) for k in range(1, self.D)]
        out += [(self.d, self.fs(self.y, self.up(self.x, k, self.X), self.c)) for k in range(1, self.X)]
        out += [(self.d, self.fs(self.up(self.y, k, self.Y), self.x, self.c)) for k in range(1, self.Y)]
        out.append((self.d, self.fs(self.y, self.x, 1 - self.c)))
        return out

    def everyone(self):
        out = [(self.up(self.d, k, self.D), self.f) for k in range(1, self.D)]
        return out + [(self.d, self.up(self.f, k, self.F)) for k in range(1, self.F)]


def meet(devices):
    barrier = pltpu.get_barrier_semaphore()
    for device in devices:
        pl.semaphore_signal(barrier, inc=1, device_id=device, device_id_type=MESH)
    pl.semaphore_wait(barrier, len(devices))


class Gather:
    @staticmethod
    def count(D, X, Y):
        return (D - 1) + 2 * (X - 1) + 2 * (Y - 1) + 1

    def __init__(self, at, src, out, send, recv, own):
        self.at, self.src, self.out, self.send, self.recv, self.own = at, src, out, send, recv, own
        D, X, Y = at.D, at.X, at.Y
        self.n_z = 0
        self.n_x = D - 1
        self.n_y = self.n_x + X - 1
        self.n_c = self.n_y + Y - 1

    def copy(self, src, dst, number, device):
        return pltpu.make_async_remote_copy(
            src_ref=src,
            dst_ref=dst,
            send_sem=self.send.at[number],
            recv_sem=self.recv.at[number],
            device_id=device,
            device_id_type=MESH,
        )

    def z_copy(self, k):
        at = self.at
        return self.copy(
            self.src,
            self.out.at[at.d, at.y, at.x, at.c],
            self.n_z + k - 1,
            (at.up(at.d, k, at.D), at.f),
        )

    def z_got(self, k):
        at = self.at
        here = self.out.at[at.up(at.d, at.D - k, at.D), at.y, at.x, at.c]
        return self.copy(here, here, self.n_z + k - 1, (at.up(at.d, at.D - k, at.D), at.f))

    def part(self, axis, order, y, x, c):
        if axis == order[0]:
            return self.out.at[:, y, x, c]
        return self.out.at[:, y, :, c] if axis == "y" else self.out.at[:, :, x, c]

    def side(self, axis, order, k, sent):
        at = self.at
        size = at.X if axis == "x" else at.Y
        first = self.n_x if axis == "x" else self.n_y
        mine = at.x if axis == "x" else at.y
        other = at.up(mine, k if sent else size - k, size)
        y, x = (at.y, other) if axis == "x" else (other, at.x)
        block = self.part(axis, order, at.y, at.x, at.c) if sent else self.part(axis, order, y, x, at.c)
        return self.copy(block, block, first + k - 1, (at.d, at.fs(y, x, at.c)))

    def pieces(self, order, c):
        at = self.at
        out = [self.out.at[:, at.y, at.x, c]]
        for axis in order:
            size = at.X if axis == "x" else at.Y
            for k in range(1, size):
                other = at.up(at.x if axis == "x" else at.y, size - k, size)
                y, x = (at.y, other) if axis == "x" else (other, at.x)
                out.append(self.part(axis, order, y, x, c))
        return out

    def sibling(self, block, number):
        at = self.at
        return self.copy(block, block, self.n_c + number, (at.d, at.fs(at.y, at.x, 1 - at.c)))

    def local(self):
        at = self.at
        return pltpu.make_async_copy(self.src, self.out.at[at.d, at.y, at.x, at.c], self.own)

    def size_of(self, axis):
        return self.at.X if axis == "x" else self.at.Y

    def phase(self, number):
        at = self.at
        if number == 0:
            self.local().start()
            for k in range(1, at.D):
                self.z_copy(k).start()
            return
        if number == 1:
            self.local().wait()
            for k in range(1, at.D):
                self.z_got(k).wait_recv()
        for core, order in ((0, ("x", "y")), (1, ("y", "x"))):

            @pl.when(at.c == core)
            def _(core=core, order=order):
                mine = self.pieces(order, core)
                first = 1 + (self.size_of(order[0]) - 1)
                if number == 1:
                    for k in range(1, self.size_of(order[0])):
                        self.side(order[0], order, k, True).start()
                    self.sibling(mine[0], 0).start()
                elif number == 2:
                    for k in range(1, self.size_of(order[0])):
                        self.side(order[0], order, k, False).wait_recv()
                    for k in range(1, self.size_of(order[1])):
                        self.side(order[1], order, k, True).start()
                    for i in range(1, first):
                        self.sibling(mine[i], i).start()
                elif number == 3:
                    for k in range(1, self.size_of(order[1])):
                        self.side(order[1], order, k, False).wait_recv()
                    for i in range(first, len(mine)):
                        self.sibling(mine[i], i).start()
                elif number == 4:
                    for k in range(1, at.D):
                        self.z_copy(k).wait_send()
                    for axis in order:
                        for k in range(1, self.size_of(axis)):
                            self.side(axis, order, k, True).wait_send()
                    for i, block in enumerate(mine):
                        self.sibling(block, i).wait_send()
                    for i, block in enumerate(self.pieces(order[::-1], 1 - core)):
                        self.sibling(block, i).wait_recv()


class Scatter:
    @staticmethod
    def count(D, X, Y):
        return 1 + (Y - 1) + (X - 1) + (D - 1)

    @staticmethod
    def scratch(D, X, Y, R, N, held=False):
        out = [] if held else [pltpu.VMEM((D, Y, X, R, N), BF)]
        out.append(pltpu.VMEM((D, Y, X, R, N), BF))
        out += [pltpu.VMEM((Y - 1, D, X, R, N), BF), pltpu.VMEM((Y - 1, D, R, N), BF)]
        if X != Y:
            out += [pltpu.VMEM((X - 1, D, Y, R, N), BF), pltpu.VMEM((X - 1, D, R, N), BF)]
        return out + [pltpu.VMEM((D - 1, R, N), BF)]

    def __init__(self, at, grad, total, bufs, send, recv, own):
        self.at, self.grad, self.total = at, grad, total
        self.held = len(bufs) % 2 == 0
        bufs = list(bufs)
        self.acc = None if self.held else bufs.pop(0)
        self.r1, self.r2y, self.r3y = bufs[:3]
        self.r2x, self.r3x = (self.r2y, self.r3y) if at.X == at.Y else bufs[3:5]
        self.r4 = bufs[-1]
        self.send, self.recv, self.own = send, recv, own
        self.n_y = 1
        self.n_x = self.n_y + at.Y - 1
        self.n_z = self.n_x + at.X - 1

    def view(self, d, y, x):
        return self.grad.at[d, y, x, self.at.c] if self.held else self.acc.at[d, y, x]

    def get(self, d, y, x):
        return self.grad[d, y, x, self.at.c] if self.held else self.acc[d, y, x]

    def put(self, d, y, x, value):
        if self.held:
            self.grad[d, y, x, self.at.c] = value
        else:
            self.acc[d, y, x] = value

    def fill(self, values, first_column=0):
        at = self.at
        R = self.grad.shape[-2]
        into = slice(first_column, first_column + values.shape[1])

        def one(i, _):
            rest, c = lax.div(i, 2), lax.rem(i, 2)
            rest, x = lax.div(rest, at.X), lax.rem(rest, at.X)
            d, y = lax.div(rest, at.Y), lax.rem(rest, at.Y)
            first = i * R
            if R % 8 == 0:
                block = values[pl.ds(pl.multiple_of(first, 8), R), :].astype(BF)
            else:
                shape = (16, values.shape[0])
                row = lax.broadcasted_iota(jnp.int32, shape, 0)
                pick = jnp.where(lax.broadcasted_iota(jnp.int32, shape, 1) == row + first, 1.0, 0.0)
                block = nn(pick.astype(BF), values[...].astype(BF))[:R].astype(BF)
            self.grad[d, y, x, c, :, into] = block
            return 0

        lax.fori_loop(0, at.D * at.F, one, 0)

    def copy(self, src, dst, number, device):
        return pltpu.make_async_remote_copy(
            src_ref=src,
            dst_ref=dst,
            send_sem=self.send.at[number],
            recv_sem=self.recv.at[number],
            device_id=device,
            device_id_type=MESH,
        )

    def core_copy(self):
        at = self.at
        return self.copy(
            self.grad.at[:, :, :, 1 - at.c], self.r1, 0, (at.d, at.fs(at.y, at.x, 1 - at.c))
        )

    def local(self):
        return pltpu.make_async_copy(self.grad.at[:, :, :, self.at.c], self.acc, self.own)

    def side(self, axis, order, k):
        at, all_d = self.at, slice(None)
        if axis == "y":
            y = at.up(at.y, k, at.Y)
            device = (at.d, at.fs(y, at.x, at.c))
            if axis == order[0]:
                src, dst = self.view(all_d, y, slice(None)), self.r2y
            else:
                src, dst = self.view(all_d, y, at.x), self.r3y
            return self.copy(src, dst.at[k - 1], self.n_y + k - 1, device)
        x = at.up(at.x, k, at.X)
        device = (at.d, at.fs(at.y, x, at.c))
        if axis == order[0]:
            src, dst = self.view(all_d, slice(None), x), self.r2x
        else:
            src, dst = self.view(all_d, at.y, x), self.r3x
        return self.copy(src, dst.at[k - 1], self.n_x + k - 1, device)

    def z_copy(self, k):
        at = self.at
        d = at.up(at.d, k, at.D)
        return self.copy(self.view(d, at.y, at.x), self.r4.at[k - 1], self.n_z + k - 1, (d, at.f))

    def size_of(self, axis):
        return self.at.X if axis == "x" else self.at.Y

    def store(self, total):
        self.total[...] = total

    def phase(self, number):
        at = self.at
        if number == 0:
            if not self.held:
                self.local().start()
            self.core_copy().start()
            return
        if number == 1:
            if not self.held:
                self.local().wait()
            self.core_copy().wait_recv()

            def add(i, _):
                d, rest = lax.div(i, at.Y * at.X), lax.rem(i, at.Y * at.X)
                y, x = lax.div(rest, at.X), lax.rem(rest, at.X)
                self.put(d, y, x, self.get(d, y, x) + self.r1[d, y, x])
                return 0

            lax.fori_loop(0, at.D * at.Y * at.X, add, 0)
        if number == 4:
            for k in range(1, at.D):
                self.z_copy(k).wait_recv()
            total = self.get(at.d, at.y, at.x).astype(F32)
            for k in range(1, at.D):
                total = total + self.r4[k - 1].astype(F32)
            self.store(total)
            self.core_copy().wait_send()
            for k in range(1, at.D):
                self.z_copy(k).wait_send()
        for core, order in ((0, ("y", "x")), (1, ("x", "y"))):

            @pl.when(at.c == core)
            def _(core=core, order=order):
                n0, n1 = self.size_of(order[0]), self.size_of(order[1])
                if number == 1:
                    for k in range(1, n0):
                        self.side(order[0], order, k).start()
                elif number == 2:
                    for k in range(1, n0):
                        self.side(order[0], order, k).wait_recv()

                    def add(i, _):
                        d, j = lax.div(i, n1), lax.rem(i, n1)
                        y, x = (at.y, j) if order[0] == "y" else (j, at.x)
                        got = self.r2y if order[0] == "y" else self.r2x
                        value = self.get(d, y, x)
                        for k in range(1, n0):
                            value = value + got[k - 1, d, j]
                        self.put(d, y, x, value)
                        return 0

                    lax.fori_loop(0, at.D * n1, add, 0)
                    for k in range(1, n1):
                        self.side(order[1], order, k).start()
                elif number == 3:
                    for k in range(1, n1):
                        self.side(order[1], order, k).wait_recv()

                    def add(d, _):
                        got = self.r3y if order[1] == "y" else self.r3x
                        value = self.get(d, at.y, at.x)
                        for k in range(1, n1):
                            value = value + got[k - 1, d]
                        self.put(d, at.y, at.x, value)
                        return 0

                    lax.fori_loop(0, at.D, add, 0)
                elif number == 4:
                    for axis in order:
                        for k in range(1, self.size_of(axis)):
                            self.side(axis, order, k).wait_send()

        if number == 3:
            for k in range(1, at.D):
                self.z_copy(k).start()


class Total:
    @staticmethod
    def count(D, F):
        return (D - 1) + (F // 4 - 1) + 1 + 1

    @staticmethod
    def scratch(D, F, rows, cols):
        return [pltpu.VMEM((D + F // 4 + 2 + 2, rows, cols), F32)]

    def __init__(self, at, buf, send, recv):
        self.at, self.buf, self.send, self.recv = at, buf, send, recv
        device = {
            "d": lambda i: (i, at.f),
            "x": lambda i: (at.d, at.fs(at.y, i, at.c)),
            "y": lambda i: (at.d, at.fs(i, at.x, at.c)),
            "c": lambda i: (at.d, at.fs(at.y, at.x, i)),
        }
        self.stages, slot, number = [], 0, 0
        for axis, size, mine in (("d", at.D, at.d), ("x", at.X, at.x), ("y", at.Y, at.y), ("c", 2, at.c)):
            self.stages.append((slot, number, size, mine, device[axis]))
            slot, number = slot + size, number + size - 1

    def copies(self, stage, sent):
        slot, number, size, mine, device = self.stages[stage]
        out = []
        for k in range(1, size):
            other = self.at.up(mine, k if sent else size - k, size)
            block = self.buf.at[slot + (mine if sent else other)]
            out.append(
                pltpu.make_async_remote_copy(
                    src_ref=block,
                    dst_ref=block,
                    send_sem=self.send.at[number + k - 1],
                    recv_sem=self.recv.at[number + k - 1],
                    device_id=device(other),
                    device_id_type=MESH,
                )
            )
        return out

    def put(self, stage, value):
        slot, _, _, mine, _ = self.stages[stage]
        self.buf[slot + mine] = value
        for copy in self.copies(stage, True):
            copy.start()

    def take(self, stage):
        for copy in self.copies(stage, False):
            copy.wait_recv()
        slot, _, size, _, _ = self.stages[stage]
        total = self.buf[slot]
        for i in range(1, size):
            total = total + self.buf[slot + i]
        return total

    def start(self, value):
        self.put(0, value)

    def advance(self, stage):
        self.put(stage + 1, self.take(stage))

    def end(self):
        total = self.take(3)
        for stage in range(4):
            for copy in self.copies(stage, True):
                copy.wait_send()
        return total


LAGS = (0, 2, 4, 6, 8)


def steps_of(arrays, lags=(0, 1, 3, 5, 6)):
    for step in range(len(arrays) + lags[-1]):
        yield [
            (arrays[i], lags.index(step - i))
            for i in reversed(range(len(arrays)))
            if step - i in lags
        ]


def spread(arrays, slots):
    steps = list(steps_of(arrays, LAGS))
    due = {slot: [] for slot in range(slots)}
    for i, step in enumerate(steps):
        due[(i * (slots - 1)) // (len(steps) - 1)] += step
    return due


def columns(ref, part, parts):
    size = ref.shape[-1] // parts
    return ref.at[(slice(None),) * (len(ref.shape) - 1) + (pl.ds(part * size, size),)]


def placed(values, first, width):
    count = values.shape[1]
    row = lax.broadcasted_iota(jnp.int32, (count, width), 0)
    column = lax.broadcasted_iota(jnp.int32, (count, width), 1)
    return nn(values, jnp.where(column == row + first, 1.0, 0.0).astype(BF))


def head_kernel(
    D, F,
    lens, patches, pos_in, vec_in, qkv_in, bias_in, proj_in, fc1_in, fc2_in,
    stats, bias, qs, ks, proj_b, fc1_b, fc2_b, pos_out, qkv_out,
    pos_b, qkv_b, total_buf, s_send, s_recv, send, recv, own,
):
    at = Place(D, F)
    rows, width = patches.shape
    pos_b[...] = jnp.zeros_like(pos_b)
    pos_b[:, :LONG] = pos_in[...].astype(BF)
    lane = lax.broadcasted_iota(jnp.int32, (8, 128), 1)
    spread_out = jnp.where(lane == LONG - (POS_PAD - 128) + lax.broadcasted_iota(jnp.int32, (8, 128), 0), 1.0, 0.0)
    beside = tn(vec_in[...].astype(BF), spread_out.astype(BF))
    pos_b[:, POS_PAD - 128 :] = (pos_b[:, POS_PAD - 128 :].astype(F32) + beside).astype(BF)
    qkv_b[...] = qkv_in[...].astype(BF)
    meet(at.partners())
    pieces = pieces_of((pos_b, qkv_b), (pos_out, qkv_out), HEAD_PARTS)
    arrays = [
        Gather(at, src, out, send.at[i], recv.at[i], own.at[i]) for i, (src, out) in enumerate(pieces)
    ]
    steps = list(steps_of(arrays))
    arrays[0].phase(0)
    arrays[1].phase(0)
    step_rows = 64
    valid_rows = lens[0, 0] + lens[0, 1]

    def accumulate(i, sums):
        block = pl.ds(pl.multiple_of(i * step_rows, step_rows), step_rows)
        row = i * step_rows + lax.broadcasted_iota(jnp.int32, (step_rows, width), 0)
        values = jnp.where(row < valid_rows, patches[block, :].astype(F32), 0.0)
        first = values.reshape(step_rows // 8, 8, -1)
        return (sums[0] + jnp.sum(first, axis=0), sums[1] + jnp.sum(first * first, axis=0))

    empty = jnp.zeros((8, width), F32)
    plain, square = lax.fori_loop(0, rows // step_rows, accumulate, (empty, empty))
    row = lax.broadcasted_iota(jnp.int32, empty.shape, 0)
    plain = jnp.sum(plain, axis=0, keepdims=True)
    square = jnp.sum(square, axis=0, keepdims=True)
    me = at.d * F + at.f
    count = jnp.zeros((1, width), F32) + valid_rows.astype(F32)
    packed = jnp.where(row == 0, plain, jnp.where(row == 1, square, jnp.where(row == 2, count, 0.0)))
    n_bias = bias_in.shape[1]
    hidden = n_bias * D * F
    own_bias = jnp.broadcast_to(bias_in[...].astype(BF), (8, n_bias))
    for i in range(hidden // width):
        packed = jnp.where(row == 4 + i, placed(own_bias, me * n_bias - i * width, width), packed)
    total = Total(at, total_buf, s_send, s_recv)
    total.start(packed)
    for number, step in enumerate(steps):
        for array, phase in step:
            if phase > 0 or array not in arrays[:2]:
                array.phase(phase)
        if number == 1:
            proj_b[...] = proj_in[...].astype(BF)
            fc1_b[...] = fc1_in[...].astype(BF)
            fc2_b[...] = fc2_in[...].astype(BF)
            position = lax.broadcasted_iota(jnp.int32, qs.shape, 0)
            lane = lax.broadcasted_iota(jnp.int32, qs.shape, 1)
            segment = jnp.where(position < lens[0, 0], 0, jnp.where(position < valid_rows, 1, 2))
            same = segment == lane
            qs[...] = jnp.where(same, 1.0, 0.0).astype(BF)
            ks[...] = jnp.where(same, 0.0, jnp.where(lane < 3, -1e30, 0.0)).astype(BF)
        if number in (2, 4, 6):
            total.advance(number // 2 - 1)
        if number == 8:
            summed = total.end()
            inv_count = 1.0 / summed[2:3]
            mean = summed[0:1] * inv_count
            mean = summed[0:1] / summed[2:3]
            var = summed[1:2] / summed[2:3] - mean * mean
            stats[0:1, :] = mean
            stats[1:2, :] = lax.rsqrt(var + INPUT_EPS)
            stats[2:3, :] = inv_count
            stats[3:4, :] = count
            stats[4:5, :] = var
            stats[5:8, :] = jnp.zeros((3, width), F32)
            for i in range(hidden // width):
                bias[0:1, i * width : (i + 1) * width] = summed[4 + i : 5 + i]


def head(D, F, clip_len, patches, pos, vec, w_qkv, bias, w_proj, w_fc1, w_fc2, collective_id):
    X, Y = F // 4, 2
    rows, width = patches.shape
    hidden = bias.shape[0] * D * F
    count = sum(HEAD_PARTS)
    n = Gather.count(D, X, Y)
    hbm = pl.BlockSpec(memory_space=pl.ANY)
    vmem = pl.BlockSpec(memory_space=pltpu.VMEM)
    own_rows = pos.shape[0]
    sent = [(own_rows, POS_PAD), w_qkv.shape]
    return pl.pallas_call(
        partial(head_kernel, D, F),
        name="head",
        out_shape=[
            jax.ShapeDtypeStruct((8, width), F32),
            jax.ShapeDtypeStruct((1, hidden), F32),
            jax.ShapeDtypeStruct((rows, 128), BF),
            jax.ShapeDtypeStruct((rows, 128), BF),
        ]
        + [jax.ShapeDtypeStruct(w.shape, BF) for w in (w_proj, w_fc1, w_fc2)]
        + [jax.ShapeDtypeStruct((D, Y, X, 2) + shape, BF) for shape in sent],
        in_specs=[pl.BlockSpec(memory_space=pltpu.SMEM)] + [vmem] * 8,
        out_specs=[vmem] * 7 + [hbm] * 2,
        scratch_shapes=[pltpu.VMEM(shape, BF) for shape in sent]
        + Total.scratch(D, F, 8, width)
        + [pltpu.SemaphoreType.DMA((Total.count(D, F),)), pltpu.SemaphoreType.DMA((Total.count(D, F),))]
        + copy_semaphores(count, n),
        compiler_params=pltpu.CompilerParams(
            collective_id=collective_id, has_side_effects=True, vmem_limit_bytes=VMEM_LIMIT
        ),
        cost_estimate=pl.CostEstimate(flops=0, bytes_accessed=20 * 2**20, transcendentals=0),
    )(clip_len, patches, pos, vec.T, w_qkv, bias.reshape(1, -1), w_proj, w_fc1, w_fc2)


def pieces_of(grads, totals, parts):
    return [
        (columns(g, j, n), columns(t, j, n)) for g, t, n in zip(grads, totals, parts) for j in range(n)
    ]


def scatter_arrays(at, pieces, bufs, send, recv, own):
    per = len(bufs) // len(pieces)
    return [
        Scatter(at, grad, total, bufs[i * per : (i + 1) * per], send.at[i], recv.at[i], own.at[i])
        for i, (grad, total) in enumerate(pieces)
    ]


def blocks_shape(D, X, Y, rows, N):
    return (D, Y, X, 2, rows // (D * X * Y * 2), N)


def scatter_scratch(D, X, Y, grads, parts):
    out = []
    for g, n in zip(grads, parts):
        for _ in range(n):
            out += Scatter.scratch(D, X, Y, g.shape[-2], g.shape[-1] // n)
    return out


def copy_semaphores(count, n):
    return [
        pltpu.SemaphoreType.DMA((count, n)),
        pltpu.SemaphoreType.DMA((count, n)),
        pltpu.SemaphoreType.DMA((count,)),
    ]


def row_of(first, rows, width):
    return first + lax.broadcasted_iota(jnp.int32, (rows, width), 0)


def attend_pair(q_ref, k_ref, v_ref, qs_ref, ks_ref, q_block):
    rows = q_ref.shape[0]
    lane = lax.broadcasted_iota(jnp.int32, (q_block, 128), 1)

    def half(values, head):
        keep = lane < 64 if head == 0 else lane >= 64
        return jnp.where(keep, values, jnp.zeros_like(values))

    def query(block, head):
        scaled = q_ref[block, :] * jnp.asarray(0.125, BF)
        return jnp.concatenate([half(scaled, head), qs_ref[block, :]], axis=1)

    keys = jnp.concatenate([k_ref[...], ks_ref[...]], axis=1)
    return keys, query, half


def forward_kernel(
    D, F,
    lens, patches, stats, sel_long, sel_short, pos, w_ref, qs_ref, ks_ref, proj_ref, fc1_ref, fc2_ref,
    emb_out, norm_out, qkv_out, out_ref, lse_ref, vec, proj_out, fc1_out, fc2_out,
    qkv_buf, q_ref, k_ref, key_buf, v_buf, o_buf, send, recv, own,
):
    step = pl.program_id(0)
    part_rows, width = patches.shape
    rows = qkv_buf.shape[0]
    parts = rows // part_rows
    pairs = HEADS // 2
    q_block = 256
    blocks = rows // q_block
    at = Place(D, F)

    @pl.when(step == 0)
    def _():
        meet(at.partners())
        ahead = LONG - (POS_PAD - 128)
        vec[...] = jnp.transpose(pos[:, POS_PAD - 128 :].astype(F32))[ahead : ahead + 8]

    pieces = pieces_of((proj_ref, fc1_ref, fc2_ref), (proj_out, fc1_out, fc2_out), FORWARD_PARTS)
    arrays = [
        Gather(at, src, out, send.at[i], recv.at[i], own.at[i]) for i, (src, out) in enumerate(pieces)
    ]
    due = spread(arrays, parts + 2 * pairs + 1)

    @pl.when(step < parts)
    def _():
        run_due({k: due[k] for k in range(parts)}, step, parts, 0, 1)
        mean, inv_std = stats[0:1, :], stats[1:2, :]
        normed = (patches[...].astype(F32) - mean) * inv_std
        row = lax.broadcasted_iota(jnp.int32, (part_rows, width), 0).astype(F32)
        first_row = (step * part_rows).astype(F32)
        sel = jnp.where(lens[0, 1] > 0, sel_short[0], sel_long[0])
        embedded = jnp.where(row + first_row < stats[3:4, :], normed + nt(sel, pos[...]), 0.0)
        emb_out[...] = embedded
        n, _rho = norm_parts(embedded)
        first = (n * vec[0:1, :] + vec[1:2, :]).astype(BF)
        norm_out[...] = jnp.transpose(first)
        bias = jnp.concatenate([vec[2:3, :], jnp.zeros((1, width), F32), vec[3:4, :]], axis=1)
        projected = (nn(first, w_ref[...]) + bias).astype(BF)
        qkv_out[...] = projected
        qkv_buf[pl.ds(pl.multiple_of(step * part_rows, part_rows), part_rows), :] = projected

    @pl.when(step >= parts)
    def _():
        pair = step - parts
        slots = {k: due[k + parts] for k in range(2 * pairs + 1)}

        def columns_of(i):
            return qkv_buf[:, pl.ds(pl.multiple_of(i * width + pair * 128, 128), 128)]

        q_ref[...] = columns_of(0)
        k_ref[...] = columns_of(1)
        keys, query, _ = attend_pair(q_ref, k_ref, None, qs_ref, ks_ref, q_block)
        key_buf[...] = keys
        v_t = jnp.transpose(columns_of(2))
        ones = jnp.ones((16, rows), BF)
        for head in range(2):
            v_buf[head] = jnp.concatenate([v_t[64 * head : 64 * head + 64], ones], axis=0)
        for i in range(blocks):
            if i in (0, 3):
                run_due(slots, pair, pairs, i // 3, 2)
            block = pl.ds(i * q_block, q_block)
            for head in range(2):
                scores = nt(key_buf[...], query(block, head))
                top = jnp.max(scores, axis=0, keepdims=True)
                probs = jnp.exp(scores - top).astype(BF)
                out = nn(v_buf[head], probs)
                total = out[64:65, :]
                o_buf[64 * head : 64 * head + 64, block] = (out[:64] / total).astype(BF)
                lse_ref[0, head : head + 1, block] = top + jnp.log(total)
        out_ref[...] = jnp.transpose(o_buf[...])
        run_due(slots, pair, pairs, 2, 2)


def run_due(due, step, steps, point, points):
    for k in range(steps):
        work = due.get(k * points + point, [])
        if k < steps - 1 and point >= points:
            continue
        if work:

            @pl.when(step == k)
            def _(work=work):
                for array, number in work:
                    array.phase(number)


def timed(arrays, starts, lags, slots):
    due = {slot: [] for slot in range(slots)}
    for array, start, own_lags in reversed(list(zip(arrays, starts, lags))):
        for number, lag in enumerate(own_lags):
            due[min(start + lag, slots - 1)].append((array, number))
    for work in due.values():
        work.sort(key=lambda item: item[1])
    return due


def pair_specs(rows):
    pair = lambda first: pl.BlockSpec((rows, 128), lambda p: (0, first + p))
    whole = pl.BlockSpec((rows, 128), lambda p: (0, 0))
    return pair, whole


def forward(D, F, clip_len, patches, stats, table, pos, w_qkv, q_seg, k_seg, shards, collective_id):
    rows, width = patches.shape
    pairs = HEADS // 2
    part = 256
    parts = rows // part
    hbm = pl.BlockSpec(memory_space=pl.ANY)
    once = lambda a: pl.BlockSpec(a.shape, lambda p: (0,) * a.ndim, pipeline_mode=pl.Buffered(1))
    by_row = lambda n: pl.BlockSpec((part, n), lambda p: (jnp.minimum(p, parts - 1), 0))
    X, Y = F // 4, 2
    n = Gather.count(D, X, Y)
    return pl.pallas_call(
        partial(forward_kernel, D, F),
        name="forward",
        grid=(parts + pairs,),
        in_specs=[
            pl.BlockSpec(memory_space=pltpu.SMEM),
            by_row(width),
            once(stats),
            pl.BlockSpec((1, part, POS_PAD), lambda p: (0, jnp.minimum(p, parts - 1), 0)),
            pl.BlockSpec((1, part, POS_PAD), lambda p: (1, jnp.minimum(p, parts - 1), 0)),
        ]
        + [once(a) for a in (pos, w_qkv, q_seg, k_seg)]
        + [hbm] * 3,
        out_specs=[
            by_row(width),
            pl.BlockSpec((width, part), lambda p: (0, jnp.minimum(p, parts - 1))),
            by_row(3 * width),
            pl.BlockSpec((rows, 128), lambda p: (0, jnp.maximum(p - parts, 0))),
            pl.BlockSpec((1, 8, rows), lambda p: (jnp.maximum(p - parts, 0), 0, 0)),
            pl.BlockSpec((8, width), lambda p: (0, 0)),
        ]
        + [hbm] * 3,
        out_shape=[
            jax.ShapeDtypeStruct((rows, width), F32),
            jax.ShapeDtypeStruct((width, rows), BF),
            jax.ShapeDtypeStruct((rows, 3 * width), BF),
            jax.ShapeDtypeStruct((rows, 128 * pairs), BF),
            jax.ShapeDtypeStruct((pairs, 8, rows), F32),
            jax.ShapeDtypeStruct((8, width), F32),
        ]
        + [jax.ShapeDtypeStruct((D, Y, X, 2) + s.shape, s.dtype) for s in shards],
        scratch_shapes=[
            pltpu.VMEM((rows, 3 * width), BF),
            pltpu.VMEM((rows, 128), BF),
            pltpu.VMEM((rows, 128), BF),
            pltpu.VMEM((rows, 256), BF),
            pltpu.VMEM((2, 80, rows), BF),
            pltpu.VMEM((128, rows), BF),
        ]
        + copy_semaphores(sum(FORWARD_PARTS), n),
        compiler_params=pltpu.CompilerParams(
            collective_id=collective_id, has_side_effects=True, vmem_limit_bytes=VMEM_LIMIT
        ),
        cost_estimate=pl.CostEstimate(
            flops=4 * 12 * rows * rows * 256 + 2 * rows * width * (3 * width + POS_PAD),
            bytes_accessed=40 * 2**20,
            transcendentals=12 * rows * rows,
        ),
    )(clip_len, patches, stats, table, table, pos, w_qkv, q_seg, k_seg, *shards)


class PairScatter(Scatter):
    def __init__(self, first_pair, *rest):
        super().__init__(*rest)
        self.first_pair = first_pair

    def store(self, total):
        width = self.total.shape[-1] // 3
        for k in range(total.shape[1] // 384):
            for i in range(3):
                first = i * width + 128 * (self.first_pair + k)
                source = 384 * k + 128 * i
                self.total[:, first : first + 128] = total[:, source : source + 128]


def backward_pair(
    D, F,
    q_ref, k_ref, v_ref, do_ref, qs_ref, ks_ref, lse_ref, delta_ref, first_t, g_fc2, g_proj, g_fc1, *refs,
):
    dq_ref, dk_ref, dv_ref, g_last, t_fc2, t_proj, t_fc1, t_qkv = refs[:8]
    key_buf, kt_buf, dk_acc, dv_acc, dqt_buf, wide = refs[8:14]
    pairs = HEADS // 2
    groups = EARLY_PAIRS // PAIR_GROUP
    held, rest = refs[14 : 14 + groups], refs[14 + groups : -3]
    send, recv, own = refs[-3:]
    pair = pl.program_id(0)
    rows = q_ref.shape[0]
    q_block = 256
    blocks = rows // q_block
    at = Place(D, F)

    @pl.when(pair == 0)
    def _():
        meet(at.partners())

    pieces = pieces_of((g_fc2, g_proj, g_fc1), (t_fc2, t_proj, t_fc1), BACKWARD_PARTS)
    early = sum(BACKWARD_PARTS)
    per_held = 4 if at.X == at.Y else 6
    split = len(rest) - per_held * groups
    arrays = scatter_arrays(at, pieces, rest[:split], send, recv, own)
    for p in range(groups):
        bufs = rest[split + p * per_held : split + (p + 1) * per_held]
        i = early + p
        arrays.append(
            PairScatter(
                p * PAIR_GROUP, at, held[p], t_qkv, bufs, send.at[i], recv.at[i], own.at[i]
            )
        )
    starts = list(range(early)) + [2 * PAIR_GROUP * (p + 1) for p in range(groups)]
    due = timed(arrays, starts, BACKWARD_LAGS, 2 * pairs + 1)
    keys, query, half = attend_pair(q_ref, k_ref, v_ref, qs_ref, ks_ref, q_block)
    key_buf[...] = keys
    kt_buf[...] = jnp.transpose(k_ref[...])
    for i in range(blocks):
        if i in (0, 3):
            run_due(due, pair, pairs, i // 3, 2)
        block = pl.ds(i * q_block, q_block)
        for head in range(2):
            q_ext = query(block, head)
            d_out = half(do_ref[block, :], head)
            scores = nt(key_buf[...], q_ext)
            probs = jnp.exp(scores - lse_ref[0, head : head + 1, block])
            d_probs = nt(v_ref[...], d_out)
            d_scores = (probs * (d_probs - delta_ref[0, head : head + 1, block])).astype(BF)
            dv = nn(probs.astype(BF), d_out)
            dk = nn(d_scores, q_ext[:, :128])
            if i == 0 and head == 0:
                dv_acc[...] = dv
                dk_acc[...] = dk
            else:
                dv_acc[...] += dv
                dk_acc[...] += dk
            dq = nn(kt_buf[64 * head : 64 * head + 64, :], d_scores)
            dqt_buf[64 * head : 64 * head + 64, block] = (dq * 0.125).astype(BF)
    dq_ref[...] = jnp.transpose(dqt_buf[...])
    dk_ref[...] = dk_acc[...].astype(BF)
    dv_ref[...] = dv_acc[...].astype(BF)
    joined = jnp.concatenate([dq_ref[...], dk_ref[...], dv_ref[...]], axis=1)
    wide[...] = nn(first_t[...], joined)
    for p in range(EARLY_PAIRS):

        @pl.when(pair == p)
        def _(p=p):
            arrays[early + p // PAIR_GROUP].fill(wide, 384 * (p % PAIR_GROUP))

    @pl.when(pair >= EARLY_PAIRS)
    def _():
        g_last[...] = wide[...].astype(BF)

    run_due(due, pair, pairs, 2, 2)


def attend_backward(D, F, qkv, grad_attended, q_seg, k_seg, lse, delta, first_t, grads, collective_id):
    rows = qkv.shape[0]
    width = first_t.shape[0]
    pairs = HEADS // 2
    pair, whole = pair_specs(rows)
    line = pl.BlockSpec((1, 8, rows), lambda p: (p, 0, 0))
    hbm = pl.BlockSpec(memory_space=pl.ANY)
    once = lambda shape: pl.BlockSpec(shape, lambda p: (0,) * len(shape), pipeline_mode=pl.Buffered(1))
    X, Y = F // 4, 2
    n = Scatter.count(D, X, Y)
    own_rows = width // (D * F)
    groups = EARLY_PAIRS // PAIR_GROUP
    held = [pltpu.VMEM(blocks_shape(D, X, Y, width, 384 * PAIR_GROUP), BF)] * groups
    held_scratch = Scatter.scratch(D, X, Y, own_rows, 384 * PAIR_GROUP, held=True) * groups
    totals = [jax.ShapeDtypeStruct(g.shape[-2:], F32) for g in grads]
    totals.append(jax.ShapeDtypeStruct((own_rows, 3 * width), F32))
    return pl.pallas_call(
        partial(backward_pair, D, F),
        name="attend_backward",
        grid=(pairs,),
        in_specs=[pair(0), pair(pairs), pair(2 * pairs), pair(0), whole, whole, line, line]
        + [once(first_t.shape)]
        + [hbm] * 3,
        out_specs=[pair(0)] * 3
        + [pl.BlockSpec((width, 384), lambda p: (0, jnp.maximum(p - EARLY_PAIRS, 0)))]
        + [once(t.shape) for t in totals],
        out_shape=[jax.ShapeDtypeStruct((rows, 128 * pairs), BF)] * 3
        + [jax.ShapeDtypeStruct((width, 384 * (pairs - EARLY_PAIRS)), BF)]
        + totals,
        scratch_shapes=[
            pltpu.VMEM((rows, 256), BF),
            pltpu.VMEM((128, rows), BF),
            pltpu.VMEM((rows, 128), F32),
            pltpu.VMEM((rows, 128), F32),
            pltpu.VMEM((128, rows), BF),
            pltpu.VMEM((width, 384), F32),
        ]
        + held
        + scatter_scratch(D, X, Y, grads, BACKWARD_PARTS)
        + held_scratch
        + copy_semaphores(sum(BACKWARD_PARTS) + groups, n),
        compiler_params=pltpu.CompilerParams(
            collective_id=collective_id, has_side_effects=True, vmem_limit_bytes=VMEM_LIMIT
        ),
        cost_estimate=pl.CostEstimate(
            flops=10 * 12 * rows * rows * 256,
            bytes_accessed=14 * rows * 768,
            transcendentals=12 * rows * rows,
        ),
    )(qkv, qkv, qkv, grad_attended, q_seg, k_seg, lse, delta, first_t, *grads)


def gelu_both(u):
    z = jnp.abs(u)
    falling = jnp.exp(-0.5 * u * u)
    t = 1.0 / (1.0 + TAIL_P * z)
    poly = TAIL_C[-1]
    for coefficient in TAIL_C[-2::-1]:
        poly = poly * t + coefficient
    tail = poly * t * falling
    upper = jnp.where(u >= 0, 1.0 - tail, tail)
    return u * upper, upper + u * falling * 0.3989422804014327


def norm_parts(values):
    center = values - jnp.mean(values, axis=1, keepdims=True)
    spread = jnp.mean(center * center, axis=1, keepdims=True)
    rho = lax.rsqrt(spread + NORM_EPS)
    return center * rho, rho


def norm_back(n, rho, grad, gain):
    q = grad * gain
    return rho * (q - jnp.mean(q, axis=1, keepdims=True) - n * jnp.mean(q * n, axis=1, keepdims=True))


def fold(values):
    return jnp.sum(values.reshape(-1, 8, values.shape[1]), axis=0)


def middle_kernel(
    D, F, tiles,
    stats, emb, att, cot, wo, w1, b1, w2, vec, pick,
    layer_out, res_grad, att_grad, delta_out, g_proj, g_fc1, g_b1, g_fc2, g_small, t_fc1,
    residual, second, second_t, mlp, g_second, act_buf, pre_buf, wide, *rest,
):
    step = pl.program_id(0)
    rows, width = emb.shape
    tile = w1.shape[1]
    block_rows = 256
    blocks = rows // block_rows
    ones = jnp.ones((8, block_rows), BF)
    masked, branch = layer_out, second
    at = Place(D, F)
    held, bufs, (send, recv, own) = rest[:EARLY_TILES], rest[EARLY_TILES:-3], rest[-3:]
    per = len(bufs) // EARLY_TILES
    arrays = [
        Scatter(
            at, held[j], t_fc1.at[:, pl.ds(j * tile, tile)], bufs[j * per : (j + 1) * per],
            send.at[j], recv.at[j], own.at[j],
        )
        for j in range(EARLY_TILES)
    ]
    due = timed(arrays, [2 * j + 2 for j in range(EARLY_TILES)], MIDDLE_LAGS, 2 * tiles + 2)

    def take(i):
        return pl.ds(pl.multiple_of(i * block_rows, block_rows), block_rows)

    def flags(i):
        row = lax.broadcasted_iota(jnp.int32, (block_rows, width), 0).astype(F32)
        return row + jnp.asarray(i * block_rows, jnp.int32).astype(F32) < stats[3:4, :]

    @pl.when(step == 0)
    def _():
        meet(at.partners())

        def one(i, _):
            block = take(i)
            branch_out = nn(att[block, :], wo[...]) + vec[4:5, :]
            res = emb[block, :] + branch_out
            residual[block, :] = res
            n, _rho = norm_parts(res)
            sn = (n * vec[5:6, :] + vec[6:7, :]).astype(BF)
            second[block, :] = sn
            second_t[i] = jnp.transpose(sn)
            masked[block, :] = jnp.where(flags(i), cot[block, :].astype(F32), 0.0).astype(BF)
            mlp[block, :] = jnp.zeros((block_rows, width), F32)
            g_second[block, :] = jnp.zeros((block_rows, width), F32)
            return 0

        lax.fori_loop(0, blocks, one, 0)

    bias = b1[...]
    for i in range(blocks):
        if i in (0, 3):
            run_due(due, step, tiles, i // 3, 2)
        block = pl.ds(i * block_rows, block_rows)
        pre = nn(second[block, :], w1[...]) + bias
        act, slope = gelu_both(pre)
        act = act.astype(BF)
        act_buf[block, :] = act
        grad_act = nt(masked[block, :], w2[...]).astype(BF).astype(F32)
        grad_pre = (grad_act * slope).astype(BF)
        pre_buf[block, :] = grad_pre
        mlp[block, :] += nn(act, w2[...])
        g_second[block, :] += nt(grad_pre, w1[...])
    g_fc2[...] = tn(act_buf[...], masked[...]).astype(BF)
    for i in range(blocks):
        block = pl.ds(i * block_rows, block_rows)
        part = nn(second_t[i], pre_buf[block, :])
        line = nn(ones, pre_buf[block, :])
        total = part if i == 0 else total + part
        lines = line if i == 0 else lines + line
    wide[...] = total
    g_b1[...] = lines
    for j in range(EARLY_TILES):

        @pl.when(step == j)
        def _(j=j):
            arrays[j].fill(wide)

    @pl.when(step >= EARLY_TILES)
    def _():
        g_fc1[...] = wide[...].astype(BF)

    run_due(due, step, tiles, 2, 2)

    @pl.when(step == tiles - 1)
    def _():
        def one(i, sums):
            block = take(i)
            res = residual[block, :]
            n, rho = norm_parts(res)
            out_grad = masked[block, :]
            layer_out[block, :] = jnp.where(flags(i), res + mlp[block, :] + vec[7:8, :], 0.0).astype(BF)
            grad = g_second[block, :].astype(BF).astype(F32)
            back = norm_back(n, rho, grad, vec[5:6, :])
            total = out_grad.astype(F32) + back
            res_grad[block, :] = total
            low = total.astype(BF)
            branch[block, :] = low
            into = nt(low, wo[...]).astype(BF)
            att_grad[block, :] = into
            product = into.astype(F32) * att[block, :].astype(F32)
            high = product.astype(BF)
            rest = (product - high.astype(F32)).astype(BF)
            delta = nn(high, pick[...]) + nn(rest, pick[...])
            lines = jnp.transpose(delta)
            for p in range(HEADS // 2):
                delta_out[p, 0:2, block] = lines[2 * p : 2 * p + 2, :]
            return (
                sums[0] + nn(ones, low)[0:8],
                sums[1] + fold(grad * n),
                sums[2] + fold(grad),
                sums[3] + nn(ones, out_grad)[0:8],
            )

        empty = jnp.zeros((8, width), F32)
        sums = lax.fori_loop(0, blocks, one, (empty,) * 4)
        g_proj[...] = tn(att[...], branch[...]).astype(BF)
        g_small[0:1, :] = sums[0][0:1]
        g_small[1:2, :] = jnp.sum(sums[1], axis=0, keepdims=True)
        g_small[2:3, :] = jnp.sum(sums[2], axis=0, keepdims=True)
        g_small[3:4, :] = sums[3][0:1]
        g_small[4:8, :] = jnp.zeros((4, width), F32)

    run_due(due, step, tiles, 3, 2)


def middle(D, F, stats, emb, att, cot, wo, w1, b1, w2, vec, collective_id):
    rows, width = emb.shape
    hidden = w1.shape[1]
    tile = 512
    tiles = hidden // tile
    X, Y = F // 4, 2
    own_rows = width // (D * F)
    once = pl.Buffered(1)
    whole = lambda shape: pl.BlockSpec(shape, lambda j: (0,) * len(shape), pipeline_mode=once)
    pick = np.zeros((width, 128), np.float32)
    pick[np.arange(width), np.arange(width) // 64] = 1.0
    pick = jnp.asarray(pick.astype(ml_dtypes.bfloat16))
    out_shape = [
        jax.ShapeDtypeStruct((rows, width), BF),
        jax.ShapeDtypeStruct((rows, width), F32),
        jax.ShapeDtypeStruct((rows, width), BF),
        jax.ShapeDtypeStruct((HEADS // 2, 8, rows), F32),
        jax.ShapeDtypeStruct((width, width), BF),
        jax.ShapeDtypeStruct((width, tile * (tiles - EARLY_TILES)), BF),
        jax.ShapeDtypeStruct((8, hidden), F32),
        jax.ShapeDtypeStruct((hidden, width), BF),
        jax.ShapeDtypeStruct((8, width), F32),
        jax.ShapeDtypeStruct((own_rows, tile * EARLY_TILES), F32),
    ]
    scatter = []
    for _ in range(EARLY_TILES):
        scatter += Scatter.scratch(D, X, Y, own_rows, tile, held=True)
    return pl.pallas_call(
        partial(middle_kernel, D, F, tiles),
        name="middle",
        grid=(tiles,),
        in_specs=[
            whole(stats.shape),
            whole((rows, width)),
            whole((rows, width)),
            whole((rows, width)),
            whole((width, width)),
            pl.BlockSpec((width, tile), lambda j: (0, j)),
            pl.BlockSpec((1, tile), lambda j: (0, j)),
            pl.BlockSpec((tile, width), lambda j: (j, 0)),
            whole((8, width)),
            whole((width, 128)),
        ],
        out_specs=[whole(s.shape) for s in out_shape[:5]]
        + [
            pl.BlockSpec((width, tile), lambda j: (0, jnp.maximum(j - EARLY_TILES, 0))),
            pl.BlockSpec((8, tile), lambda j: (0, j)),
            pl.BlockSpec((tile, width), lambda j: (j, 0)),
            whole((8, width)),
            whole(out_shape[9].shape),
        ],
        scratch_shapes=[
            pltpu.VMEM((rows, width), F32),
            pltpu.VMEM((rows, width), BF),
            pltpu.VMEM((rows // 256, width, 256), BF),
            pltpu.VMEM((rows, width), F32),
            pltpu.VMEM((rows, width), F32),
            pltpu.VMEM((rows, tile), BF),
            pltpu.VMEM((rows, tile), BF),
            pltpu.VMEM((width, tile), F32),
        ]
        + [pltpu.VMEM(blocks_shape(D, X, Y, width, tile), BF)] * EARLY_TILES
        + scatter
        + copy_semaphores(EARLY_TILES, Scatter.count(D, X, Y)),
        out_shape=out_shape,
        compiler_params=pltpu.CompilerParams(
            collective_id=collective_id, has_side_effects=True, vmem_limit_bytes=VMEM_LIMIT
        ),
        cost_estimate=pl.CostEstimate(
            flops=2 * rows * width * (6 * hidden + 3 * width),
            bytes_accessed=40 * 2**20,
            transcendentals=rows * hidden,
        ),
    )(stats, emb, att, cot, wo, w1, b1, w2, vec, pick)


def last_kernel(
    D, F,
    lens, gq, gk, gv, emb, res_grad, patches, stats, sel_long, sel_short, w_ref, vec, small_in, bias_in, g_last,
    patch_grad, small_out, t_last, t_pos,
    pos_acc, masked, normed_buf, sums, pos_a, pos_b, total_buf, s_send, s_recv, *rest,
):
    step = pl.program_id(0)
    rows, width = emb.shape
    total_rows = patch_grad.shape[0]
    steps = total_rows // rows
    ones = jnp.ones((8, rows), BF)
    at = Place(D, F)
    bufs, (send, recv, own) = rest[:-3], rest[-3:]
    per_held = 4 if at.X == at.Y else 6
    early = Scatter(at, g_last, t_last, bufs[: per_held + 1], send.at[0], recv.at[0], own.at[0])
    pos_blocks = (pos_a, pos_b)
    half = POS_PAD // 2
    pos = [
        Scatter(
            at, pos_blocks[i], t_pos.at[:, pl.ds(half * i, half)],
            bufs[per_held + 1 + per_held * i : per_held + 1 + per_held * (i + 1)],
            send.at[1 + i], recv.at[1 + i], own.at[1 + i],
        )
        for i in range(2)
    ]
    total = Total(at, total_buf, s_send, s_recv)

    @pl.when(step == 0)
    def _():
        meet(at.partners())
        early.phase(0)
        sums[...] = jnp.zeros_like(sums)

    for number in range(1, 5):

        @pl.when(step == number)
        def _(number=number):
            early.phase(number)

    parts = [gq[...], gk[...], gv[...]]
    for i, part in enumerate(parts):
        into = nt(part, w_ref[:, i * width : (i + 1) * width])
        grad = into if i == 0 else grad + into
    grad = grad.astype(BF).astype(F32)
    n, rho = norm_parts(emb[...])
    row = lax.broadcasted_iota(jnp.int32, (rows, width), 0).astype(F32) + (step * rows).astype(F32)
    valid = row < stats[3:4, :]
    whole = jnp.where(valid, res_grad[...] + norm_back(n, rho, grad, vec[0:1, :]), 0.0)
    block = pl.ds(pl.multiple_of(step * rows, rows), rows)
    masked[block, :] = whole
    sel = jnp.where(lens[0, 1] > 0, sel_short[0], sel_long[0])
    moved = tn(whole.astype(BF), sel)

    @pl.when(step == 0)
    def _():
        pos_acc[...] = moved

    @pl.when(step > 0)
    def _():
        pos_acc[...] += moved

    normed = (patches[...].astype(F32) - stats[0:1, :]) * stats[1:2, :]
    normed_buf[block, :] = jnp.where(valid, normed, 0.0)
    sums[0] += fold(grad * n)
    sums[1] += fold(grad)
    sums[2] += nn(ones, parts[0])
    sums[3] += nn(ones, parts[2])
    sums[4] += fold(whole)
    sums[5] += fold(whole * normed)

    @pl.when(step == steps - 1)
    def _():
        lines = []
        for i in range(6):
            line = sums[i]
            lines.append(line[0:1] if i in (2, 3) else jnp.sum(line, axis=0, keepdims=True))
        hidden = bias_in.shape[1]
        own_lines = lines[4:] + [bias_in[0:1, i * width : (i + 1) * width] for i in range(hidden // width)]
        own_lines += [jnp.zeros((1, width), F32)] * (8 - len(own_lines))
        total.start(jnp.concatenate(own_lines, axis=0))
        own_vec = lines[:4] + [small_in[i : i + 1, :] for i in range(4)]
        ahead = LONG - (POS_PAD - 128)
        own_vec = [jnp.zeros((ahead, width), F32)] + own_vec + [jnp.zeros((128 - ahead - 8, width), F32)]
        pos_acc[:, POS_PAD - 128 :] += jnp.transpose(jnp.concatenate(own_vec, axis=0))
        pos[0].fill(pos_acc.at[:, :half])
        pos[0].phase(0)
        pos[1].fill(pos_acc.at[:, half:])
        pos[1].phase(0)
        pos[0].phase(1)
        pos[1].phase(1)
        total.advance(0)
        pos[0].phase(2)
        pos[1].phase(2)
        total.advance(1)
        pos[0].phase(3)
        pos[1].phase(3)
        total.advance(2)
        summed = total.end()
        small_out[...] = summed
        inv_std, inv_count = stats[1:2, :], stats[2:3, :]
        plain, scaled = summed[0:1] * inv_count, summed[1:2] * inv_count

        def one(i, _):
            part = pl.ds(pl.multiple_of(i * 64, 64), 64)
            valid = flag_buf(i)
            value = masked[part, :] - valid * plain - normed_buf[part, :] * scaled
            patch_grad[part, :] = (inv_std * value).astype(BF)
            return 0

        valid_rows = stats[3:4, :]

        def flag_buf(i):
            row = lax.broadcasted_iota(jnp.int32, (64, width), 0).astype(F32)
            return jnp.where(row + (i * 64).astype(F32) < valid_rows, 1.0, 0.0)

        lax.fori_loop(0, total_rows // 64, one, 0)
        pos[0].phase(4)
        pos[1].phase(4)


def last_back(D, F, clip_len, gq, gk, gv, emb, res_grad, patches, stats, table, w_qkv, vec, small, bias, g_last, collective_id):
    rows, width = emb.shape
    block = 256
    once = pl.Buffered(1)
    whole = lambda shape: pl.BlockSpec(shape, lambda i: (0,) * len(shape), pipeline_mode=once)
    by_row = lambda n: pl.BlockSpec((block, n), lambda i: (i, 0))
    X, Y = F // 4, 2
    own_rows = width // (D * F)
    n = Scatter.count(D, X, Y)
    out_shape = [
        jax.ShapeDtypeStruct((rows, width), BF),
        jax.ShapeDtypeStruct((8, width), F32),
        jax.ShapeDtypeStruct((own_rows, g_last.shape[-1]), F32),
        jax.ShapeDtypeStruct((own_rows, POS_PAD), F32),
    ]
    return pl.pallas_call(
        partial(last_kernel, D, F),
        name="last_back",
        grid=(rows // block,),
        in_specs=[pl.BlockSpec(memory_space=pltpu.SMEM)]
        + [by_row(width)] * 6
        + [
            whole(stats.shape),
            pl.BlockSpec((1, block, POS_PAD), lambda i: (0, i, 0)),
            pl.BlockSpec((1, block, POS_PAD), lambda i: (1, i, 0)),
            whole(w_qkv.shape),
            whole(vec.shape),
        ]
        + [whole(small.shape), whole(bias.shape), pl.BlockSpec(memory_space=pl.ANY)],
        out_specs=[whole(o.shape) for o in out_shape],
        out_shape=out_shape,
        scratch_shapes=[
            pltpu.VMEM((width, POS_PAD), F32),
            pltpu.VMEM((rows, width), F32),
            pltpu.VMEM((rows, width), F32),
            pltpu.VMEM((6, 8, width), F32),
            pltpu.VMEM(blocks_shape(D, X, Y, width, POS_PAD // 2), BF),
            pltpu.VMEM(blocks_shape(D, X, Y, width, POS_PAD // 2), BF),
        ]
        + Total.scratch(D, F, 8, width)
        + [pltpu.SemaphoreType.DMA((Total.count(D, F),)), pltpu.SemaphoreType.DMA((Total.count(D, F),))]
        + Scatter.scratch(D, X, Y, own_rows, g_last.shape[-1])
        + Scatter.scratch(D, X, Y, own_rows, POS_PAD // 2, held=True) * 2
        + copy_semaphores(3, n),
        compiler_params=pltpu.CompilerParams(
            collective_id=collective_id, has_side_effects=True, vmem_limit_bytes=VMEM_LIMIT
        ),
        cost_estimate=pl.CostEstimate(
            flops=2 * rows * width * (6 * width + POS_PAD),
            bytes_accessed=30 * 2**20,
            transcendentals=0,
        ),
    )(clip_len, gq, gk, gv, emb, res_grad, patches, stats, table, table, w_qkv, vec, small, bias, g_last)


def average_keep():
    return min(0.99, (1.0 + PRIOR_STEPS) / (10.0 + PRIOR_STEPS))


def stepped(rate, g, w, m, e):
    keep = average_keep()
    moved = MOMENTUM * m + g
    update = -(rate * (g + MOMENTUM * moved))
    return g, update, moved, keep * e + (1.0 - keep) * (w + update)


def optimizer_kernel(rate, t_pos, t_early, t_late, t_proj, t_most, t_last, t_fc2, *refs):
    states, outs = refs[:18], refs[18:]
    names = 6

    def write(i, where, g):
        w, m, e = (states[3 * i + j][where] for j in range(3))
        for out, value in zip(outs[4 * i : 4 * i + 4], stepped(rate, g, w, m, e)):
            out[where] = value

    everything = (slice(None), slice(None))
    write(0, everything, t_pos[:, :LONG])
    ahead = LONG - (POS_PAD - 128)
    write(1, everything, jnp.transpose(t_pos[:, POS_PAD - 128 :])[ahead : ahead + 8])
    width = t_early.shape[1] // 3
    early = 128 * EARLY_PAIRS
    for i in range(3):
        first = i * width
        write(2, (slice(None), slice(first, first + early)), t_early[:, first : first + early])
        for k in range(HEADS // 2 - EARLY_PAIRS):
            to = first + early + 128 * k
            source = 384 * k + 128 * i
            write(2, (slice(None), slice(to, to + 128)), t_late[:, source : source + 128])
    write(3, everything, t_proj[...])
    most = t_most.shape[1]
    write(4, (slice(None), slice(0, most)), t_most[...])
    write(4, (slice(None), slice(most, most + t_last.shape[1])), t_last[...])
    write(5, everything, t_fc2[...])


def optimize(rate, totals, states):
    vmem = pl.BlockSpec(memory_space=pltpu.VMEM)
    flat = [a for group in states for a in group]
    out = pl.pallas_call(
        partial(optimizer_kernel, rate),
        name="optimizer",
        in_specs=[vmem] * (len(totals) + len(flat)),
        out_specs=[vmem] * (4 * len(states)),
        out_shape=[jax.ShapeDtypeStruct(group[0].shape, F32) for group in states for _ in range(4)],
        compiler_params=pltpu.CompilerParams(vmem_limit_bytes=VMEM_LIMIT),
    )(*totals, *flat)
    return [tuple(out[4 * i : 4 * i + 4]) for i in range(len(states))]


def local(
    D, F,
    patches, cotangent, clip_len,
    pos_table, vector_params, w_qkv, w_proj, w_fc1, b_fc1, w_fc2,
    *states,
):
    params = (pos_table, vector_params, w_qkv, w_proj, w_fc1, b_fc1, w_fc2)
    momenta, averages = states[:7], states[7:]
    local_rows, width = patches.shape
    hidden = w_fc1.shape[1]
    group_size = D * F
    X, Y = F // 4, 2
    table = selectors(local_rows)
    stats, bias_full, q_seg, k_seg, proj_b, fc1_b, fc2_b, pos_full, qkv_full = head(
        D, F, clip_len, patches, pos_table, vector_params, w_qkv, b_fc1, w_proj, w_fc1, w_fc2, 0
    )
    pos_full, qkv_full = (w.reshape(-1, w.shape[-1]) for w in (pos_full, qkv_full))
    emb, first_t, qkv, attended, lse, vec, *full = forward(
        D, F, clip_len, patches, stats, table, pos_full, qkv_full, q_seg, k_seg,
        (proj_b, fc1_b, fc2_b), 1,
    )
    proj_full, fc1_full, fc2_full = (w.reshape(-1, w.shape[-1]) for w in full)
    layer_out, res_grad, att_grad, delta, g_proj, g_fc1, g_b1, g_fc2, g_small_mid, t_fc1_most = middle(
        D, F, stats, emb, attended, cotangent, proj_full, fc1_full, bias_full, fc2_full, vec, 4
    )
    spans = lambda g: g.reshape(D, Y, X, 2, -1, g.shape[-1])
    gq, gk, gv, g_last, t_fc2, t_proj, t_fc1, t_qkv = attend_backward(
        D, F, qkv, att_grad, q_seg, k_seg, lse, delta, first_t,
        [spans(g) for g in (g_fc2, g_proj, g_fc1)], 2,
    )
    patch_grad, small_sum, t_late, t_pos = last_back(
        D, F, clip_len, gq, gk, gv, emb, res_grad, patches, stats, table, qkv_full, vec,
        g_small_mid, g_b1, spans(g_last), 3,
    )
    rate = 0.02 * (local_rows * group_size) ** (-0.5)
    groups = list(zip(params, momenta, averages))
    groups[1] = tuple(a.T for a in groups[1])
    big = [groups[i] for i in (0, 1, 2, 3, 4, 6)]
    done = optimize(rate, (t_pos, t_qkv, t_late, t_proj, t_fc1_most, t_fc1, t_fc2), big)
    me = lax.axis_index("dp") * F + lax.axis_index("fsdp")
    n_bias = b_fc1.size
    g_bias = lax.dynamic_slice(small_sum[2 : 2 + hidden // width].reshape(-1), (me * n_bias,), (n_bias,))
    done[1] = tuple(a.T for a in done[1])
    done.insert(5, stepped(rate, g_bias, *groups[5]))
    feature_stats = jnp.stack([stats[0], stats[4]])
    return (layer_out, patch_grad, feature_stats) + tuple(d[i] for i in range(4) for d in done)


def solution(mesh):
    rows, line = P(AXES, None), P(AXES)
    params = (rows, rows, rows, rows, rows, line, rows)
    return jax.shard_map(
        partial(local, mesh.shape["dp"], mesh.shape["fsdp"]),
        mesh=mesh,
        in_specs=(rows,) * 3 + params * 3,
        out_specs=(rows, rows, P()) + params * 4,
        check_vma=False,
    )
```

```python
from functools import partial

import jax
import jax.numpy as jnp
import ml_dtypes
import numpy as np
from jax import lax
from jax.experimental import pallas as pl
from jax.experimental.pallas import tpu as pltpu
from jax.sharding import PartitionSpec as P

HEADS = 12
FREQ_L = 12
TIME_L = 101
FREQ_S = 8
TIME_S = 64
PRIOR_STEPS = 3
LONG = 1214
SHORT = 514

NORM_EPS = 1e-06
INPUT_EPS = 1e-05
MOMENTUM = 0.9
MESH = pl.DeviceIdType.MESH
AXES = ("dp", "fsdp")
BF = jnp.bfloat16
F32 = jnp.float32
VMEM_LIMIT = 60 * 2**20
POS_PAD = 1280
HEAD_PARTS = (2, 3)
FORWARD_BLOCK = 640
BACKWARD_BLOCK = 256
FORWARD_PARTS = (1, 4, 3)
BACKWARD_PARTS = (2, 1, 1)
BACKWARD_LAGS = ((0, 2, 4, 6, 8),) * 4 + ((0, 2, 4, 6, 7), (0, 1, 2, 3, 4))
EARLY_PAIRS = 4
PAIR_GROUP = 2
MIDDLE_LAGS = ((0, 2, 4, 6, 8),) * 3
EARLY_TILES = 3


TAIL_P = 0.305
TAIL_C = (
    0.121639732,
    0.122466826,
    0.10342081,
    0.121021868,
    -0.037977191,
    0.185717298,
    -0.152988541,
    0.036699245,
)


def resize_rows(size_in, size_out):
    resize_table = np.zeros((size_out, size_in), np.float64)
    for target_row in range(size_out):
        source_pos = max((target_row + 0.5) * size_in / size_out - 0.5, 0.0)
        lower_cell = min(int(np.floor(source_pos)), size_in - 1)
        upper_cell = min(lower_cell + 1, size_in - 1)
        fraction = source_pos - lower_cell
        resize_table[target_row, lower_cell] += 1.0 - fraction
        resize_table[target_row, upper_cell] += fraction
    return resize_table


def selectors(local_rows):
    table = np.zeros((2, local_rows, POS_PAD), np.float64)
    table[0, :LONG, :LONG] = np.eye(LONG)
    short = np.zeros((SHORT, LONG), np.float64)
    short[0, 0] = short[1, 1] = 1.0
    short[2:, 2:] = np.kron(resize_rows(FREQ_L, FREQ_S), resize_rows(TIME_L, TIME_S))
    for first in (0, SHORT):
        table[1, first : first + SHORT, :LONG] = short
    return jnp.asarray(table.astype(ml_dtypes.bfloat16))


def nn(left, right):
    return lax.dot_general(left, right, (((1,), (0,)), ((), ())), preferred_element_type=F32)


def nt(left, right):
    return lax.dot_general(left, right, (((1,), (1,)), ((), ())), preferred_element_type=F32)


def tn(left, right):
    return lax.dot_general(left, right, (((0,), (0,)), ((), ())), preferred_element_type=F32)


class Place:
    def __init__(self, dp_size, fsdp_size):
        self.D, self.F = dp_size, fsdp_size
        self.X, self.Y = fsdp_size // 4, 2
        self.d = lax.axis_index("dp")
        self.f = lax.axis_index("fsdp")
        self.c = lax.rem(self.f, 2)
        self.x = lax.rem(lax.div(self.f, 2), self.X)
        self.y = lax.div(self.f, 2 * self.X)

    def fs(self, y, x, c):
        return (y * self.X + x) * 2 + c

    def up(self, value, step, size):
        return lax.rem(value + step, size)

    def partners(self):
        out = [(self.up(self.d, k, self.D), self.f) for k in range(1, self.D)]
        out += [(self.d, self.fs(self.y, self.up(self.x, k, self.X), self.c)) for k in range(1, self.X)]
        out += [(self.d, self.fs(self.up(self.y, k, self.Y), self.x, self.c)) for k in range(1, self.Y)]
        out.append((self.d, self.fs(self.y, self.x, 1 - self.c)))
        return out

    def everyone(self):
        out = [(self.up(self.d, k, self.D), self.f) for k in range(1, self.D)]
        return out + [(self.d, self.up(self.f, k, self.F)) for k in range(1, self.F)]


def meet(devices):
    barrier = pltpu.get_barrier_semaphore()
    for device in devices:
        pl.semaphore_signal(barrier, inc=1, device_id=device, device_id_type=MESH)
    pl.semaphore_wait(barrier, len(devices))


class Gather:
    @staticmethod
    def count(D, X, Y):
        return (D - 1) + 2 * (X - 1) + 2 * (Y - 1) + 1

    def __init__(self, at, src, out, send, recv, own):
        self.at, self.src, self.out, self.send, self.recv, self.own = at, src, out, send, recv, own
        D, X, Y = at.D, at.X, at.Y
        self.n_z = 0
        self.n_x = D - 1
        self.n_y = self.n_x + X - 1
        self.n_c = self.n_y + Y - 1

    def copy(self, src, dst, number, device):
        return pltpu.make_async_remote_copy(
            src_ref=src,
            dst_ref=dst,
            send_sem=self.send.at[number],
            recv_sem=self.recv.at[number],
            device_id=device,
            device_id_type=MESH,
        )

    def z_copy(self, k):
        at = self.at
        return self.copy(
            self.src,
            self.out.at[at.d, at.y, at.x, at.c],
            self.n_z + k - 1,
            (at.up(at.d, k, at.D), at.f),
        )

    def z_got(self, k):
        at = self.at
        here = self.out.at[at.up(at.d, at.D - k, at.D), at.y, at.x, at.c]
        return self.copy(here, here, self.n_z + k - 1, (at.up(at.d, at.D - k, at.D), at.f))

    def part(self, axis, order, y, x, c):
        if axis == order[0]:
            return self.out.at[:, y, x, c]
        return self.out.at[:, y, :, c] if axis == "y" else self.out.at[:, :, x, c]

    def side(self, axis, order, k, sent):
        at = self.at
        size = at.X if axis == "x" else at.Y
        first = self.n_x if axis == "x" else self.n_y
        mine = at.x if axis == "x" else at.y
        other = at.up(mine, k if sent else size - k, size)
        y, x = (at.y, other) if axis == "x" else (other, at.x)
        block = self.part(axis, order, at.y, at.x, at.c) if sent else self.part(axis, order, y, x, at.c)
        return self.copy(block, block, first + k - 1, (at.d, at.fs(y, x, at.c)))

    def pieces(self, order, c):
        at = self.at
        out = [self.out.at[:, at.y, at.x, c]]
        for axis in order:
            size = at.X if axis == "x" else at.Y
            for k in range(1, size):
                other = at.up(at.x if axis == "x" else at.y, size - k, size)
                y, x = (at.y, other) if axis == "x" else (other, at.x)
                out.append(self.part(axis, order, y, x, c))
        return out

    def sibling(self, block, number):
        at = self.at
        return self.copy(block, block, self.n_c + number, (at.d, at.fs(at.y, at.x, 1 - at.c)))

    def local(self):
        at = self.at
        return pltpu.make_async_copy(self.src, self.out.at[at.d, at.y, at.x, at.c], self.own)

    def size_of(self, axis):
        return self.at.X if axis == "x" else self.at.Y

    def phase(self, number):
        at = self.at
        if number == 0:
            self.local().start()
            for k in range(1, at.D):
                self.z_copy(k).start()
            return
        if number == 1:
            self.local().wait()
            for k in range(1, at.D):
                self.z_got(k).wait_recv()
        for core, order in ((0, ("x", "y")), (1, ("y", "x"))):

            @pl.when(at.c == core)
            def _(core=core, order=order):
                mine = self.pieces(order, core)
                first = 1 + (self.size_of(order[0]) - 1)
                if number == 1:
                    for k in range(1, self.size_of(order[0])):
                        self.side(order[0], order, k, True).start()
                    self.sibling(mine[0], 0).start()
                elif number == 2:
                    for k in range(1, self.size_of(order[0])):
                        self.side(order[0], order, k, False).wait_recv()
                    for k in range(1, self.size_of(order[1])):
                        self.side(order[1], order, k, True).start()
                    for i in range(1, first):
                        self.sibling(mine[i], i).start()
                elif number == 3:
                    for k in range(1, self.size_of(order[1])):
                        self.side(order[1], order, k, False).wait_recv()
                    for i in range(first, len(mine)):
                        self.sibling(mine[i], i).start()
                elif number == 4:
                    for k in range(1, at.D):
                        self.z_copy(k).wait_send()
                    for axis in order:
                        for k in range(1, self.size_of(axis)):
                            self.side(axis, order, k, True).wait_send()
                    for i, block in enumerate(mine):
                        self.sibling(block, i).wait_send()
                    for i, block in enumerate(self.pieces(order[::-1], 1 - core)):
                        self.sibling(block, i).wait_recv()


class Scatter:
    @staticmethod
    def count(D, X, Y):
        return 1 + (Y - 1) + (X - 1) + (D - 1)

    @staticmethod
    def scratch(D, X, Y, R, N, held=False):
        out = [] if held else [pltpu.VMEM((D, Y, X, R, N), BF)]
        out.append(pltpu.VMEM((D, Y, X, R, N), BF))
        out += [pltpu.VMEM((Y - 1, D, X, R, N), BF), pltpu.VMEM((Y - 1, D, R, N), BF)]
        if X != Y:
            out += [pltpu.VMEM((X - 1, D, Y, R, N), BF), pltpu.VMEM((X - 1, D, R, N), BF)]
        return out + [pltpu.VMEM((D - 1, R, N), BF)]

    def __init__(self, at, grad, total, bufs, send, recv, own):
        self.at, self.grad, self.total = at, grad, total
        self.held = len(bufs) % 2 == 0
        bufs = list(bufs)
        self.acc = None if self.held else bufs.pop(0)
        self.r1, self.r2y, self.r3y = bufs[:3]
        self.r2x, self.r3x = (self.r2y, self.r3y) if at.X == at.Y else bufs[3:5]
        self.r4 = bufs[-1]
        self.send, self.recv, self.own = send, recv, own
        self.n_y = 1
        self.n_x = self.n_y + at.Y - 1
        self.n_z = self.n_x + at.X - 1

    def view(self, d, y, x):
        return self.grad.at[d, y, x, self.at.c] if self.held else self.acc.at[d, y, x]

    def get(self, d, y, x):
        return self.grad[d, y, x, self.at.c] if self.held else self.acc[d, y, x]

    def put(self, d, y, x, value):
        if self.held:
            self.grad[d, y, x, self.at.c] = value
        else:
            self.acc[d, y, x] = value

    def fill(self, values, first_column=0):
        at = self.at
        R = self.grad.shape[-2]
        into = slice(first_column, first_column + values.shape[1])

        def one(i, _):
            rest, c = lax.div(i, 2), lax.rem(i, 2)
            rest, x = lax.div(rest, at.X), lax.rem(rest, at.X)
            d, y = lax.div(rest, at.Y), lax.rem(rest, at.Y)
            first = i * R
            if R % 8 == 0:
                block = values[pl.ds(pl.multiple_of(first, 8), R), :].astype(BF)
            else:
                shape = (16, values.shape[0])
                row = lax.broadcasted_iota(jnp.int32, shape, 0)
                pick = jnp.where(lax.broadcasted_iota(jnp.int32, shape, 1) == row + first, 1.0, 0.0)
                block = nn(pick.astype(BF), values[...].astype(BF))[:R].astype(BF)
            self.grad[d, y, x, c, :, into] = block
            return 0

        lax.fori_loop(0, at.D * at.F, one, 0)

    def copy(self, src, dst, number, device):
        return pltpu.make_async_remote_copy(
            src_ref=src,
            dst_ref=dst,
            send_sem=self.send.at[number],
            recv_sem=self.recv.at[number],
            device_id=device,
            device_id_type=MESH,
        )

    def core_copy(self):
        at = self.at
        return self.copy(
            self.grad.at[:, :, :, 1 - at.c], self.r1, 0, (at.d, at.fs(at.y, at.x, 1 - at.c))
        )

    def local(self):
        return pltpu.make_async_copy(self.grad.at[:, :, :, self.at.c], self.acc, self.own)

    def side(self, axis, order, k):
        at, all_d = self.at, slice(None)
        if axis == "y":
            y = at.up(at.y, k, at.Y)
            device = (at.d, at.fs(y, at.x, at.c))
            if axis == order[0]:
                src, dst = self.view(all_d, y, slice(None)), self.r2y
            else:
                src, dst = self.view(all_d, y, at.x), self.r3y
            return self.copy(src, dst.at[k - 1], self.n_y + k - 1, device)
        x = at.up(at.x, k, at.X)
        device = (at.d, at.fs(at.y, x, at.c))
        if axis == order[0]:
            src, dst = self.view(all_d, slice(None), x), self.r2x
        else:
            src, dst = self.view(all_d, at.y, x), self.r3x
        return self.copy(src, dst.at[k - 1], self.n_x + k - 1, device)

    def z_copy(self, k):
        at = self.at
        d = at.up(at.d, k, at.D)
        return self.copy(self.view(d, at.y, at.x), self.r4.at[k - 1], self.n_z + k - 1, (d, at.f))

    def size_of(self, axis):
        return self.at.X if axis == "x" else self.at.Y

    def store(self, total):
        self.total[...] = total

    def phase(self, number):
        at = self.at
        if number == 0:
            if not self.held:
                self.local().start()
            self.core_copy().start()
            return
        if number == 1:
            if not self.held:
                self.local().wait()
            self.core_copy().wait_recv()

            def add(i, _):
                d, rest = lax.div(i, at.Y * at.X), lax.rem(i, at.Y * at.X)
                y, x = lax.div(rest, at.X), lax.rem(rest, at.X)
                self.put(d, y, x, self.get(d, y, x) + self.r1[d, y, x])
                return 0

            lax.fori_loop(0, at.D * at.Y * at.X, add, 0)
        if number == 4:
            for k in range(1, at.D):
                self.z_copy(k).wait_recv()
            total = self.get(at.d, at.y, at.x).astype(F32)
            for k in range(1, at.D):
                total = total + self.r4[k - 1].astype(F32)
            self.store(total)
            self.core_copy().wait_send()
            for k in range(1, at.D):
                self.z_copy(k).wait_send()
        for core, order in ((0, ("y", "x")), (1, ("x", "y"))):

            @pl.when(at.c == core)
            def _(core=core, order=order):
                n0, n1 = self.size_of(order[0]), self.size_of(order[1])
                if number == 1:
                    for k in range(1, n0):
                        self.side(order[0], order, k).start()
                elif number == 2:
                    for k in range(1, n0):
                        self.side(order[0], order, k).wait_recv()

                    def add(i, _):
                        d, j = lax.div(i, n1), lax.rem(i, n1)
                        y, x = (at.y, j) if order[0] == "y" else (j, at.x)
                        got = self.r2y if order[0] == "y" else self.r2x
                        value = self.get(d, y, x)
                        for k in range(1, n0):
                            value = value + got[k - 1, d, j]
                        self.put(d, y, x, value)
                        return 0

                    lax.fori_loop(0, at.D * n1, add, 0)
                    for k in range(1, n1):
                        self.side(order[1], order, k).start()
                elif number == 3:
                    for k in range(1, n1):
                        self.side(order[1], order, k).wait_recv()

                    def add(d, _):
                        got = self.r3y if order[1] == "y" else self.r3x
                        value = self.get(d, at.y, at.x)
                        for k in range(1, n1):
                            value = value + got[k - 1, d]
                        self.put(d, at.y, at.x, value)
                        return 0

                    lax.fori_loop(0, at.D, add, 0)
                elif number == 4:
                    for axis in order:
                        for k in range(1, self.size_of(axis)):
                            self.side(axis, order, k).wait_send()

        if number == 3:
            for k in range(1, at.D):
                self.z_copy(k).start()


class Total:
    @staticmethod
    def count(D, F):
        return (D - 1) + (F // 4 - 1) + 1 + 1

    @staticmethod
    def scratch(D, F, rows, cols):
        return [pltpu.VMEM((D + F // 4 + 2 + 2, rows, cols), F32)]

    def __init__(self, at, buf, send, recv):
        self.at, self.buf, self.send, self.recv = at, buf, send, recv
        device = {
            "d": lambda i: (i, at.f),
            "x": lambda i: (at.d, at.fs(at.y, i, at.c)),
            "y": lambda i: (at.d, at.fs(i, at.x, at.c)),
            "c": lambda i: (at.d, at.fs(at.y, at.x, i)),
        }
        self.stages, slot, number = [], 0, 0
        for axis, size, mine in (("d", at.D, at.d), ("x", at.X, at.x), ("y", at.Y, at.y), ("c", 2, at.c)):
            self.stages.append((slot, number, size, mine, device[axis]))
            slot, number = slot + size, number + size - 1

    def copies(self, stage, sent):
        slot, number, size, mine, device = self.stages[stage]
        out = []
        for k in range(1, size):
            other = self.at.up(mine, k if sent else size - k, size)
            block = self.buf.at[slot + (mine if sent else other)]
            out.append(
                pltpu.make_async_remote_copy(
                    src_ref=block,
                    dst_ref=block,
                    send_sem=self.send.at[number + k - 1],
                    recv_sem=self.recv.at[number + k - 1],
                    device_id=device(other),
                    device_id_type=MESH,
                )
            )
        return out

    def put(self, stage, value):
        slot, _, _, mine, _ = self.stages[stage]
        self.buf[slot + mine] = value
        for copy in self.copies(stage, True):
            copy.start()

    def take(self, stage):
        for copy in self.copies(stage, False):
            copy.wait_recv()
        slot, _, size, _, _ = self.stages[stage]
        total = self.buf[slot]
        for i in range(1, size):
            total = total + self.buf[slot + i]
        return total

    def start(self, value):
        self.put(0, value)

    def advance(self, stage):
        self.put(stage + 1, self.take(stage))

    def end(self):
        total = self.take(3)
        for stage in range(4):
            for copy in self.copies(stage, True):
                copy.wait_send()
        return total


LAGS = (0, 2, 4, 6, 7)


def steps_of(arrays, lags=(0, 1, 3, 5, 6)):
    for step in range(len(arrays) + lags[-1]):
        yield [
            (arrays[i], lags.index(step - i))
            for i in reversed(range(len(arrays)))
            if step - i in lags
        ]


def spread(arrays, slots):
    steps = list(steps_of(arrays, LAGS))
    due = {slot: [] for slot in range(slots)}
    for i, step in enumerate(steps):
        due[(i * (slots - 1)) // (len(steps) - 1)] += step
    return due


def columns(ref, part, parts):
    size = ref.shape[-1] // parts
    return ref.at[(slice(None),) * (len(ref.shape) - 1) + (pl.ds(part * size, size),)]


def placed(values, first, width):
    count = values.shape[1]
    row = lax.broadcasted_iota(jnp.int32, (count, width), 0)
    column = lax.broadcasted_iota(jnp.int32, (count, width), 1)
    return nn(values, jnp.where(column == row + first, 1.0, 0.0).astype(BF))


def head_kernel(
    D, F,
    lens, patches, pos_in, vec_in, qkv_in, bias_in, proj_in, fc1_in, fc2_in,
    stats, bias, qs, ks, proj_b, fc1_b, fc2_b, pos_out, qkv_out,
    pos_b, qkv_b, total_buf, s_send, s_recv, send, recv, own,
):
    at = Place(D, F)
    rows, width = patches.shape
    pos_b[...] = jnp.zeros_like(pos_b)
    pos_b[:, :LONG] = pos_in[...].astype(BF)
    lane = lax.broadcasted_iota(jnp.int32, (8, 128), 1)
    spread_out = jnp.where(lane == LONG - (POS_PAD - 128) + lax.broadcasted_iota(jnp.int32, (8, 128), 0), 1.0, 0.0)
    beside = tn(vec_in[...].astype(BF), spread_out.astype(BF))
    pos_b[:, POS_PAD - 128 :] = (pos_b[:, POS_PAD - 128 :].astype(F32) + beside).astype(BF)
    qkv_b[...] = qkv_in[...].astype(BF)
    meet(at.partners())
    pieces = pieces_of((pos_b, qkv_b), (pos_out, qkv_out), HEAD_PARTS)
    arrays = [
        Gather(at, src, out, send.at[i], recv.at[i], own.at[i]) for i, (src, out) in enumerate(pieces)
    ]
    steps = list(steps_of(arrays))
    arrays[0].phase(0)
    arrays[1].phase(0)
    step_rows = 64
    valid_rows = lens[0, 0] + lens[0, 1]

    def accumulate(i, sums):
        block = pl.ds(pl.multiple_of(i * step_rows, step_rows), step_rows)
        row = i * step_rows + lax.broadcasted_iota(jnp.int32, (step_rows, width), 0)
        values = jnp.where(row < valid_rows, patches[block, :].astype(F32), 0.0)
        first = values.reshape(step_rows // 8, 8, -1)
        return (sums[0] + jnp.sum(first, axis=0), sums[1] + jnp.sum(first * first, axis=0))

    empty = jnp.zeros((8, width), F32)
    plain, square = lax.fori_loop(0, rows // step_rows, accumulate, (empty, empty))
    row = lax.broadcasted_iota(jnp.int32, empty.shape, 0)
    plain = jnp.sum(plain, axis=0, keepdims=True)
    square = jnp.sum(square, axis=0, keepdims=True)
    me = at.d * F + at.f
    count = jnp.zeros((1, width), F32) + valid_rows.astype(F32)
    packed = jnp.where(row == 0, plain, jnp.where(row == 1, square, jnp.where(row == 2, count, 0.0)))
    n_bias = bias_in.shape[1]
    hidden = n_bias * D * F
    own_bias = jnp.broadcast_to(bias_in[...].astype(BF), (8, n_bias))
    for i in range(hidden // width):
        packed = jnp.where(row == 4 + i, placed(own_bias, me * n_bias - i * width, width), packed)
    total = Total(at, total_buf, s_send, s_recv)
    total.start(packed)
    for number, step in enumerate(steps):
        for array, phase in step:
            if phase > 0 or array not in arrays[:2]:
                array.phase(phase)
        if number == 1:
            proj_b[...] = proj_in[...].astype(BF)
            fc1_b[...] = fc1_in[...].astype(BF)
            fc2_b[...] = fc2_in[...].astype(BF)
            position = lax.broadcasted_iota(jnp.int32, qs.shape, 0)
            lane = lax.broadcasted_iota(jnp.int32, qs.shape, 1)
            segment = jnp.where(position < lens[0, 0], 0, jnp.where(position < valid_rows, 1, 2))
            same = segment == lane
            qs[...] = jnp.where(same, 1.0, 0.0).astype(BF)
            ks[...] = jnp.where(same, 0.0, jnp.where(lane < 3, -1e30, 0.0)).astype(BF)
        if number in (2, 4, 6):
            total.advance(number // 2 - 1)
        if number == 8:
            summed = total.end()
            inv_count = 1.0 / summed[2:3]
            mean = summed[0:1] * inv_count
            mean = summed[0:1] / summed[2:3]
            var = summed[1:2] / summed[2:3] - mean * mean
            stats[0:1, :] = mean
            stats[1:2, :] = lax.rsqrt(var + INPUT_EPS)
            stats[2:3, :] = inv_count
            stats[3:4, :] = count
            stats[4:5, :] = var
            stats[5:8, :] = jnp.zeros((3, width), F32)
            for i in range(hidden // width):
                bias[0:1, i * width : (i + 1) * width] = summed[4 + i : 5 + i]


def head(D, F, clip_len, patches, pos, vec, w_qkv, bias, w_proj, w_fc1, w_fc2, collective_id):
    X, Y = F // 4, 2
    rows, width = patches.shape
    hidden = bias.shape[0] * D * F
    count = sum(HEAD_PARTS)
    n = Gather.count(D, X, Y)
    hbm = pl.BlockSpec(memory_space=pl.ANY)
    vmem = pl.BlockSpec(memory_space=pltpu.VMEM)
    own_rows = pos.shape[0]
    sent = [(own_rows, POS_PAD), w_qkv.shape]
    return pl.pallas_call(
        partial(head_kernel, D, F),
        name="head",
        out_shape=[
            jax.ShapeDtypeStruct((8, width), F32),
            jax.ShapeDtypeStruct((1, hidden), F32),
            jax.ShapeDtypeStruct((rows, 128), BF),
            jax.ShapeDtypeStruct((rows, 128), BF),
        ]
        + [jax.ShapeDtypeStruct(w.shape, BF) for w in (w_proj, w_fc1, w_fc2)]
        + [jax.ShapeDtypeStruct((D, Y, X, 2) + shape, BF) for shape in sent],
        in_specs=[pl.BlockSpec(memory_space=pltpu.SMEM)] + [vmem] * 8,
        out_specs=[vmem] * 7 + [hbm] * 2,
        scratch_shapes=[pltpu.VMEM(shape, BF) for shape in sent]
        + Total.scratch(D, F, 8, width)
        + [pltpu.SemaphoreType.DMA((Total.count(D, F),)), pltpu.SemaphoreType.DMA((Total.count(D, F),))]
        + copy_semaphores(count, n),
        compiler_params=pltpu.CompilerParams(
            collective_id=collective_id, has_side_effects=True, vmem_limit_bytes=VMEM_LIMIT
        ),
        cost_estimate=pl.CostEstimate(flops=0, bytes_accessed=20 * 2**20, transcendentals=0),
    )(clip_len, patches, pos, vec.T, w_qkv, bias.reshape(1, -1), w_proj, w_fc1, w_fc2)


def pieces_of(grads, totals, parts):
    return [
        (columns(g, j, n), columns(t, j, n)) for g, t, n in zip(grads, totals, parts) for j in range(n)
    ]


def scatter_arrays(at, pieces, bufs, send, recv, own):
    per = len(bufs) // len(pieces)
    return [
        Scatter(at, grad, total, bufs[i * per : (i + 1) * per], send.at[i], recv.at[i], own.at[i])
        for i, (grad, total) in enumerate(pieces)
    ]


def blocks_shape(D, X, Y, rows, N):
    return (D, Y, X, 2, rows // (D * X * Y * 2), N)


def scatter_scratch(D, X, Y, grads, parts):
    out = []
    for g, n in zip(grads, parts):
        for _ in range(n):
            out += Scatter.scratch(D, X, Y, g.shape[-2], g.shape[-1] // n)
    return out


def copy_semaphores(count, n):
    return [
        pltpu.SemaphoreType.DMA((count, n)),
        pltpu.SemaphoreType.DMA((count, n)),
        pltpu.SemaphoreType.DMA((count,)),
    ]


def row_of(first, rows, width):
    return first + lax.broadcasted_iota(jnp.int32, (rows, width), 0)


def attend_pair(q_ref, k_ref, v_ref, qs_ref, ks_ref, q_block):
    rows = q_ref.shape[0]
    lane = lax.broadcasted_iota(jnp.int32, (q_block, 128), 1)

    def half(values, head):
        keep = lane < 64 if head == 0 else lane >= 64
        return jnp.where(keep, values, jnp.zeros_like(values))

    def query(block, head):
        scaled = q_ref[block, :] * jnp.asarray(0.125, BF)
        return jnp.concatenate([half(scaled, head), qs_ref[block, :]], axis=1)

    keys = jnp.concatenate([k_ref[...], ks_ref[...]], axis=1)
    return keys, query, half


def forward_kernel(
    D, F,
    lens, patches, stats, sel_long, sel_short, pos, w_ref, qs_ref, ks_ref, proj_ref, fc1_ref, fc2_ref,
    emb_out, norm_out, qkv_out, out_ref, lse_ref, vec, proj_out, fc1_out, fc2_out,
    qkv_buf, q_ref, k_ref, key_buf, v_buf, o_buf, send, recv, own,
):
    step = pl.program_id(0)
    part_rows, width = patches.shape
    rows = qkv_buf.shape[0]
    parts = rows // part_rows
    pairs = HEADS // 2
    q_block = FORWARD_BLOCK
    blocks = rows // q_block
    at = Place(D, F)

    @pl.when(step == 0)
    def _():
        meet(at.partners())
        ahead = LONG - (POS_PAD - 128)
        vec[...] = jnp.transpose(pos[:, POS_PAD - 128 :].astype(F32))[ahead : ahead + 8]

    pieces = pieces_of((proj_ref, fc1_ref, fc2_ref), (proj_out, fc1_out, fc2_out), FORWARD_PARTS)
    arrays = [
        Gather(at, src, out, send.at[i], recv.at[i], own.at[i]) for i, (src, out) in enumerate(pieces)
    ]
    due = spread(arrays, parts + 2 * pairs + 1)

    @pl.when(step < parts)
    def _():
        run_due({k: due[k] for k in range(parts)}, step, parts, 0, 1)
        mean, inv_std = stats[0:1, :], stats[1:2, :]
        normed = (patches[...].astype(F32) - mean) * inv_std
        row = lax.broadcasted_iota(jnp.int32, (part_rows, width), 0).astype(F32)
        first_row = (step * part_rows).astype(F32)
        sel = jnp.where(lens[0, 1] > 0, sel_short[0], sel_long[0])
        embedded = jnp.where(row + first_row < stats[3:4, :], normed + nt(sel, pos[...]), 0.0)
        emb_out[...] = embedded
        n, _rho = norm_parts(embedded)
        first = (n * vec[0:1, :] + vec[1:2, :]).astype(BF)
        norm_out[...] = jnp.transpose(first)
        bias = jnp.concatenate([vec[2:3, :], jnp.zeros((1, width), F32), vec[3:4, :]], axis=1)
        projected = (nn(first, w_ref[...]) + bias).astype(BF)
        qkv_out[...] = projected
        qkv_buf[pl.ds(pl.multiple_of(step * part_rows, part_rows), part_rows), :] = projected

    @pl.when(step >= parts)
    def _():
        pair = step - parts
        slots = {k: due[k + parts] for k in range(2 * pairs + 1)}

        def columns_of(i):
            return qkv_buf[:, pl.ds(pl.multiple_of(i * width + pair * 128, 128), 128)]

        q_ref[...] = columns_of(0)
        k_ref[...] = columns_of(1)
        keys, query, _ = attend_pair(q_ref, k_ref, None, qs_ref, ks_ref, q_block)
        key_buf[...] = keys
        v_t = jnp.transpose(columns_of(2))
        ones = jnp.ones((16, rows), BF)
        for head in range(2):
            v_buf[head] = jnp.concatenate([v_t[64 * head : 64 * head + 64], ones], axis=0)
        for i in range(blocks):
            if i in (0, (blocks + 1) // 2):
                run_due(slots, pair, pairs, min(i, 1), 2)
            block = pl.ds(i * q_block, q_block)
            for head in range(2):
                scores = nt(key_buf[...], query(block, head))
                top = jnp.max(scores, axis=0, keepdims=True)
                probs = jnp.exp(scores - top).astype(BF)
                out = nn(v_buf[head], probs)
                total = out[64:65, :]
                o_buf[64 * head : 64 * head + 64, block] = (out[:64] / total).astype(BF)
                lse_ref[0, head : head + 1, block] = top + jnp.log(total)
        out_ref[...] = jnp.transpose(o_buf[...])
        run_due(slots, pair, pairs, 2, 2)


def run_due(due, step, steps, point, points):
    for k in range(steps):
        work = due.get(k * points + point, [])
        if k < steps - 1 and point >= points:
            continue
        if work:

            @pl.when(step == k)
            def _(work=work):
                for array, number in work:
                    array.phase(number)


def timed(arrays, starts, lags, slots):
    due = {slot: [] for slot in range(slots)}
    for array, start, own_lags in reversed(list(zip(arrays, starts, lags))):
        for number, lag in enumerate(own_lags):
            due[min(start + lag, slots - 1)].append((array, number))
    for work in due.values():
        work.sort(key=lambda item: item[1])
    return due


def pair_specs(rows):
    pair = lambda first: pl.BlockSpec((rows, 128), lambda p: (0, first + p))
    whole = pl.BlockSpec((rows, 128), lambda p: (0, 0))
    return pair, whole


def forward(D, F, clip_len, patches, stats, table, pos, w_qkv, q_seg, k_seg, shards, collective_id):
    rows, width = patches.shape
    pairs = HEADS // 2
    part = 256
    parts = rows // part
    hbm = pl.BlockSpec(memory_space=pl.ANY)
    once = lambda a: pl.BlockSpec(a.shape, lambda p: (0,) * a.ndim, pipeline_mode=pl.Buffered(1))
    by_row = lambda n: pl.BlockSpec((part, n), lambda p: (jnp.minimum(p, parts - 1), 0))
    X, Y = F // 4, 2
    n = Gather.count(D, X, Y)
    return pl.pallas_call(
        partial(forward_kernel, D, F),
        name="forward",
        grid=(parts + pairs,),
        in_specs=[
            pl.BlockSpec(memory_space=pltpu.SMEM),
            by_row(width),
            once(stats),
            pl.BlockSpec((1, part, POS_PAD), lambda p: (0, jnp.minimum(p, parts - 1), 0)),
            pl.BlockSpec((1, part, POS_PAD), lambda p: (1, jnp.minimum(p, parts - 1), 0)),
        ]
        + [once(a) for a in (pos, w_qkv, q_seg, k_seg)]
        + [hbm] * 3,
        out_specs=[
            by_row(width),
            pl.BlockSpec((width, part), lambda p: (0, jnp.minimum(p, parts - 1))),
            by_row(3 * width),
            pl.BlockSpec((rows, 128), lambda p: (0, jnp.maximum(p - parts, 0))),
            pl.BlockSpec((1, 8, rows), lambda p: (jnp.maximum(p - parts, 0), 0, 0)),
            pl.BlockSpec((8, width), lambda p: (0, 0)),
        ]
        + [hbm] * 3,
        out_shape=[
            jax.ShapeDtypeStruct((rows, width), F32),
            jax.ShapeDtypeStruct((width, rows), BF),
            jax.ShapeDtypeStruct((rows, 3 * width), BF),
            jax.ShapeDtypeStruct((rows, 128 * pairs), BF),
            jax.ShapeDtypeStruct((pairs, 8, rows), F32),
            jax.ShapeDtypeStruct((8, width), F32),
        ]
        + [jax.ShapeDtypeStruct((D, Y, X, 2) + s.shape, s.dtype) for s in shards],
        scratch_shapes=[
            pltpu.VMEM((rows, 3 * width), BF),
            pltpu.VMEM((rows, 128), BF),
            pltpu.VMEM((rows, 128), BF),
            pltpu.VMEM((rows, 256), BF),
            pltpu.VMEM((2, 80, rows), BF),
            pltpu.VMEM((128, rows), BF),
        ]
        + copy_semaphores(sum(FORWARD_PARTS), n),
        compiler_params=pltpu.CompilerParams(
            collective_id=collective_id, has_side_effects=True, vmem_limit_bytes=VMEM_LIMIT
        ),
        cost_estimate=pl.CostEstimate(
            flops=4 * 12 * rows * rows * 256 + 2 * rows * width * (3 * width + POS_PAD),
            bytes_accessed=40 * 2**20,
            transcendentals=12 * rows * rows,
        ),
    )(clip_len, patches, stats, table, table, pos, w_qkv, q_seg, k_seg, *shards)


class PairScatter(Scatter):
    def __init__(self, first_pair, *rest):
        super().__init__(*rest)
        self.first_pair = first_pair

    def store(self, total):
        width = self.total.shape[-1] // 3
        for k in range(total.shape[1] // 384):
            for i in range(3):
                first = i * width + 128 * (self.first_pair + k)
                source = 384 * k + 128 * i
                self.total[:, first : first + 128] = total[:, source : source + 128]


def backward_pair(
    D, F,
    q_ref, k_ref, v_ref, do_ref, qs_ref, ks_ref, lse_ref, delta_ref, first_t, g_fc2, g_proj, g_fc1, *refs,
):
    dq_ref, dk_ref, dv_ref, g_last, t_fc2, t_proj, t_fc1, t_qkv = refs[:8]
    key_buf, kt_buf, dk_acc, dv_acc, dqt_buf, wide = refs[8:14]
    pairs = HEADS // 2
    groups = EARLY_PAIRS // PAIR_GROUP
    held, rest = refs[14 : 14 + groups], refs[14 + groups : -3]
    send, recv, own = refs[-3:]
    pair = pl.program_id(0)
    rows = q_ref.shape[0]
    q_block = BACKWARD_BLOCK
    blocks = rows // q_block
    at = Place(D, F)

    @pl.when(pair == 0)
    def _():
        meet(at.partners())

    pieces = pieces_of((g_fc2, g_proj, g_fc1), (t_fc2, t_proj, t_fc1), BACKWARD_PARTS)
    early = sum(BACKWARD_PARTS)
    per_held = 4 if at.X == at.Y else 6
    split = len(rest) - per_held * groups
    arrays = scatter_arrays(at, pieces, rest[:split], send, recv, own)
    for p in range(groups):
        bufs = rest[split + p * per_held : split + (p + 1) * per_held]
        i = early + p
        arrays.append(
            PairScatter(
                p * PAIR_GROUP, at, held[p], t_qkv, bufs, send.at[i], recv.at[i], own.at[i]
            )
        )
    starts = list(range(early)) + [2 * PAIR_GROUP * (p + 1) for p in range(groups)]
    due = timed(arrays, starts, BACKWARD_LAGS, 2 * pairs + 1)
    keys, query, half = attend_pair(q_ref, k_ref, v_ref, qs_ref, ks_ref, q_block)
    key_buf[...] = keys
    kt_buf[...] = jnp.transpose(k_ref[...])
    for i in range(blocks):
        if i in (0, (blocks + 1) // 2):
            run_due(due, pair, pairs, min(i, 1), 2)
        block = pl.ds(i * q_block, q_block)
        for head in range(2):
            q_ext = query(block, head)
            d_out = half(do_ref[block, :], head)
            scores = nt(key_buf[...], q_ext)
            probs = jnp.exp(scores - lse_ref[0, head : head + 1, block])
            d_probs = nt(v_ref[...], d_out)
            d_scores = (probs * (d_probs - delta_ref[0, head : head + 1, block])).astype(BF)
            dv = nn(probs.astype(BF), d_out)
            dk = nn(d_scores, q_ext[:, :128])
            if i == 0 and head == 0:
                dv_acc[...] = dv
                dk_acc[...] = dk
            else:
                dv_acc[...] += dv
                dk_acc[...] += dk
            dq = nn(kt_buf[64 * head : 64 * head + 64, :], d_scores)
            dqt_buf[64 * head : 64 * head + 64, block] = (dq * 0.125).astype(BF)
    dq_ref[...] = jnp.transpose(dqt_buf[...])
    dk_ref[...] = dk_acc[...].astype(BF)
    dv_ref[...] = dv_acc[...].astype(BF)
    joined = jnp.concatenate([dq_ref[...], dk_ref[...], dv_ref[...]], axis=1)
    wide[...] = nn(first_t[...], joined)
    for p in range(EARLY_PAIRS):

        @pl.when(pair == p)
        def _(p=p):
            arrays[early + p // PAIR_GROUP].fill(wide, 384 * (p % PAIR_GROUP))

    @pl.when(pair >= EARLY_PAIRS)
    def _():
        g_last[...] = wide[...].astype(BF)

    run_due(due, pair, pairs, 2, 2)


def attend_backward(D, F, qkv, grad_attended, q_seg, k_seg, lse, delta, first_t, grads, collective_id):
    rows = qkv.shape[0]
    width = first_t.shape[0]
    pairs = HEADS // 2
    pair, whole = pair_specs(rows)
    line = pl.BlockSpec((1, 8, rows), lambda p: (p, 0, 0))
    hbm = pl.BlockSpec(memory_space=pl.ANY)
    once = lambda shape: pl.BlockSpec(shape, lambda p: (0,) * len(shape), pipeline_mode=pl.Buffered(1))
    X, Y = F // 4, 2
    n = Scatter.count(D, X, Y)
    own_rows = width // (D * F)
    groups = EARLY_PAIRS // PAIR_GROUP
    held = [pltpu.VMEM(blocks_shape(D, X, Y, width, 384 * PAIR_GROUP), BF)] * groups
    held_scratch = Scatter.scratch(D, X, Y, own_rows, 384 * PAIR_GROUP, held=True) * groups
    totals = [jax.ShapeDtypeStruct(g.shape[-2:], F32) for g in grads]
    totals.append(jax.ShapeDtypeStruct((own_rows, 3 * width), F32))
    return pl.pallas_call(
        partial(backward_pair, D, F),
        name="attend_backward",
        grid=(pairs,),
        in_specs=[pair(0), pair(pairs), pair(2 * pairs), pair(0), whole, whole, line, line]
        + [once(first_t.shape)]
        + [hbm] * 3,
        out_specs=[pair(0)] * 3
        + [pl.BlockSpec((width, 384), lambda p: (0, jnp.maximum(p - EARLY_PAIRS, 0)))]
        + [once(t.shape) for t in totals],
        out_shape=[jax.ShapeDtypeStruct((rows, 128 * pairs), BF)] * 3
        + [jax.ShapeDtypeStruct((width, 384 * (pairs - EARLY_PAIRS)), BF)]
        + totals,
        scratch_shapes=[
            pltpu.VMEM((rows, 256), BF),
            pltpu.VMEM((128, rows), BF),
            pltpu.VMEM((rows, 128), F32),
            pltpu.VMEM((rows, 128), F32),
            pltpu.VMEM((128, rows), BF),
            pltpu.VMEM((width, 384), F32),
        ]
        + held
        + scatter_scratch(D, X, Y, grads, BACKWARD_PARTS)
        + held_scratch
        + copy_semaphores(sum(BACKWARD_PARTS) + groups, n),
        compiler_params=pltpu.CompilerParams(
            collective_id=collective_id, has_side_effects=True, vmem_limit_bytes=VMEM_LIMIT
        ),
        cost_estimate=pl.CostEstimate(
            flops=10 * 12 * rows * rows * 256,
            bytes_accessed=14 * rows * 768,
            transcendentals=12 * rows * rows,
        ),
    )(qkv, qkv, qkv, grad_attended, q_seg, k_seg, lse, delta, first_t, *grads)


def gelu_both(u):
    z = jnp.abs(u)
    falling = jnp.exp(-0.5 * u * u)
    t = 1.0 / (1.0 + TAIL_P * z)
    poly = TAIL_C[-1]
    for coefficient in TAIL_C[-2::-1]:
        poly = poly * t + coefficient
    tail = poly * t * falling
    upper = jnp.where(u >= 0, 1.0 - tail, tail)
    return u * upper, upper + u * falling * 0.3989422804014327


def norm_parts(values):
    center = values - jnp.mean(values, axis=1, keepdims=True)
    spread = jnp.mean(center * center, axis=1, keepdims=True)
    rho = lax.rsqrt(spread + NORM_EPS)
    return center * rho, rho


def norm_back(n, rho, grad, gain):
    q = grad * gain
    return rho * (q - jnp.mean(q, axis=1, keepdims=True) - n * jnp.mean(q * n, axis=1, keepdims=True))


def fold(values):
    return jnp.sum(values.reshape(-1, 8, values.shape[1]), axis=0)


def middle_kernel(
    D, F, tiles,
    stats, emb, att, cot, wo, w1, b1, w2, vec, pick,
    layer_out, res_grad, att_grad, delta_out, g_proj, g_fc1, g_b1, g_fc2, g_small, t_fc1,
    residual, second, second_t, mlp, g_second, act_buf, pre_buf, wide, *rest,
):
    step = pl.program_id(0)
    rows, width = emb.shape
    tile = w1.shape[1]
    block_rows = 256
    blocks = rows // block_rows
    ones = jnp.ones((8, block_rows), BF)
    masked, branch = layer_out, second
    at = Place(D, F)
    held, bufs, (send, recv, own) = rest[:EARLY_TILES], rest[EARLY_TILES:-3], rest[-3:]
    per = len(bufs) // EARLY_TILES
    arrays = [
        Scatter(
            at, held[j], t_fc1.at[:, pl.ds(j * tile, tile)], bufs[j * per : (j + 1) * per],
            send.at[j], recv.at[j], own.at[j],
        )
        for j in range(EARLY_TILES)
    ]
    due = timed(arrays, [2 * j + 2 for j in range(EARLY_TILES)], MIDDLE_LAGS, 2 * tiles + 2)

    def take(i):
        return pl.ds(pl.multiple_of(i * block_rows, block_rows), block_rows)

    def flags(i):
        row = lax.broadcasted_iota(jnp.int32, (block_rows, width), 0).astype(F32)
        return row + jnp.asarray(i * block_rows, jnp.int32).astype(F32) < stats[3:4, :]

    @pl.when(step == 0)
    def _():
        meet(at.partners())

        def one(i, _):
            block = take(i)
            branch_out = nn(att[block, :], wo[...]) + vec[4:5, :]
            res = emb[block, :] + branch_out
            residual[block, :] = res
            n, _rho = norm_parts(res)
            sn = (n * vec[5:6, :] + vec[6:7, :]).astype(BF)
            second[block, :] = sn
            second_t[i] = jnp.transpose(sn)
            masked[block, :] = jnp.where(flags(i), cot[block, :].astype(F32), 0.0).astype(BF)
            mlp[block, :] = jnp.zeros((block_rows, width), F32)
            g_second[block, :] = jnp.zeros((block_rows, width), F32)
            return 0

        lax.fori_loop(0, blocks, one, 0)

    bias = b1[...]
    for i in range(blocks):
        if i in (0, 3):
            run_due(due, step, tiles, i // 3, 2)
        block = pl.ds(i * block_rows, block_rows)
        pre = nn(second[block, :], w1[...]) + bias
        act, slope = gelu_both(pre)
        act = act.astype(BF)
        act_buf[block, :] = act
        grad_act = nt(masked[block, :], w2[...]).astype(BF).astype(F32)
        grad_pre = (grad_act * slope).astype(BF)
        pre_buf[block, :] = grad_pre
        mlp[block, :] += nn(act, w2[...])
        g_second[block, :] += nt(grad_pre, w1[...])
    g_fc2[...] = tn(act_buf[...], masked[...]).astype(BF)
    for i in range(blocks):
        block = pl.ds(i * block_rows, block_rows)
        part = nn(second_t[i], pre_buf[block, :])
        line = nn(ones, pre_buf[block, :])
        total = part if i == 0 else total + part
        lines = line if i == 0 else lines + line
    wide[...] = total
    g_b1[...] = lines
    for j in range(EARLY_TILES):

        @pl.when(step == j)
        def _(j=j):
            arrays[j].fill(wide)

    @pl.when(step >= EARLY_TILES)
    def _():
        g_fc1[...] = wide[...].astype(BF)

    run_due(due, step, tiles, 2, 2)

    @pl.when(step == tiles - 1)
    def _():
        def one(i, sums):
            block = take(i)
            res = residual[block, :]
            n, rho = norm_parts(res)
            out_grad = masked[block, :]
            layer_out[block, :] = jnp.where(flags(i), res + mlp[block, :] + vec[7:8, :], 0.0).astype(BF)
            grad = g_second[block, :].astype(BF).astype(F32)
            back = norm_back(n, rho, grad, vec[5:6, :])
            total = out_grad.astype(F32) + back
            res_grad[block, :] = total
            low = total.astype(BF)
            branch[block, :] = low
            into = nt(low, wo[...]).astype(BF)
            att_grad[block, :] = into
            product = into.astype(F32) * att[block, :].astype(F32)
            high = product.astype(BF)
            rest = (product - high.astype(F32)).astype(BF)
            delta = nn(high, pick[...]) + nn(rest, pick[...])
            lines = jnp.transpose(delta)
            for p in range(HEADS // 2):
                delta_out[p, 0:2, block] = lines[2 * p : 2 * p + 2, :]
            return (
                sums[0] + nn(ones, low)[0:8],
                sums[1] + fold(grad * n),
                sums[2] + fold(grad),
                sums[3] + nn(ones, out_grad)[0:8],
            )

        empty = jnp.zeros((8, width), F32)
        sums = lax.fori_loop(0, blocks, one, (empty,) * 4)
        g_proj[...] = tn(att[...], branch[...]).astype(BF)
        g_small[0:1, :] = sums[0][0:1]
        g_small[1:2, :] = jnp.sum(sums[1], axis=0, keepdims=True)
        g_small[2:3, :] = jnp.sum(sums[2], axis=0, keepdims=True)
        g_small[3:4, :] = sums[3][0:1]
        g_small[4:8, :] = jnp.zeros((4, width), F32)

    run_due(due, step, tiles, 3, 2)


def middle(D, F, stats, emb, att, cot, wo, w1, b1, w2, vec, collective_id):
    rows, width = emb.shape
    hidden = w1.shape[1]
    tile = 512
    tiles = hidden // tile
    X, Y = F // 4, 2
    own_rows = width // (D * F)
    once = pl.Buffered(1)
    whole = lambda shape: pl.BlockSpec(shape, lambda j: (0,) * len(shape), pipeline_mode=once)
    pick = np.zeros((width, 128), np.float32)
    pick[np.arange(width), np.arange(width) // 64] = 1.0
    pick = jnp.asarray(pick.astype(ml_dtypes.bfloat16))
    out_shape = [
        jax.ShapeDtypeStruct((rows, width), BF),
        jax.ShapeDtypeStruct((rows, width), F32),
        jax.ShapeDtypeStruct((rows, width), BF),
        jax.ShapeDtypeStruct((HEADS // 2, 8, rows), F32),
        jax.ShapeDtypeStruct((width, width), BF),
        jax.ShapeDtypeStruct((width, tile * (tiles - EARLY_TILES)), BF),
        jax.ShapeDtypeStruct((8, hidden), F32),
        jax.ShapeDtypeStruct((hidden, width), BF),
        jax.ShapeDtypeStruct((8, width), F32),
        jax.ShapeDtypeStruct((own_rows, tile * EARLY_TILES), F32),
    ]
    scatter = []
    for _ in range(EARLY_TILES):
        scatter += Scatter.scratch(D, X, Y, own_rows, tile, held=True)
    return pl.pallas_call(
        partial(middle_kernel, D, F, tiles),
        name="middle",
        grid=(tiles,),
        in_specs=[
            whole(stats.shape),
            whole((rows, width)),
            whole((rows, width)),
            whole((rows, width)),
            whole((width, width)),
            pl.BlockSpec((width, tile), lambda j: (0, j)),
            pl.BlockSpec((1, tile), lambda j: (0, j)),
            pl.BlockSpec((tile, width), lambda j: (j, 0)),
            whole((8, width)),
            whole((width, 128)),
        ],
        out_specs=[whole(s.shape) for s in out_shape[:5]]
        + [
            pl.BlockSpec((width, tile), lambda j: (0, jnp.maximum(j - EARLY_TILES, 0))),
            pl.BlockSpec((8, tile), lambda j: (0, j)),
            pl.BlockSpec((tile, width), lambda j: (j, 0)),
            whole((8, width)),
            whole(out_shape[9].shape),
        ],
        scratch_shapes=[
            pltpu.VMEM((rows, width), F32),
            pltpu.VMEM((rows, width), BF),
            pltpu.VMEM((rows // 256, width, 256), BF),
            pltpu.VMEM((rows, width), F32),
            pltpu.VMEM((rows, width), F32),
            pltpu.VMEM((rows, tile), BF),
            pltpu.VMEM((rows, tile), BF),
            pltpu.VMEM((width, tile), F32),
        ]
        + [pltpu.VMEM(blocks_shape(D, X, Y, width, tile), BF)] * EARLY_TILES
        + scatter
        + copy_semaphores(EARLY_TILES, Scatter.count(D, X, Y)),
        out_shape=out_shape,
        compiler_params=pltpu.CompilerParams(
            collective_id=collective_id, has_side_effects=True, vmem_limit_bytes=VMEM_LIMIT
        ),
        cost_estimate=pl.CostEstimate(
            flops=2 * rows * width * (6 * hidden + 3 * width),
            bytes_accessed=40 * 2**20,
            transcendentals=rows * hidden,
        ),
    )(stats, emb, att, cot, wo, w1, b1, w2, vec, pick)


def last_kernel(
    D, F,
    lens, gq, gk, gv, emb, res_grad, patches, stats, sel_long, sel_short, w_ref, vec, small_in, bias_in, g_last,
    patch_grad, small_out, t_last, t_pos,
    pos_acc, masked, normed_buf, sums, pos_a, pos_b, total_buf, s_send, s_recv, *rest,
):
    step = pl.program_id(0)
    rows, width = emb.shape
    total_rows = patch_grad.shape[0]
    steps = total_rows // rows
    ones = jnp.ones((8, rows), BF)
    at = Place(D, F)
    bufs, (send, recv, own) = rest[:-3], rest[-3:]
    per_held = 4 if at.X == at.Y else 6
    early = Scatter(at, g_last, t_last, bufs[: per_held + 1], send.at[0], recv.at[0], own.at[0])
    pos_blocks = (pos_a, pos_b)
    half = POS_PAD // 2
    pos = [
        Scatter(
            at, pos_blocks[i], t_pos.at[:, pl.ds(half * i, half)],
            bufs[per_held + 1 + per_held * i : per_held + 1 + per_held * (i + 1)],
            send.at[1 + i], recv.at[1 + i], own.at[1 + i],
        )
        for i in range(2)
    ]
    total = Total(at, total_buf, s_send, s_recv)

    @pl.when(step == 0)
    def _():
        meet(at.partners())
        early.phase(0)
        sums[...] = jnp.zeros_like(sums)

    for number in range(1, 5):

        @pl.when(step == number)
        def _(number=number):
            early.phase(number)

    parts = [gq[...], gk[...], gv[...]]
    for i, part in enumerate(parts):
        into = nt(part, w_ref[:, i * width : (i + 1) * width])
        grad = into if i == 0 else grad + into
    grad = grad.astype(BF).astype(F32)
    n, rho = norm_parts(emb[...])
    row = lax.broadcasted_iota(jnp.int32, (rows, width), 0).astype(F32) + (step * rows).astype(F32)
    valid = row < stats[3:4, :]
    whole = jnp.where(valid, res_grad[...] + norm_back(n, rho, grad, vec[0:1, :]), 0.0)
    block = pl.ds(pl.multiple_of(step * rows, rows), rows)
    masked[block, :] = whole
    sel = jnp.where(lens[0, 1] > 0, sel_short[0], sel_long[0])
    moved = tn(whole.astype(BF), sel)

    @pl.when(step == 0)
    def _():
        pos_acc[...] = moved

    @pl.when(step > 0)
    def _():
        pos_acc[...] += moved

    normed = (patches[...].astype(F32) - stats[0:1, :]) * stats[1:2, :]
    normed_buf[block, :] = jnp.where(valid, normed, 0.0)
    sums[0] += fold(grad * n)
    sums[1] += fold(grad)
    sums[2] += nn(ones, parts[0])
    sums[3] += nn(ones, parts[2])
    sums[4] += fold(whole)
    sums[5] += fold(whole * normed)

    @pl.when(step == steps - 1)
    def _():
        lines = []
        for i in range(6):
            line = sums[i]
            lines.append(line[0:1] if i in (2, 3) else jnp.sum(line, axis=0, keepdims=True))
        hidden = bias_in.shape[1]
        own_lines = lines[4:] + [bias_in[0:1, i * width : (i + 1) * width] for i in range(hidden // width)]
        own_lines += [jnp.zeros((1, width), F32)] * (8 - len(own_lines))
        total.start(jnp.concatenate(own_lines, axis=0))
        own_vec = lines[:4] + [small_in[i : i + 1, :] for i in range(4)]
        ahead = LONG - (POS_PAD - 128)
        own_vec = [jnp.zeros((ahead, width), F32)] + own_vec + [jnp.zeros((128 - ahead - 8, width), F32)]
        pos_acc[:, POS_PAD - 128 :] += jnp.transpose(jnp.concatenate(own_vec, axis=0))
        pos[0].fill(pos_acc.at[:, :half])
        pos[0].phase(0)
        pos[1].fill(pos_acc.at[:, half:])
        pos[1].phase(0)
        pos[0].phase(1)
        pos[1].phase(1)
        total.advance(0)
        pos[0].phase(2)
        pos[1].phase(2)
        total.advance(1)
        pos[0].phase(3)
        pos[1].phase(3)
        total.advance(2)
        summed = total.end()
        small_out[...] = summed
        inv_std, inv_count = stats[1:2, :], stats[2:3, :]
        plain, scaled = summed[0:1] * inv_count, summed[1:2] * inv_count

        def one(i, _):
            part = pl.ds(pl.multiple_of(i * 64, 64), 64)
            valid = flag_buf(i)
            value = masked[part, :] - valid * plain - normed_buf[part, :] * scaled
            patch_grad[part, :] = (inv_std * value).astype(BF)
            return 0

        valid_rows = stats[3:4, :]

        def flag_buf(i):
            row = lax.broadcasted_iota(jnp.int32, (64, width), 0).astype(F32)
            return jnp.where(row + (i * 64).astype(F32) < valid_rows, 1.0, 0.0)

        lax.fori_loop(0, total_rows // 64, one, 0)
        pos[0].phase(4)
        pos[1].phase(4)


def last_back(D, F, clip_len, gq, gk, gv, emb, res_grad, patches, stats, table, w_qkv, vec, small, bias, g_last, collective_id):
    rows, width = emb.shape
    block = 256
    once = pl.Buffered(1)
    whole = lambda shape: pl.BlockSpec(shape, lambda i: (0,) * len(shape), pipeline_mode=once)
    by_row = lambda n: pl.BlockSpec((block, n), lambda i: (i, 0))
    X, Y = F // 4, 2
    own_rows = width // (D * F)
    n = Scatter.count(D, X, Y)
    out_shape = [
        jax.ShapeDtypeStruct((rows, width), BF),
        jax.ShapeDtypeStruct((8, width), F32),
        jax.ShapeDtypeStruct((own_rows, g_last.shape[-1]), F32),
        jax.ShapeDtypeStruct((own_rows, POS_PAD), F32),
    ]
    return pl.pallas_call(
        partial(last_kernel, D, F),
        name="last_back",
        grid=(rows // block,),
        in_specs=[pl.BlockSpec(memory_space=pltpu.SMEM)]
        + [by_row(width)] * 6
        + [
            whole(stats.shape),
            pl.BlockSpec((1, block, POS_PAD), lambda i: (0, i, 0)),
            pl.BlockSpec((1, block, POS_PAD), lambda i: (1, i, 0)),
            whole(w_qkv.shape),
            whole(vec.shape),
        ]
        + [whole(small.shape), whole(bias.shape), pl.BlockSpec(memory_space=pl.ANY)],
        out_specs=[whole(o.shape) for o in out_shape],
        out_shape=out_shape,
        scratch_shapes=[
            pltpu.VMEM((width, POS_PAD), F32),
            pltpu.VMEM((rows, width), F32),
            pltpu.VMEM((rows, width), F32),
            pltpu.VMEM((6, 8, width), F32),
            pltpu.VMEM(blocks_shape(D, X, Y, width, POS_PAD // 2), BF),
            pltpu.VMEM(blocks_shape(D, X, Y, width, POS_PAD // 2), BF),
        ]
        + Total.scratch(D, F, 8, width)
        + [pltpu.SemaphoreType.DMA((Total.count(D, F),)), pltpu.SemaphoreType.DMA((Total.count(D, F),))]
        + Scatter.scratch(D, X, Y, own_rows, g_last.shape[-1])
        + Scatter.scratch(D, X, Y, own_rows, POS_PAD // 2, held=True) * 2
        + copy_semaphores(3, n),
        compiler_params=pltpu.CompilerParams(
            collective_id=collective_id, has_side_effects=True, vmem_limit_bytes=VMEM_LIMIT
        ),
        cost_estimate=pl.CostEstimate(
            flops=2 * rows * width * (6 * width + POS_PAD),
            bytes_accessed=30 * 2**20,
            transcendentals=0,
        ),
    )(clip_len, gq, gk, gv, emb, res_grad, patches, stats, table, table, w_qkv, vec, small, bias, g_last)


def average_keep():
    return min(0.99, (1.0 + PRIOR_STEPS) / (10.0 + PRIOR_STEPS))


def stepped(rate, g, w, m, e):
    keep = average_keep()
    moved = MOMENTUM * m + g
    update = -(rate * (g + MOMENTUM * moved))
    return g, update, moved, keep * e + (1.0 - keep) * (w + update)


def optimizer_kernel(rate, t_pos, t_early, t_late, t_proj, t_most, t_last, t_fc2, *refs):
    states, outs = refs[:18], refs[18:]
    names = 6

    def write(i, where, g):
        w, m, e = (states[3 * i + j][where] for j in range(3))
        for out, value in zip(outs[4 * i : 4 * i + 4], stepped(rate, g, w, m, e)):
            out[where] = value

    everything = (slice(None), slice(None))
    write(0, everything, t_pos[:, :LONG])
    ahead = LONG - (POS_PAD - 128)
    write(1, everything, jnp.transpose(t_pos[:, POS_PAD - 128 :])[ahead : ahead + 8])
    width = t_early.shape[1] // 3
    early = 128 * EARLY_PAIRS
    for i in range(3):
        first = i * width
        write(2, (slice(None), slice(first, first + early)), t_early[:, first : first + early])
        for k in range(HEADS // 2 - EARLY_PAIRS):
            to = first + early + 128 * k
            source = 384 * k + 128 * i
            write(2, (slice(None), slice(to, to + 128)), t_late[:, source : source + 128])
    write(3, everything, t_proj[...])
    most = t_most.shape[1]
    write(4, (slice(None), slice(0, most)), t_most[...])
    write(4, (slice(None), slice(most, most + t_last.shape[1])), t_last[...])
    write(5, everything, t_fc2[...])


def optimize(rate, totals, states):
    vmem = pl.BlockSpec(memory_space=pltpu.VMEM)
    flat = [a for group in states for a in group]
    out = pl.pallas_call(
        partial(optimizer_kernel, rate),
        name="optimizer",
        in_specs=[vmem] * (len(totals) + len(flat)),
        out_specs=[vmem] * (4 * len(states)),
        out_shape=[jax.ShapeDtypeStruct(group[0].shape, F32) for group in states for _ in range(4)],
        compiler_params=pltpu.CompilerParams(vmem_limit_bytes=VMEM_LIMIT),
    )(*totals, *flat)
    return [tuple(out[4 * i : 4 * i + 4]) for i in range(len(states))]


def local(
    D, F,
    patches, cotangent, clip_len,
    pos_table, vector_params, w_qkv, w_proj, w_fc1, b_fc1, w_fc2,
    *states,
):
    params = (pos_table, vector_params, w_qkv, w_proj, w_fc1, b_fc1, w_fc2)
    momenta, averages = states[:7], states[7:]
    local_rows, width = patches.shape
    hidden = w_fc1.shape[1]
    group_size = D * F
    X, Y = F // 4, 2
    table = selectors(local_rows)
    stats, bias_full, q_seg, k_seg, proj_b, fc1_b, fc2_b, pos_full, qkv_full = head(
        D, F, clip_len, patches, pos_table, vector_params, w_qkv, b_fc1, w_proj, w_fc1, w_fc2, 0
    )
    pos_full, qkv_full = (w.reshape(-1, w.shape[-1]) for w in (pos_full, qkv_full))
    emb, first_t, qkv, attended, lse, vec, *full = forward(
        D, F, clip_len, patches, stats, table, pos_full, qkv_full, q_seg, k_seg,
        (proj_b, fc1_b, fc2_b), 1,
    )
    proj_full, fc1_full, fc2_full = (w.reshape(-1, w.shape[-1]) for w in full)
    layer_out, res_grad, att_grad, delta, g_proj, g_fc1, g_b1, g_fc2, g_small_mid, t_fc1_most = middle(
        D, F, stats, emb, attended, cotangent, proj_full, fc1_full, bias_full, fc2_full, vec, 4
    )
    spans = lambda g: g.reshape(D, Y, X, 2, -1, g.shape[-1])
    gq, gk, gv, g_last, t_fc2, t_proj, t_fc1, t_qkv = attend_backward(
        D, F, qkv, att_grad, q_seg, k_seg, lse, delta, first_t,
        [spans(g) for g in (g_fc2, g_proj, g_fc1)], 2,
    )
    patch_grad, small_sum, t_late, t_pos = last_back(
        D, F, clip_len, gq, gk, gv, emb, res_grad, patches, stats, table, qkv_full, vec,
        g_small_mid, g_b1, spans(g_last), 3,
    )
    rate = 0.02 * (local_rows * group_size) ** (-0.5)
    groups = list(zip(params, momenta, averages))
    groups[1] = tuple(a.T for a in groups[1])
    big = [groups[i] for i in (0, 1, 2, 3, 4, 6)]
    done = optimize(rate, (t_pos, t_qkv, t_late, t_proj, t_fc1_most, t_fc1, t_fc2), big)
    me = lax.axis_index("dp") * F + lax.axis_index("fsdp")
    n_bias = b_fc1.size
    g_bias = lax.dynamic_slice(small_sum[2 : 2 + hidden // width].reshape(-1), (me * n_bias,), (n_bias,))
    done[1] = tuple(a.T for a in done[1])
    done.insert(5, stepped(rate, g_bias, *groups[5]))
    feature_stats = jnp.stack([stats[0], stats[4]])
    return (layer_out, patch_grad, feature_stats) + tuple(d[i] for i in range(4) for d in done)


def solution(mesh):
    rows, line = P(AXES, None), P(AXES)
    params = (rows, rows, rows, rows, rows, line, rows)
    return jax.shard_map(
        partial(local, mesh.shape["dp"], mesh.shape["fsdp"]),
        mesh=mesh,
        in_specs=(rows,) * 3 + params * 3,
        out_specs=(rows, rows, P()) + params * 4,
        check_vma=False,
    )
```

```python
from functools import partial

import jax
import jax.numpy as jnp
import ml_dtypes
import numpy as np
from jax import lax
from jax.experimental import pallas as pl
from jax.experimental.pallas import tpu as pltpu
from jax.sharding import PartitionSpec as P

HEADS = 12
FREQ_L = 12
TIME_L = 101
FREQ_S = 8
TIME_S = 64
PRIOR_STEPS = 3
LONG = 1214
SHORT = 514

NORM_EPS = 1e-06
INPUT_EPS = 1e-05
MOMENTUM = 0.9
MESH = pl.DeviceIdType.MESH
AXES = ("dp", "fsdp")
BF = jnp.bfloat16
F32 = jnp.float32
VMEM_LIMIT = 60 * 2**20
POS_PAD = 1280
HEAD_PARTS = (2, 3)
FORWARD_BLOCK = 640
BACKWARD_BLOCK = 256
FORWARD_PARTS = (1, 4, 3)
BACKWARD_PARTS = (2, 1, 1)
BACKWARD_LAGS = ((0, 2, 4, 6, 8),) * 4 + ((0, 2, 4, 6, 7), (0, 1, 2, 3, 4))
EARLY_PAIRS = 4
PAIR_GROUP = 2
MIDDLE_LAGS = ((0, 2, 4, 6, 8),) * 3
EARLY_TILES = 3


TAIL_P = 0.305
TAIL_C = (
    0.121639732,
    0.122466826,
    0.10342081,
    0.121021868,
    -0.037977191,
    0.185717298,
    -0.152988541,
    0.036699245,
)


def resize_rows(size_in, size_out):
    resize_table = np.zeros((size_out, size_in), np.float64)
    for target_row in range(size_out):
        source_pos = max((target_row + 0.5) * size_in / size_out - 0.5, 0.0)
        lower_cell = min(int(np.floor(source_pos)), size_in - 1)
        upper_cell = min(lower_cell + 1, size_in - 1)
        fraction = source_pos - lower_cell
        resize_table[target_row, lower_cell] += 1.0 - fraction
        resize_table[target_row, upper_cell] += fraction
    return resize_table


def selectors(local_rows):
    table = np.zeros((2, local_rows, POS_PAD), np.float64)
    table[0, :LONG, :LONG] = np.eye(LONG)
    short = np.zeros((SHORT, LONG), np.float64)
    short[0, 0] = short[1, 1] = 1.0
    short[2:, 2:] = np.kron(resize_rows(FREQ_L, FREQ_S), resize_rows(TIME_L, TIME_S))
    for first in (0, SHORT):
        table[1, first : first + SHORT, :LONG] = short
    return jnp.asarray(table.astype(ml_dtypes.bfloat16))


def nn(left, right):
    return lax.dot_general(left, right, (((1,), (0,)), ((), ())), preferred_element_type=F32)


def nt(left, right):
    return lax.dot_general(left, right, (((1,), (1,)), ((), ())), preferred_element_type=F32)


def tn(left, right):
    return lax.dot_general(left, right, (((0,), (0,)), ((), ())), preferred_element_type=F32)


class Place:
    def __init__(self, dp_size, fsdp_size):
        self.D, self.F = dp_size, fsdp_size
        self.X, self.Y = fsdp_size // 4, 2
        self.d = lax.axis_index("dp")
        self.f = lax.axis_index("fsdp")
        self.c = lax.rem(self.f, 2)
        self.x = lax.rem(lax.div(self.f, 2), self.X)
        self.y = lax.div(self.f, 2 * self.X)

    def fs(self, y, x, c):
        return (y * self.X + x) * 2 + c

    def up(self, value, step, size):
        return lax.rem(value + step, size)

    def partners(self):
        out = [(self.up(self.d, k, self.D), self.f) for k in range(1, self.D)]
        out += [(self.d, self.fs(self.y, self.up(self.x, k, self.X), self.c)) for k in range(1, self.X)]
        out += [(self.d, self.fs(self.up(self.y, k, self.Y), self.x, self.c)) for k in range(1, self.Y)]
        out.append((self.d, self.fs(self.y, self.x, 1 - self.c)))
        return out

    def everyone(self):
        out = [(self.up(self.d, k, self.D), self.f) for k in range(1, self.D)]
        return out + [(self.d, self.up(self.f, k, self.F)) for k in range(1, self.F)]


def meet(devices):
    barrier = pltpu.get_barrier_semaphore()
    for device in devices:
        pl.semaphore_signal(barrier, inc=1, device_id=device, device_id_type=MESH)
    pl.semaphore_wait(barrier, len(devices))


class Gather:
    @staticmethod
    def count(D, X, Y):
        return (D - 1) + 2 * (X - 1) + 2 * (Y - 1) + 1

    def __init__(self, at, src, out, send, recv, own):
        self.at, self.src, self.out, self.send, self.recv, self.own = at, src, out, send, recv, own
        D, X, Y = at.D, at.X, at.Y
        self.n_z = 0
        self.n_x = D - 1
        self.n_y = self.n_x + X - 1
        self.n_c = self.n_y + Y - 1

    def copy(self, src, dst, number, device):
        return pltpu.make_async_remote_copy(
            src_ref=src,
            dst_ref=dst,
            send_sem=self.send.at[number],
            recv_sem=self.recv.at[number],
            device_id=device,
            device_id_type=MESH,
        )

    def z_copy(self, k):
        at = self.at
        return self.copy(
            self.src,
            self.out.at[at.d, at.y, at.x, at.c],
            self.n_z + k - 1,
            (at.up(at.d, k, at.D), at.f),
        )

    def z_got(self, k):
        at = self.at
        here = self.out.at[at.up(at.d, at.D - k, at.D), at.y, at.x, at.c]
        return self.copy(here, here, self.n_z + k - 1, (at.up(at.d, at.D - k, at.D), at.f))

    def part(self, axis, order, y, x, c):
        if axis == order[0]:
            return self.out.at[:, y, x, c]
        return self.out.at[:, y, :, c] if axis == "y" else self.out.at[:, :, x, c]

    def side(self, axis, order, k, sent):
        at = self.at
        size = at.X if axis == "x" else at.Y
        first = self.n_x if axis == "x" else self.n_y
        mine = at.x if axis == "x" else at.y
        other = at.up(mine, k if sent else size - k, size)
        y, x = (at.y, other) if axis == "x" else (other, at.x)
        block = self.part(axis, order, at.y, at.x, at.c) if sent else self.part(axis, order, y, x, at.c)
        return self.copy(block, block, first + k - 1, (at.d, at.fs(y, x, at.c)))

    def pieces(self, order, c):
        at = self.at
        out = [self.out.at[:, at.y, at.x, c]]
        for axis in order:
            size = at.X if axis == "x" else at.Y
            for k in range(1, size):
                other = at.up(at.x if axis == "x" else at.y, size - k, size)
                y, x = (at.y, other) if axis == "x" else (other, at.x)
                out.append(self.part(axis, order, y, x, c))
        return out

    def sibling(self, block, number):
        at = self.at
        return self.copy(block, block, self.n_c + number, (at.d, at.fs(at.y, at.x, 1 - at.c)))

    def local(self):
        at = self.at
        return pltpu.make_async_copy(self.src, self.out.at[at.d, at.y, at.x, at.c], self.own)

    def size_of(self, axis):
        return self.at.X if axis == "x" else self.at.Y

    def phase(self, number):
        at = self.at
        if number == 0:
            self.local().start()
            for k in range(1, at.D):
                self.z_copy(k).start()
            return
        if number == 1:
            self.local().wait()
            for k in range(1, at.D):
                self.z_got(k).wait_recv()
        for core, order in ((0, ("x", "y")), (1, ("y", "x"))):

            @pl.when(at.c == core)
            def _(core=core, order=order):
                mine = self.pieces(order, core)
                first = 1 + (self.size_of(order[0]) - 1)
                if number == 1:
                    for k in range(1, self.size_of(order[0])):
                        self.side(order[0], order, k, True).start()
                    self.sibling(mine[0], 0).start()
                elif number == 2:
                    for k in range(1, self.size_of(order[0])):
                        self.side(order[0], order, k, False).wait_recv()
                    for k in range(1, self.size_of(order[1])):
                        self.side(order[1], order, k, True).start()
                    for i in range(1, first):
                        self.sibling(mine[i], i).start()
                elif number == 3:
                    for k in range(1, self.size_of(order[1])):
                        self.side(order[1], order, k, False).wait_recv()
                    for i in range(first, len(mine)):
                        self.sibling(mine[i], i).start()
                elif number == 4:
                    for k in range(1, at.D):
                        self.z_copy(k).wait_send()
                    for axis in order:
                        for k in range(1, self.size_of(axis)):
                            self.side(axis, order, k, True).wait_send()
                    for i, block in enumerate(mine):
                        self.sibling(block, i).wait_send()
                    for i, block in enumerate(self.pieces(order[::-1], 1 - core)):
                        self.sibling(block, i).wait_recv()


class Scatter:
    @staticmethod
    def count(D, X, Y):
        return 1 + (Y - 1) + (X - 1) + (D - 1)

    @staticmethod
    def scratch(D, X, Y, R, N, held=False):
        out = [] if held else [pltpu.VMEM((D, Y, X, R, N), BF)]
        out.append(pltpu.VMEM((D, Y, X, R, N), BF))
        out += [pltpu.VMEM((Y - 1, D, X, R, N), BF), pltpu.VMEM((Y - 1, D, R, N), BF)]
        if X != Y:
            out += [pltpu.VMEM((X - 1, D, Y, R, N), BF), pltpu.VMEM((X - 1, D, R, N), BF)]
        return out + [pltpu.VMEM((D - 1, R, N), BF)]

    def __init__(self, at, grad, total, bufs, send, recv, own):
        self.at, self.grad, self.total = at, grad, total
        self.held = len(bufs) % 2 == 0
        bufs = list(bufs)
        self.acc = None if self.held else bufs.pop(0)
        self.r1, self.r2y, self.r3y = bufs[:3]
        self.r2x, self.r3x = (self.r2y, self.r3y) if at.X == at.Y else bufs[3:5]
        self.r4 = bufs[-1]
        self.send, self.recv, self.own = send, recv, own
        self.n_y = 1
        self.n_x = self.n_y + at.Y - 1
        self.n_z = self.n_x + at.X - 1

    def view(self, d, y, x):
        return self.grad.at[d, y, x, self.at.c] if self.held else self.acc.at[d, y, x]

    def get(self, d, y, x):
        return self.grad[d, y, x, self.at.c] if self.held else self.acc[d, y, x]

    def put(self, d, y, x, value):
        if self.held:
            self.grad[d, y, x, self.at.c] = value
        else:
            self.acc[d, y, x] = value

    def fill(self, values, first_column=0):
        at = self.at
        R = self.grad.shape[-2]
        into = slice(first_column, first_column + values.shape[1])

        def one(i, _):
            rest, c = lax.div(i, 2), lax.rem(i, 2)
            rest, x = lax.div(rest, at.X), lax.rem(rest, at.X)
            d, y = lax.div(rest, at.Y), lax.rem(rest, at.Y)
            first = i * R
            if R % 8 == 0:
                block = values[pl.ds(pl.multiple_of(first, 8), R), :].astype(BF)
            else:
                shape = (16, values.shape[0])
                row = lax.broadcasted_iota(jnp.int32, shape, 0)
                pick = jnp.where(lax.broadcasted_iota(jnp.int32, shape, 1) == row + first, 1.0, 0.0)
                block = nn(pick.astype(BF), values[...].astype(BF))[:R].astype(BF)
            self.grad[d, y, x, c, :, into] = block
            return 0

        lax.fori_loop(0, at.D * at.F, one, 0)

    def copy(self, src, dst, number, device):
        return pltpu.make_async_remote_copy(
            src_ref=src,
            dst_ref=dst,
            send_sem=self.send.at[number],
            recv_sem=self.recv.at[number],
            device_id=device,
            device_id_type=MESH,
        )

    def core_copy(self):
        at = self.at
        return self.copy(
            self.grad.at[:, :, :, 1 - at.c], self.r1, 0, (at.d, at.fs(at.y, at.x, 1 - at.c))
        )

    def local(self):
        return pltpu.make_async_copy(self.grad.at[:, :, :, self.at.c], self.acc, self.own)

    def side(self, axis, order, k):
        at, all_d = self.at, slice(None)
        if axis == "y":
            y = at.up(at.y, k, at.Y)
            device = (at.d, at.fs(y, at.x, at.c))
            if axis == order[0]:
                src, dst = self.view(all_d, y, slice(None)), self.r2y
            else:
                src, dst = self.view(all_d, y, at.x), self.r3y
            return self.copy(src, dst.at[k - 1], self.n_y + k - 1, device)
        x = at.up(at.x, k, at.X)
        device = (at.d, at.fs(at.y, x, at.c))
        if axis == order[0]:
            src, dst = self.view(all_d, slice(None), x), self.r2x
        else:
            src, dst = self.view(all_d, at.y, x), self.r3x
        return self.copy(src, dst.at[k - 1], self.n_x + k - 1, device)

    def z_copy(self, k):
        at = self.at
        d = at.up(at.d, k, at.D)
        return self.copy(self.view(d, at.y, at.x), self.r4.at[k - 1], self.n_z + k - 1, (d, at.f))

    def size_of(self, axis):
        return self.at.X if axis == "x" else self.at.Y

    def store(self, total):
        self.total[...] = total

    def phase(self, number):
        at = self.at
        if number == 0:
            if not self.held:
                self.local().start()
            self.core_copy().start()
            return
        if number == 1:
            if not self.held:
                self.local().wait()
            self.core_copy().wait_recv()

            def add(i, _):
                d, rest = lax.div(i, at.Y * at.X), lax.rem(i, at.Y * at.X)
                y, x = lax.div(rest, at.X), lax.rem(rest, at.X)
                self.put(d, y, x, self.get(d, y, x) + self.r1[d, y, x])
                return 0

            lax.fori_loop(0, at.D * at.Y * at.X, add, 0)
        if number == 4:
            for k in range(1, at.D):
                self.z_copy(k).wait_recv()
            total = self.get(at.d, at.y, at.x).astype(F32)
            for k in range(1, at.D):
                total = total + self.r4[k - 1].astype(F32)
            self.store(total)
            self.core_copy().wait_send()
            for k in range(1, at.D):
                self.z_copy(k).wait_send()
        for core, order in ((0, ("y", "x")), (1, ("x", "y"))):

            @pl.when(at.c == core)
            def _(core=core, order=order):
                n0, n1 = self.size_of(order[0]), self.size_of(order[1])
                if number == 1:
                    for k in range(1, n0):
                        self.side(order[0], order, k).start()
                elif number == 2:
                    for k in range(1, n0):
                        self.side(order[0], order, k).wait_recv()

                    def add(i, _):
                        d, j = lax.div(i, n1), lax.rem(i, n1)
                        y, x = (at.y, j) if order[0] == "y" else (j, at.x)
                        got = self.r2y if order[0] == "y" else self.r2x
                        value = self.get(d, y, x)
                        for k in range(1, n0):
                            value = value + got[k - 1, d, j]
                        self.put(d, y, x, value)
                        return 0

                    lax.fori_loop(0, at.D * n1, add, 0)
                    for k in range(1, n1):
                        self.side(order[1], order, k).start()
                elif number == 3:
                    for k in range(1, n1):
                        self.side(order[1], order, k).wait_recv()

                    def add(d, _):
                        got = self.r3y if order[1] == "y" else self.r3x
                        value = self.get(d, at.y, at.x)
                        for k in range(1, n1):
                            value = value + got[k - 1, d]
                        self.put(d, at.y, at.x, value)
                        return 0

                    lax.fori_loop(0, at.D, add, 0)
                elif number == 4:
                    for axis in order:
                        for k in range(1, self.size_of(axis)):
                            self.side(axis, order, k).wait_send()

        if number == 3:
            for k in range(1, at.D):
                self.z_copy(k).start()


class Total:
    @staticmethod
    def count(D, F):
        return (D - 1) + (F // 4 - 1) + 1 + 1

    @staticmethod
    def scratch(D, F, rows, cols):
        return [pltpu.VMEM((D + F // 4 + 2 + 2, rows, cols), F32)]

    def __init__(self, at, buf, send, recv):
        self.at, self.buf, self.send, self.recv = at, buf, send, recv
        device = {
            "d": lambda i: (i, at.f),
            "x": lambda i: (at.d, at.fs(at.y, i, at.c)),
            "y": lambda i: (at.d, at.fs(i, at.x, at.c)),
            "c": lambda i: (at.d, at.fs(at.y, at.x, i)),
        }
        self.stages, slot, number = [], 0, 0
        for axis, size, mine in (("d", at.D, at.d), ("x", at.X, at.x), ("y", at.Y, at.y), ("c", 2, at.c)):
            self.stages.append((slot, number, size, mine, device[axis]))
            slot, number = slot + size, number + size - 1

    def copies(self, stage, sent):
        slot, number, size, mine, device = self.stages[stage]
        out = []
        for k in range(1, size):
            other = self.at.up(mine, k if sent else size - k, size)
            block = self.buf.at[slot + (mine if sent else other)]
            out.append(
                pltpu.make_async_remote_copy(
                    src_ref=block,
                    dst_ref=block,
                    send_sem=self.send.at[number + k - 1],
                    recv_sem=self.recv.at[number + k - 1],
                    device_id=device(other),
                    device_id_type=MESH,
                )
            )
        return out

    def put(self, stage, value):
        slot, _, _, mine, _ = self.stages[stage]
        self.buf[slot + mine] = value
        for copy in self.copies(stage, True):
            copy.start()

    def take(self, stage):
        for copy in self.copies(stage, False):
            copy.wait_recv()
        slot, _, size, _, _ = self.stages[stage]
        total = self.buf[slot]
        for i in range(1, size):
            total = total + self.buf[slot + i]
        return total

    def start(self, value):
        self.put(0, value)

    def advance(self, stage):
        self.put(stage + 1, self.take(stage))

    def end(self):
        total = self.take(3)
        for stage in range(4):
            for copy in self.copies(stage, True):
                copy.wait_send()
        return total


LAGS = (0, 1, 3, 5, 6)


def steps_of(arrays, lags=(0, 1, 3, 5, 6)):
    for step in range(len(arrays) + lags[-1]):
        yield [
            (arrays[i], lags.index(step - i))
            for i in reversed(range(len(arrays)))
            if step - i in lags
        ]


def spread(arrays, slots):
    steps = list(steps_of(arrays, LAGS))
    due = {slot: [] for slot in range(slots)}
    for i, step in enumerate(steps):
        due[(i * (slots - 1)) // (len(steps) - 1)] += step
    return due


def columns(ref, part, parts):
    size = ref.shape[-1] // parts
    return ref.at[(slice(None),) * (len(ref.shape) - 1) + (pl.ds(part * size, size),)]


def placed(values, first, width):
    count = values.shape[1]
    row = lax.broadcasted_iota(jnp.int32, (count, width), 0)
    column = lax.broadcasted_iota(jnp.int32, (count, width), 1)
    return nn(values, jnp.where(column == row + first, 1.0, 0.0).astype(BF))


def head_kernel(
    D, F,
    lens, patches, pos_in, vec_in, qkv_in, bias_in, proj_in, fc1_in, fc2_in,
    stats, bias, qs, ks, proj_b, fc1_b, fc2_b, pos_out, qkv_out,
    pos_b, qkv_b, total_buf, s_send, s_recv, send, recv, own,
):
    at = Place(D, F)
    rows, width = patches.shape
    pos_b[...] = jnp.zeros_like(pos_b)
    pos_b[:, :LONG] = pos_in[...].astype(BF)
    lane = lax.broadcasted_iota(jnp.int32, (8, 128), 1)
    spread_out = jnp.where(lane == LONG - (POS_PAD - 128) + lax.broadcasted_iota(jnp.int32, (8, 128), 0), 1.0, 0.0)
    beside = tn(vec_in[...].astype(BF), spread_out.astype(BF))
    pos_b[:, POS_PAD - 128 :] = (pos_b[:, POS_PAD - 128 :].astype(F32) + beside).astype(BF)
    qkv_b[...] = qkv_in[...].astype(BF)
    meet(at.partners())
    pieces = pieces_of((pos_b, qkv_b), (pos_out, qkv_out), HEAD_PARTS)
    arrays = [
        Gather(at, src, out, send.at[i], recv.at[i], own.at[i]) for i, (src, out) in enumerate(pieces)
    ]
    steps = list(steps_of(arrays))
    arrays[0].phase(0)
    arrays[1].phase(0)
    step_rows = 64
    valid_rows = lens[0, 0] + lens[0, 1]

    def accumulate(i, sums):
        block = pl.ds(pl.multiple_of(i * step_rows, step_rows), step_rows)
        row = i * step_rows + lax.broadcasted_iota(jnp.int32, (step_rows, width), 0)
        values = jnp.where(row < valid_rows, patches[block, :].astype(F32), 0.0)
        first = values.reshape(step_rows // 8, 8, -1)
        return (sums[0] + jnp.sum(first, axis=0), sums[1] + jnp.sum(first * first, axis=0))

    empty = jnp.zeros((8, width), F32)
    plain, square = lax.fori_loop(0, rows // step_rows, accumulate, (empty, empty))
    row = lax.broadcasted_iota(jnp.int32, empty.shape, 0)
    plain = jnp.sum(plain, axis=0, keepdims=True)
    square = jnp.sum(square, axis=0, keepdims=True)
    me = at.d * F + at.f
    count = jnp.zeros((1, width), F32) + valid_rows.astype(F32)
    packed = jnp.where(row == 0, plain, jnp.where(row == 1, square, jnp.where(row == 2, count, 0.0)))
    n_bias = bias_in.shape[1]
    hidden = n_bias * D * F
    own_bias = jnp.broadcast_to(bias_in[...].astype(BF), (8, n_bias))
    for i in range(hidden // width):
        packed = jnp.where(row == 4 + i, placed(own_bias, me * n_bias - i * width, width), packed)
    total = Total(at, total_buf, s_send, s_recv)
    total.start(packed)
    for number, step in enumerate(steps):
        for array, phase in step:
            if phase > 0 or array not in arrays[:2]:
                array.phase(phase)
        if number == 1:
            proj_b[...] = proj_in[...].astype(BF)
            fc1_b[...] = fc1_in[...].astype(BF)
            fc2_b[...] = fc2_in[...].astype(BF)
            position = lax.broadcasted_iota(jnp.int32, qs.shape, 0)
            lane = lax.broadcasted_iota(jnp.int32, qs.shape, 1)
            segment = jnp.where(position < lens[0, 0], 0, jnp.where(position < valid_rows, 1, 2))
            same = segment == lane
            qs[...] = jnp.where(same, 1.0, 0.0).astype(BF)
            ks[...] = jnp.where(same, 0.0, jnp.where(lane < 3, -1e30, 0.0)).astype(BF)
        if number in (2, 4, 6):
            total.advance(number // 2 - 1)
        if number == 8:
            summed = total.end()
            inv_count = 1.0 / summed[2:3]
            mean = summed[0:1] * inv_count
            mean = summed[0:1] / summed[2:3]
            var = summed[1:2] / summed[2:3] - mean * mean
            stats[0:1, :] = mean
            stats[1:2, :] = lax.rsqrt(var + INPUT_EPS)
            stats[2:3, :] = inv_count
            stats[3:4, :] = count
            stats[4:5, :] = var
            stats[5:8, :] = jnp.zeros((3, width), F32)
            for i in range(hidden // width):
                bias[0:1, i * width : (i + 1) * width] = summed[4 + i : 5 + i]


def head(D, F, clip_len, patches, pos, vec, w_qkv, bias, w_proj, w_fc1, w_fc2, collective_id):
    X, Y = F // 4, 2
    rows, width = patches.shape
    hidden = bias.shape[0] * D * F
    count = sum(HEAD_PARTS)
    n = Gather.count(D, X, Y)
    hbm = pl.BlockSpec(memory_space=pl.ANY)
    vmem = pl.BlockSpec(memory_space=pltpu.VMEM)
    own_rows = pos.shape[0]
    sent = [(own_rows, POS_PAD), w_qkv.shape]
    return pl.pallas_call(
        partial(head_kernel, D, F),
        name="head",
        out_shape=[
            jax.ShapeDtypeStruct((8, width), F32),
            jax.ShapeDtypeStruct((1, hidden), F32),
            jax.ShapeDtypeStruct((rows, 128), BF),
            jax.ShapeDtypeStruct((rows, 128), BF),
        ]
        + [jax.ShapeDtypeStruct(w.shape, BF) for w in (w_proj, w_fc1, w_fc2)]
        + [jax.ShapeDtypeStruct((D, Y, X, 2) + shape, BF) for shape in sent],
        in_specs=[pl.BlockSpec(memory_space=pltpu.SMEM)] + [vmem] * 8,
        out_specs=[vmem] * 7 + [hbm] * 2,
        scratch_shapes=[pltpu.VMEM(shape, BF) for shape in sent]
        + Total.scratch(D, F, 8, width)
        + [pltpu.SemaphoreType.DMA((Total.count(D, F),)), pltpu.SemaphoreType.DMA((Total.count(D, F),))]
        + copy_semaphores(count, n),
        compiler_params=pltpu.CompilerParams(
            collective_id=collective_id, has_side_effects=True, vmem_limit_bytes=VMEM_LIMIT
        ),
        cost_estimate=pl.CostEstimate(flops=0, bytes_accessed=20 * 2**20, transcendentals=0),
    )(clip_len, patches, pos, vec.T, w_qkv, bias.reshape(1, -1), w_proj, w_fc1, w_fc2)


def pieces_of(grads, totals, parts):
    return [
        (columns(g, j, n), columns(t, j, n)) for g, t, n in zip(grads, totals, parts) for j in range(n)
    ]


def scatter_arrays(at, pieces, bufs, send, recv, own):
    per = len(bufs) // len(pieces)
    return [
        Scatter(at, grad, total, bufs[i * per : (i + 1) * per], send.at[i], recv.at[i], own.at[i])
        for i, (grad, total) in enumerate(pieces)
    ]


def blocks_shape(D, X, Y, rows, N):
    return (D, Y, X, 2, rows // (D * X * Y * 2), N)


def scatter_scratch(D, X, Y, grads, parts):
    out = []
    for g, n in zip(grads, parts):
        for _ in range(n):
            out += Scatter.scratch(D, X, Y, g.shape[-2], g.shape[-1] // n)
    return out


def copy_semaphores(count, n):
    return [
        pltpu.SemaphoreType.DMA((count, n)),
        pltpu.SemaphoreType.DMA((count, n)),
        pltpu.SemaphoreType.DMA((count,)),
    ]


def row_of(first, rows, width):
    return first + lax.broadcasted_iota(jnp.int32, (rows, width), 0)


def attend_pair(q_ref, k_ref, v_ref, qs_ref, ks_ref, q_block):
    rows = q_ref.shape[0]
    lane = lax.broadcasted_iota(jnp.int32, (q_block, 128), 1)

    def half(values, head):
        keep = lane < 64 if head == 0 else lane >= 64
        return jnp.where(keep, values, jnp.zeros_like(values))

    def query(block, head):
        scaled = q_ref[block, :] * jnp.asarray(0.125, BF)
        return jnp.concatenate([half(scaled, head), qs_ref[block, :]], axis=1)

    keys = jnp.concatenate([k_ref[...], ks_ref[...]], axis=1)
    return keys, query, half


def forward_kernel(
    D, F,
    lens, patches, stats, sel_long, sel_short, pos, w_ref, qs_ref, ks_ref, proj_ref, fc1_ref, fc2_ref,
    emb_out, norm_out, qkv_out, out_ref, lse_ref, vec, proj_out, fc1_out, fc2_out,
    qkv_buf, q_ref, k_ref, key_buf, v_buf, o_buf, send, recv, own,
):
    step = pl.program_id(0)
    part_rows, width = patches.shape
    rows = qkv_buf.shape[0]
    parts = rows // part_rows
    pairs = HEADS // 2
    q_block = FORWARD_BLOCK
    blocks = rows // q_block
    at = Place(D, F)

    @pl.when(step == 0)
    def _():
        meet(at.partners())
        ahead = LONG - (POS_PAD - 128)
        vec[...] = jnp.transpose(pos[:, POS_PAD - 128 :].astype(F32))[ahead : ahead + 8]

    pieces = pieces_of((proj_ref, fc1_ref, fc2_ref), (proj_out, fc1_out, fc2_out), FORWARD_PARTS)
    arrays = [
        Gather(at, src, out, send.at[i], recv.at[i], own.at[i]) for i, (src, out) in enumerate(pieces)
    ]
    due = spread(arrays, parts + 2 * pairs + 1)

    @pl.when(step < parts)
    def _():
        run_due({k: due[k] for k in range(parts)}, step, parts, 0, 1)
        mean, inv_std = stats[0:1, :], stats[1:2, :]
        normed = (patches[...].astype(F32) - mean) * inv_std
        row = lax.broadcasted_iota(jnp.int32, (part_rows, width), 0).astype(F32)
        first_row = (step * part_rows).astype(F32)
        sel = jnp.where(lens[0, 1] > 0, sel_short[0], sel_long[0])
        embedded = jnp.where(row + first_row < stats[3:4, :], normed + nt(sel, pos[...]), 0.0)
        emb_out[...] = embedded
        n, _rho = norm_parts(embedded)
        first = (n * vec[0:1, :] + vec[1:2, :]).astype(BF)
        norm_out[...] = jnp.transpose(first)
        bias = jnp.concatenate([vec[2:3, :], jnp.zeros((1, width), F32), vec[3:4, :]], axis=1)
        projected = (nn(first, w_ref[...]) + bias).astype(BF)
        qkv_out[...] = projected
        qkv_buf[pl.ds(pl.multiple_of(step * part_rows, part_rows), part_rows), :] = projected

    @pl.when(step >= parts)
    def _():
        pair = step - parts
        slots = {k: due[k + parts] for k in range(2 * pairs + 1)}

        def columns_of(i):
            return qkv_buf[:, pl.ds(pl.multiple_of(i * width + pair * 128, 128), 128)]

        q_ref[...] = columns_of(0)
        k_ref[...] = columns_of(1)
        keys, query, _ = attend_pair(q_ref, k_ref, None, qs_ref, ks_ref, q_block)
        key_buf[...] = keys
        v_t = jnp.transpose(columns_of(2))
        ones = jnp.ones((16, rows), BF)
        for head in range(2):
            v_buf[head] = jnp.concatenate([v_t[64 * head : 64 * head + 64], ones], axis=0)
        for i in range(blocks):
            if i in (0, (blocks + 1) // 2):
                run_due(slots, pair, pairs, min(i, 1), 2)
            block = pl.ds(i * q_block, q_block)
            for head in range(2):
                scores = nt(key_buf[...], query(block, head))
                top = jnp.max(scores, axis=0, keepdims=True)
                probs = jnp.exp(scores - top).astype(BF)
                out = nn(v_buf[head], probs)
                total = out[64:65, :]
                o_buf[64 * head : 64 * head + 64, block] = (out[:64] / total).astype(BF)
                lse_ref[0, head : head + 1, block] = top + jnp.log(total)
        out_ref[...] = jnp.transpose(o_buf[...])
        run_due(slots, pair, pairs, 2, 2)


def run_due(due, step, steps, point, points):
    for k in range(steps):
        work = due.get(k * points + point, [])
        if k < steps - 1 and point >= points:
            continue
        if work:

            @pl.when(step == k)
            def _(work=work):
                for array, number in work:
                    array.phase(number)


def timed(arrays, starts, lags, slots):
    due = {slot: [] for slot in range(slots)}
    for array, start, own_lags in reversed(list(zip(arrays, starts, lags))):
        for number, lag in enumerate(own_lags):
            due[min(start + lag, slots - 1)].append((array, number))
    for work in due.values():
        work.sort(key=lambda item: item[1])
    return due


def pair_specs(rows):
    pair = lambda first: pl.BlockSpec((rows, 128), lambda p: (0, first + p))
    whole = pl.BlockSpec((rows, 128), lambda p: (0, 0))
    return pair, whole


def forward(D, F, clip_len, patches, stats, table, pos, w_qkv, q_seg, k_seg, shards, collective_id):
    rows, width = patches.shape
    pairs = HEADS // 2
    part = 256
    parts = rows // part
    hbm = pl.BlockSpec(memory_space=pl.ANY)
    once = lambda a: pl.BlockSpec(a.shape, lambda p: (0,) * a.ndim, pipeline_mode=pl.Buffered(1))
    by_row = lambda n: pl.BlockSpec((part, n), lambda p: (jnp.minimum(p, parts - 1), 0))
    X, Y = F // 4, 2
    n = Gather.count(D, X, Y)
    return pl.pallas_call(
        partial(forward_kernel, D, F),
        name="forward",
        grid=(parts + pairs,),
        in_specs=[
            pl.BlockSpec(memory_space=pltpu.SMEM),
            by_row(width),
            once(stats),
            pl.BlockSpec((1, part, POS_PAD), lambda p: (0, jnp.minimum(p, parts - 1), 0)),
            pl.BlockSpec((1, part, POS_PAD), lambda p: (1, jnp.minimum(p, parts - 1), 0)),
        ]
        + [once(a) for a in (pos, w_qkv, q_seg, k_seg)]
        + [hbm] * 3,
        out_specs=[
            by_row(width),
            pl.BlockSpec((width, part), lambda p: (0, jnp.minimum(p, parts - 1))),
            by_row(3 * width),
            pl.BlockSpec((rows, 128), lambda p: (0, jnp.maximum(p - parts, 0))),
            pl.BlockSpec((1, 8, rows), lambda p: (jnp.maximum(p - parts, 0), 0, 0)),
            pl.BlockSpec((8, width), lambda p: (0, 0)),
        ]
        + [hbm] * 3,
        out_shape=[
            jax.ShapeDtypeStruct((rows, width), F32),
            jax.ShapeDtypeStruct((width, rows), BF),
            jax.ShapeDtypeStruct((rows, 3 * width), BF),
            jax.ShapeDtypeStruct((rows, 128 * pairs), BF),
            jax.ShapeDtypeStruct((pairs, 8, rows), F32),
            jax.ShapeDtypeStruct((8, width), F32),
        ]
        + [jax.ShapeDtypeStruct((D, Y, X, 2) + s.shape, s.dtype) for s in shards],
        scratch_shapes=[
            pltpu.VMEM((rows, 3 * width), BF),
            pltpu.VMEM((rows, 128), BF),
            pltpu.VMEM((rows, 128), BF),
            pltpu.VMEM((rows, 256), BF),
            pltpu.VMEM((2, 80, rows), BF),
            pltpu.VMEM((128, rows), BF),
        ]
        + copy_semaphores(sum(FORWARD_PARTS), n),
        compiler_params=pltpu.CompilerParams(
            collective_id=collective_id, has_side_effects=True, vmem_limit_bytes=VMEM_LIMIT
        ),
        cost_estimate=pl.CostEstimate(
            flops=4 * 12 * rows * rows * 256 + 2 * rows * width * (3 * width + POS_PAD),
            bytes_accessed=40 * 2**20,
            transcendentals=12 * rows * rows,
        ),
    )(clip_len, patches, stats, table, table, pos, w_qkv, q_seg, k_seg, *shards)


class PairScatter(Scatter):
    def __init__(self, first_pair, *rest):
        super().__init__(*rest)
        self.first_pair = first_pair

    def store(self, total):
        width = self.total.shape[-1] // 3
        for k in range(total.shape[1] // 384):
            for i in range(3):
                first = i * width + 128 * (self.first_pair + k)
                source = 384 * k + 128 * i
                self.total[:, first : first + 128] = total[:, source : source + 128]


def backward_pair(
    D, F,
    q_ref, k_ref, v_ref, do_ref, qs_ref, ks_ref, lse_ref, delta_ref, first_t, g_fc2, g_proj, g_fc1, *refs,
):
    dq_ref, dk_ref, dv_ref, g_last, t_fc2, t_proj, t_fc1, t_qkv = refs[:8]
    key_buf, kt_buf, dk_acc, dv_acc, dqt_buf, wide = refs[8:14]
    pairs = HEADS // 2
    groups = EARLY_PAIRS // PAIR_GROUP
    held, rest = refs[14 : 14 + groups], refs[14 + groups : -3]
    send, recv, own = refs[-3:]
    pair = pl.program_id(0)
    rows = q_ref.shape[0]
    q_block = BACKWARD_BLOCK
    blocks = rows // q_block
    at = Place(D, F)

    @pl.when(pair == 0)
    def _():
        meet(at.partners())

    pieces = pieces_of((g_fc2, g_proj, g_fc1), (t_fc2, t_proj, t_fc1), BACKWARD_PARTS)
    early = sum(BACKWARD_PARTS)
    per_held = 4 if at.X == at.Y else 6
    split = len(rest) - per_held * groups
    arrays = scatter_arrays(at, pieces, rest[:split], send, recv, own)
    for p in range(groups):
        bufs = rest[split + p * per_held : split + (p + 1) * per_held]
        i = early + p
        arrays.append(
            PairScatter(
                p * PAIR_GROUP, at, held[p], t_qkv, bufs, send.at[i], recv.at[i], own.at[i]
            )
        )
    starts = list(range(early)) + [2 * PAIR_GROUP * (p + 1) for p in range(groups)]
    due = timed(arrays, starts, BACKWARD_LAGS, 2 * pairs + 1)
    keys, query, half = attend_pair(q_ref, k_ref, v_ref, qs_ref, ks_ref, q_block)
    key_buf[...] = keys
    kt_buf[...] = jnp.transpose(k_ref[...])
    for i in range(blocks):
        if i in (0, (blocks + 1) // 2):
            run_due(due, pair, pairs, min(i, 1), 2)
        block = pl.ds(i * q_block, q_block)
        for head in range(2):
            q_ext = query(block, head)
            d_out = half(do_ref[block, :], head)
            scores = nt(key_buf[...], q_ext)
            probs = jnp.exp(scores - lse_ref[0, head : head + 1, block])
            d_probs = nt(v_ref[...], d_out)
            d_scores = (probs * (d_probs - delta_ref[0, head : head + 1, block])).astype(BF)
            dv = nn(probs.astype(BF), d_out)
            dk = nn(d_scores, q_ext[:, :128])
            if i == 0 and head == 0:
                dv_acc[...] = dv
                dk_acc[...] = dk
            else:
                dv_acc[...] += dv
                dk_acc[...] += dk
            dq = nn(kt_buf[64 * head : 64 * head + 64, :], d_scores)
            dqt_buf[64 * head : 64 * head + 64, block] = (dq * 0.125).astype(BF)
    dq_ref[...] = jnp.transpose(dqt_buf[...])
    dk_ref[...] = dk_acc[...].astype(BF)
    dv_ref[...] = dv_acc[...].astype(BF)
    joined = jnp.concatenate([dq_ref[...], dk_ref[...], dv_ref[...]], axis=1)
    wide[...] = nn(first_t[...], joined)
    for p in range(EARLY_PAIRS):

        @pl.when(pair == p)
        def _(p=p):
            arrays[early + p // PAIR_GROUP].fill(wide, 384 * (p % PAIR_GROUP))

    @pl.when(pair >= EARLY_PAIRS)
    def _():
        g_last[...] = wide[...].astype(BF)

    run_due(due, pair, pairs, 2, 2)


def attend_backward(D, F, qkv, grad_attended, q_seg, k_seg, lse, delta, first_t, grads, collective_id):
    rows = qkv.shape[0]
    width = first_t.shape[0]
    pairs = HEADS // 2
    pair, whole = pair_specs(rows)
    line = pl.BlockSpec((1, 8, rows), lambda p: (p, 0, 0))
    hbm = pl.BlockSpec(memory_space=pl.ANY)
    once = lambda shape: pl.BlockSpec(shape, lambda p: (0,) * len(shape), pipeline_mode=pl.Buffered(1))
    X, Y = F // 4, 2
    n = Scatter.count(D, X, Y)
    own_rows = width // (D * F)
    groups = EARLY_PAIRS // PAIR_GROUP
    held = [pltpu.VMEM(blocks_shape(D, X, Y, width, 384 * PAIR_GROUP), BF)] * groups
    held_scratch = Scatter.scratch(D, X, Y, own_rows, 384 * PAIR_GROUP, held=True) * groups
    totals = [jax.ShapeDtypeStruct(g.shape[-2:], F32) for g in grads]
    totals.append(jax.ShapeDtypeStruct((own_rows, 3 * width), F32))
    return pl.pallas_call(
        partial(backward_pair, D, F),
        name="attend_backward",
        grid=(pairs,),
        in_specs=[pair(0), pair(pairs), pair(2 * pairs), pair(0), whole, whole, line, line]
        + [once(first_t.shape)]
        + [hbm] * 3,
        out_specs=[pair(0)] * 3
        + [pl.BlockSpec((width, 384), lambda p: (0, jnp.maximum(p - EARLY_PAIRS, 0)))]
        + [once(t.shape) for t in totals],
        out_shape=[jax.ShapeDtypeStruct((rows, 128 * pairs), BF)] * 3
        + [jax.ShapeDtypeStruct((width, 384 * (pairs - EARLY_PAIRS)), BF)]
        + totals,
        scratch_shapes=[
            pltpu.VMEM((rows, 256), BF),
            pltpu.VMEM((128, rows), BF),
            pltpu.VMEM((rows, 128), F32),
            pltpu.VMEM((rows, 128), F32),
            pltpu.VMEM((128, rows), BF),
            pltpu.VMEM((width, 384), F32),
        ]
        + held
        + scatter_scratch(D, X, Y, grads, BACKWARD_PARTS)
        + held_scratch
        + copy_semaphores(sum(BACKWARD_PARTS) + groups, n),
        compiler_params=pltpu.CompilerParams(
            collective_id=collective_id, has_side_effects=True, vmem_limit_bytes=VMEM_LIMIT
        ),
        cost_estimate=pl.CostEstimate(
            flops=10 * 12 * rows * rows * 256,
            bytes_accessed=14 * rows * 768,
            transcendentals=12 * rows * rows,
        ),
    )(qkv, qkv, qkv, grad_attended, q_seg, k_seg, lse, delta, first_t, *grads)


def gelu_both(u):
    z = jnp.abs(u)
    falling = jnp.exp(-0.5 * u * u)
    t = 1.0 / (1.0 + TAIL_P * z)
    poly = TAIL_C[-1]
    for coefficient in TAIL_C[-2::-1]:
        poly = poly * t + coefficient
    tail = poly * t * falling
    upper = jnp.where(u >= 0, 1.0 - tail, tail)
    return u * upper, upper + u * falling * 0.3989422804014327


def norm_parts(values):
    center = values - jnp.mean(values, axis=1, keepdims=True)
    spread = jnp.mean(center * center, axis=1, keepdims=True)
    rho = lax.rsqrt(spread + NORM_EPS)
    return center * rho, rho


def norm_back(n, rho, grad, gain):
    q = grad * gain
    return rho * (q - jnp.mean(q, axis=1, keepdims=True) - n * jnp.mean(q * n, axis=1, keepdims=True))


def fold(values):
    return jnp.sum(values.reshape(-1, 8, values.shape[1]), axis=0)


def middle_kernel(
    D, F, tiles,
    stats, emb, att, cot, wo, w1, b1, w2, vec, pick,
    layer_out, res_grad, att_grad, delta_out, g_proj, g_fc1, g_b1, g_fc2, g_small, t_fc1,
    residual, second, second_t, mlp, g_second, act_buf, pre_buf, wide, *rest,
):
    step = pl.program_id(0)
    rows, width = emb.shape
    tile = w1.shape[1]
    block_rows = 256
    blocks = rows // block_rows
    ones = jnp.ones((8, block_rows), BF)
    masked, branch = layer_out, second
    at = Place(D, F)
    held, bufs, (send, recv, own) = rest[:EARLY_TILES], rest[EARLY_TILES:-3], rest[-3:]
    per = len(bufs) // EARLY_TILES
    arrays = [
        Scatter(
            at, held[j], t_fc1.at[:, pl.ds(j * tile, tile)], bufs[j * per : (j + 1) * per],
            send.at[j], recv.at[j], own.at[j],
        )
        for j in range(EARLY_TILES)
    ]
    due = timed(arrays, [2 * j + 2 for j in range(EARLY_TILES)], MIDDLE_LAGS, 2 * tiles + 2)

    def take(i):
        return pl.ds(pl.multiple_of(i * block_rows, block_rows), block_rows)

    def flags(i):
        row = lax.broadcasted_iota(jnp.int32, (block_rows, width), 0).astype(F32)
        return row + jnp.asarray(i * block_rows, jnp.int32).astype(F32) < stats[3:4, :]

    @pl.when(step == 0)
    def _():
        meet(at.partners())

        def one(i, _):
            block = take(i)
            branch_out = nn(att[block, :], wo[...]) + vec[4:5, :]
            res = emb[block, :] + branch_out
            residual[block, :] = res
            n, _rho = norm_parts(res)
            sn = (n * vec[5:6, :] + vec[6:7, :]).astype(BF)
            second[block, :] = sn
            second_t[i] = jnp.transpose(sn)
            masked[block, :] = jnp.where(flags(i), cot[block, :].astype(F32), 0.0).astype(BF)
            mlp[block, :] = jnp.zeros((block_rows, width), F32)
            g_second[block, :] = jnp.zeros((block_rows, width), F32)
            return 0

        lax.fori_loop(0, blocks, one, 0)

    bias = b1[...]
    for i in range(blocks):
        if i in (0, 3):
            run_due(due, step, tiles, i // 3, 2)
        block = pl.ds(i * block_rows, block_rows)
        pre = nn(second[block, :], w1[...]) + bias
        act, slope = gelu_both(pre)
        act = act.astype(BF)
        act_buf[block, :] = act
        grad_act = nt(masked[block, :], w2[...]).astype(BF).astype(F32)
        grad_pre = (grad_act * slope).astype(BF)
        pre_buf[block, :] = grad_pre
        mlp[block, :] += nn(act, w2[...])
        g_second[block, :] += nt(grad_pre, w1[...])
    g_fc2[...] = tn(act_buf[...], masked[...]).astype(BF)
    for i in range(blocks):
        block = pl.ds(i * block_rows, block_rows)
        part = nn(second_t[i], pre_buf[block, :])
        line = nn(ones, pre_buf[block, :])
        total = part if i == 0 else total + part
        lines = line if i == 0 else lines + line
    wide[...] = total
    g_b1[...] = lines
    for j in range(EARLY_TILES):

        @pl.when(step == j)
        def _(j=j):
            arrays[j].fill(wide)

    @pl.when(step >= EARLY_TILES)
    def _():
        g_fc1[...] = wide[...].astype(BF)

    run_due(due, step, tiles, 2, 2)

    @pl.when(step == tiles - 1)
    def _():
        def one(i, sums):
            block = take(i)
            res = residual[block, :]
            n, rho = norm_parts(res)
            out_grad = masked[block, :]
            layer_out[block, :] = jnp.where(flags(i), res + mlp[block, :] + vec[7:8, :], 0.0).astype(BF)
            grad = g_second[block, :].astype(BF).astype(F32)
            back = norm_back(n, rho, grad, vec[5:6, :])
            total = out_grad.astype(F32) + back
            res_grad[block, :] = total
            low = total.astype(BF)
            branch[block, :] = low
            into = nt(low, wo[...]).astype(BF)
            att_grad[block, :] = into
            product = into.astype(F32) * att[block, :].astype(F32)
            high = product.astype(BF)
            rest = (product - high.astype(F32)).astype(BF)
            delta = nn(high, pick[...]) + nn(rest, pick[...])
            lines = jnp.transpose(delta)
            for p in range(HEADS // 2):
                delta_out[p, 0:2, block] = lines[2 * p : 2 * p + 2, :]
            return (
                sums[0] + nn(ones, low)[0:8],
                sums[1] + fold(grad * n),
                sums[2] + fold(grad),
                sums[3] + nn(ones, out_grad)[0:8],
            )

        empty = jnp.zeros((8, width), F32)
        sums = lax.fori_loop(0, blocks, one, (empty,) * 4)
        g_proj[...] = tn(att[...], branch[...]).astype(BF)
        g_small[0:1, :] = sums[0][0:1]
        g_small[1:2, :] = jnp.sum(sums[1], axis=0, keepdims=True)
        g_small[2:3, :] = jnp.sum(sums[2], axis=0, keepdims=True)
        g_small[3:4, :] = sums[3][0:1]
        g_small[4:8, :] = jnp.zeros((4, width), F32)

    run_due(due, step, tiles, 3, 2)


def middle(D, F, stats, emb, att, cot, wo, w1, b1, w2, vec, collective_id):
    rows, width = emb.shape
    hidden = w1.shape[1]
    tile = 512
    tiles = hidden // tile
    X, Y = F // 4, 2
    own_rows = width // (D * F)
    once = pl.Buffered(1)
    whole = lambda shape: pl.BlockSpec(shape, lambda j: (0,) * len(shape), pipeline_mode=once)
    pick = np.zeros((width, 128), np.float32)
    pick[np.arange(width), np.arange(width) // 64] = 1.0
    pick = jnp.asarray(pick.astype(ml_dtypes.bfloat16))
    out_shape = [
        jax.ShapeDtypeStruct((rows, width), BF),
        jax.ShapeDtypeStruct((rows, width), F32),
        jax.ShapeDtypeStruct((rows, width), BF),
        jax.ShapeDtypeStruct((HEADS // 2, 8, rows), F32),
        jax.ShapeDtypeStruct((width, width), BF),
        jax.ShapeDtypeStruct((width, tile * (tiles - EARLY_TILES)), BF),
        jax.ShapeDtypeStruct((8, hidden), F32),
        jax.ShapeDtypeStruct((hidden, width), BF),
        jax.ShapeDtypeStruct((8, width), F32),
        jax.ShapeDtypeStruct((own_rows, tile * EARLY_TILES), F32),
    ]
    scatter = []
    for _ in range(EARLY_TILES):
        scatter += Scatter.scratch(D, X, Y, own_rows, tile, held=True)
    return pl.pallas_call(
        partial(middle_kernel, D, F, tiles),
        name="middle",
        grid=(tiles,),
        in_specs=[
            whole(stats.shape),
            whole((rows, width)),
            whole((rows, width)),
            whole((rows, width)),
            whole((width, width)),
            pl.BlockSpec((width, tile), lambda j: (0, j)),
            pl.BlockSpec((1, tile), lambda j: (0, j)),
            pl.BlockSpec((tile, width), lambda j: (j, 0)),
            whole((8, width)),
            whole((width, 128)),
        ],
        out_specs=[whole(s.shape) for s in out_shape[:5]]
        + [
            pl.BlockSpec((width, tile), lambda j: (0, jnp.maximum(j - EARLY_TILES, 0))),
            pl.BlockSpec((8, tile), lambda j: (0, j)),
            pl.BlockSpec((tile, width), lambda j: (j, 0)),
            whole((8, width)),
            whole(out_shape[9].shape),
        ],
        scratch_shapes=[
            pltpu.VMEM((rows, width), F32),
            pltpu.VMEM((rows, width), BF),
            pltpu.VMEM((rows // 256, width, 256), BF),
            pltpu.VMEM((rows, width), F32),
            pltpu.VMEM((rows, width), F32),
            pltpu.VMEM((rows, tile), BF),
            pltpu.VMEM((rows, tile), BF),
            pltpu.VMEM((width, tile), F32),
        ]
        + [pltpu.VMEM(blocks_shape(D, X, Y, width, tile), BF)] * EARLY_TILES
        + scatter
        + copy_semaphores(EARLY_TILES, Scatter.count(D, X, Y)),
        out_shape=out_shape,
        compiler_params=pltpu.CompilerParams(
            collective_id=collective_id, has_side_effects=True, vmem_limit_bytes=VMEM_LIMIT
        ),
        cost_estimate=pl.CostEstimate(
            flops=2 * rows * width * (6 * hidden + 3 * width),
            bytes_accessed=40 * 2**20,
            transcendentals=rows * hidden,
        ),
    )(stats, emb, att, cot, wo, w1, b1, w2, vec, pick)


def last_kernel(
    D, F,
    lens, gq, gk, gv, emb, res_grad, patches, stats, sel_long, sel_short, w_ref, vec, small_in, bias_in, g_last,
    patch_grad, small_out, t_last, t_pos,
    pos_acc, masked, normed_buf, sums, pos_a, pos_b, total_buf, s_send, s_recv, *rest,
):
    step = pl.program_id(0)
    rows, width = emb.shape
    total_rows = patch_grad.shape[0]
    steps = total_rows // rows
    ones = jnp.ones((8, rows), BF)
    at = Place(D, F)
    bufs, (send, recv, own) = rest[:-3], rest[-3:]
    per_held = 4 if at.X == at.Y else 6
    early = Scatter(at, g_last, t_last, bufs[: per_held + 1], send.at[0], recv.at[0], own.at[0])
    pos_blocks = (pos_a, pos_b)
    half = POS_PAD // 2
    pos = [
        Scatter(
            at, pos_blocks[i], t_pos.at[:, pl.ds(half * i, half)],
            bufs[per_held + 1 + per_held * i : per_held + 1 + per_held * (i + 1)],
            send.at[1 + i], recv.at[1 + i], own.at[1 + i],
        )
        for i in range(2)
    ]
    total = Total(at, total_buf, s_send, s_recv)

    @pl.when(step == 0)
    def _():
        meet(at.partners())
        early.phase(0)
        sums[...] = jnp.zeros_like(sums)

    for number in range(1, 5):

        @pl.when(step == number)
        def _(number=number):
            early.phase(number)

    parts = [gq[...], gk[...], gv[...]]
    for i, part in enumerate(parts):
        into = nt(part, w_ref[:, i * width : (i + 1) * width])
        grad = into if i == 0 else grad + into
    grad = grad.astype(BF).astype(F32)
    n, rho = norm_parts(emb[...])
    row = lax.broadcasted_iota(jnp.int32, (rows, width), 0).astype(F32) + (step * rows).astype(F32)
    valid = row < stats[3:4, :]
    whole = jnp.where(valid, res_grad[...] + norm_back(n, rho, grad, vec[0:1, :]), 0.0)
    block = pl.ds(pl.multiple_of(step * rows, rows), rows)
    masked[block, :] = whole
    sel = jnp.where(lens[0, 1] > 0, sel_short[0], sel_long[0])
    moved = tn(whole.astype(BF), sel)

    @pl.when(step == 0)
    def _():
        pos_acc[...] = moved

    @pl.when(step > 0)
    def _():
        pos_acc[...] += moved

    normed = (patches[...].astype(F32) - stats[0:1, :]) * stats[1:2, :]
    normed_buf[block, :] = jnp.where(valid, normed, 0.0)
    sums[0] += fold(grad * n)
    sums[1] += fold(grad)
    sums[2] += nn(ones, parts[0])
    sums[3] += nn(ones, parts[2])
    sums[4] += fold(whole)
    sums[5] += fold(whole * normed)

    @pl.when(step == steps - 1)
    def _():
        lines = []
        for i in range(6):
            line = sums[i]
            lines.append(line[0:1] if i in (2, 3) else jnp.sum(line, axis=0, keepdims=True))
        hidden = bias_in.shape[1]
        own_lines = lines[4:] + [bias_in[0:1, i * width : (i + 1) * width] for i in range(hidden // width)]
        own_lines += [jnp.zeros((1, width), F32)] * (8 - len(own_lines))
        total.start(jnp.concatenate(own_lines, axis=0))
        own_vec = lines[:4] + [small_in[i : i + 1, :] for i in range(4)]
        ahead = LONG - (POS_PAD - 128)
        own_vec = [jnp.zeros((ahead, width), F32)] + own_vec + [jnp.zeros((128 - ahead - 8, width), F32)]
        pos_acc[:, POS_PAD - 128 :] += jnp.transpose(jnp.concatenate(own_vec, axis=0))
        pos[0].fill(pos_acc.at[:, :half])
        pos[0].phase(0)
        pos[1].fill(pos_acc.at[:, half:])
        pos[1].phase(0)
        pos[0].phase(1)
        pos[1].phase(1)
        total.advance(0)
        pos[0].phase(2)
        pos[1].phase(2)
        total.advance(1)
        pos[0].phase(3)
        pos[1].phase(3)
        total.advance(2)
        summed = total.end()
        small_out[...] = summed
        inv_std, inv_count = stats[1:2, :], stats[2:3, :]
        plain, scaled = summed[0:1] * inv_count, summed[1:2] * inv_count

        def one(i, _):
            part = pl.ds(pl.multiple_of(i * 64, 64), 64)
            valid = flag_buf(i)
            value = masked[part, :] - valid * plain - normed_buf[part, :] * scaled
            patch_grad[part, :] = (inv_std * value).astype(BF)
            return 0

        valid_rows = stats[3:4, :]

        def flag_buf(i):
            row = lax.broadcasted_iota(jnp.int32, (64, width), 0).astype(F32)
            return jnp.where(row + (i * 64).astype(F32) < valid_rows, 1.0, 0.0)

        lax.fori_loop(0, total_rows // 64, one, 0)
        pos[0].phase(4)
        pos[1].phase(4)


def last_back(D, F, clip_len, gq, gk, gv, emb, res_grad, patches, stats, table, w_qkv, vec, small, bias, g_last, collective_id):
    rows, width = emb.shape
    block = 256
    once = pl.Buffered(1)
    whole = lambda shape: pl.BlockSpec(shape, lambda i: (0,) * len(shape), pipeline_mode=once)
    by_row = lambda n: pl.BlockSpec((block, n), lambda i: (i, 0))
    X, Y = F // 4, 2
    own_rows = width // (D * F)
    n = Scatter.count(D, X, Y)
    out_shape = [
        jax.ShapeDtypeStruct((rows, width), BF),
        jax.ShapeDtypeStruct((8, width), F32),
        jax.ShapeDtypeStruct((own_rows, g_last.shape[-1]), F32),
        jax.ShapeDtypeStruct((own_rows, POS_PAD), F32),
    ]
    return pl.pallas_call(
        partial(last_kernel, D, F),
        name="last_back",
        grid=(rows // block,),
        in_specs=[pl.BlockSpec(memory_space=pltpu.SMEM)]
        + [by_row(width)] * 6
        + [
            whole(stats.shape),
            pl.BlockSpec((1, block, POS_PAD), lambda i: (0, i, 0)),
            pl.BlockSpec((1, block, POS_PAD), lambda i: (1, i, 0)),
            whole(w_qkv.shape),
            whole(vec.shape),
        ]
        + [whole(small.shape), whole(bias.shape), pl.BlockSpec(memory_space=pl.ANY)],
        out_specs=[whole(o.shape) for o in out_shape],
        out_shape=out_shape,
        scratch_shapes=[
            pltpu.VMEM((width, POS_PAD), F32),
            pltpu.VMEM((rows, width), F32),
            pltpu.VMEM((rows, width), F32),
            pltpu.VMEM((6, 8, width), F32),
            pltpu.VMEM(blocks_shape(D, X, Y, width, POS_PAD // 2), BF),
            pltpu.VMEM(blocks_shape(D, X, Y, width, POS_PAD // 2), BF),
        ]
        + Total.scratch(D, F, 8, width)
        + [pltpu.SemaphoreType.DMA((Total.count(D, F),)), pltpu.SemaphoreType.DMA((Total.count(D, F),))]
        + Scatter.scratch(D, X, Y, own_rows, g_last.shape[-1])
        + Scatter.scratch(D, X, Y, own_rows, POS_PAD // 2, held=True) * 2
        + copy_semaphores(3, n),
        compiler_params=pltpu.CompilerParams(
            collective_id=collective_id, has_side_effects=True, vmem_limit_bytes=VMEM_LIMIT
        ),
        cost_estimate=pl.CostEstimate(
            flops=2 * rows * width * (6 * width + POS_PAD),
            bytes_accessed=30 * 2**20,
            transcendentals=0,
        ),
    )(clip_len, gq, gk, gv, emb, res_grad, patches, stats, table, table, w_qkv, vec, small, bias, g_last)


def average_keep():
    return min(0.99, (1.0 + PRIOR_STEPS) / (10.0 + PRIOR_STEPS))


def stepped(rate, g, w, m, e):
    keep = average_keep()
    moved = MOMENTUM * m + g
    update = -(rate * (g + MOMENTUM * moved))
    return g, update, moved, keep * e + (1.0 - keep) * (w + update)


def optimizer_kernel(rate, t_pos, t_early, t_late, t_proj, t_most, t_last, t_fc2, *refs):
    states, outs = refs[:18], refs[18:]
    names = 6

    def write(i, where, g):
        w, m, e = (states[3 * i + j][where] for j in range(3))
        for out, value in zip(outs[4 * i : 4 * i + 4], stepped(rate, g, w, m, e)):
            out[where] = value

    everything = (slice(None), slice(None))
    write(0, everything, t_pos[:, :LONG])
    ahead = LONG - (POS_PAD - 128)
    write(1, everything, jnp.transpose(t_pos[:, POS_PAD - 128 :])[ahead : ahead + 8])
    width = t_early.shape[1] // 3
    early = 128 * EARLY_PAIRS
    for i in range(3):
        first = i * width
        write(2, (slice(None), slice(first, first + early)), t_early[:, first : first + early])
        for k in range(HEADS // 2 - EARLY_PAIRS):
            to = first + early + 128 * k
            source = 384 * k + 128 * i
            write(2, (slice(None), slice(to, to + 128)), t_late[:, source : source + 128])
    write(3, everything, t_proj[...])
    most = t_most.shape[1]
    write(4, (slice(None), slice(0, most)), t_most[...])
    write(4, (slice(None), slice(most, most + t_last.shape[1])), t_last[...])
    write(5, everything, t_fc2[...])


def optimize(rate, totals, states):
    vmem = pl.BlockSpec(memory_space=pltpu.VMEM)
    flat = [a for group in states for a in group]
    out = pl.pallas_call(
        partial(optimizer_kernel, rate),
        name="optimizer",
        in_specs=[vmem] * (len(totals) + len(flat)),
        out_specs=[vmem] * (4 * len(states)),
        out_shape=[jax.ShapeDtypeStruct(group[0].shape, F32) for group in states for _ in range(4)],
        compiler_params=pltpu.CompilerParams(vmem_limit_bytes=VMEM_LIMIT),
    )(*totals, *flat)
    return [tuple(out[4 * i : 4 * i + 4]) for i in range(len(states))]


def local(
    D, F,
    patches, cotangent, clip_len,
    pos_table, vector_params, w_qkv, w_proj, w_fc1, b_fc1, w_fc2,
    *states,
):
    params = (pos_table, vector_params, w_qkv, w_proj, w_fc1, b_fc1, w_fc2)
    momenta, averages = states[:7], states[7:]
    local_rows, width = patches.shape
    hidden = w_fc1.shape[1]
    group_size = D * F
    X, Y = F // 4, 2
    table = selectors(local_rows)
    stats, bias_full, q_seg, k_seg, proj_b, fc1_b, fc2_b, pos_full, qkv_full = head(
        D, F, clip_len, patches, pos_table, vector_params, w_qkv, b_fc1, w_proj, w_fc1, w_fc2, 0
    )
    pos_full, qkv_full = (w.reshape(-1, w.shape[-1]) for w in (pos_full, qkv_full))
    emb, first_t, qkv, attended, lse, vec, *full = forward(
        D, F, clip_len, patches, stats, table, pos_full, qkv_full, q_seg, k_seg,
        (proj_b, fc1_b, fc2_b), 1,
    )
    proj_full, fc1_full, fc2_full = (w.reshape(-1, w.shape[-1]) for w in full)
    layer_out, res_grad, att_grad, delta, g_proj, g_fc1, g_b1, g_fc2, g_small_mid, t_fc1_most = middle(
        D, F, stats, emb, attended, cotangent, proj_full, fc1_full, bias_full, fc2_full, vec, 4
    )
    spans = lambda g: g.reshape(D, Y, X, 2, -1, g.shape[-1])
    gq, gk, gv, g_last, t_fc2, t_proj, t_fc1, t_qkv = attend_backward(
        D, F, qkv, att_grad, q_seg, k_seg, lse, delta, first_t,
        [spans(g) for g in (g_fc2, g_proj, g_fc1)], 2,
    )
    patch_grad, small_sum, t_late, t_pos = last_back(
        D, F, clip_len, gq, gk, gv, emb, res_grad, patches, stats, table, qkv_full, vec,
        g_small_mid, g_b1, spans(g_last), 3,
    )
    rate = 0.02 * (local_rows * group_size) ** (-0.5)
    groups = list(zip(params, momenta, averages))
    groups[1] = tuple(a.T for a in groups[1])
    big = [groups[i] for i in (0, 1, 2, 3, 4, 6)]
    done = optimize(rate, (t_pos, t_qkv, t_late, t_proj, t_fc1_most, t_fc1, t_fc2), big)
    me = lax.axis_index("dp") * F + lax.axis_index("fsdp")
    n_bias = b_fc1.size
    g_bias = lax.dynamic_slice(small_sum[2 : 2 + hidden // width].reshape(-1), (me * n_bias,), (n_bias,))
    done[1] = tuple(a.T for a in done[1])
    done.insert(5, stepped(rate, g_bias, *groups[5]))
    feature_stats = jnp.stack([stats[0], stats[4]])
    return (layer_out, patch_grad, feature_stats) + tuple(d[i] for i in range(4) for d in done)


def solution(mesh):
    rows, line = P(AXES, None), P(AXES)
    params = (rows, rows, rows, rows, rows, line, rows)
    return jax.shard_map(
        partial(local, mesh.shape["dp"], mesh.shape["fsdp"]),
        mesh=mesh,
        in_specs=(rows,) * 3 + params * 3,
        out_specs=(rows, rows, P()) + params * 4,
        check_vma=False,
    )
```
